32 devices in a mesh: dp: 8 (over z, x), mp: 4 (over y, core).
Axes of the slice: x: 2, y: 2, z: 4, core: 2. Of those that a mesh axis runs over, the one named last changes fastest.
Arguments:
- byte_ids: int32 [32, 2048], P('dp'), may hold values from 0 to 261
- lengths: int32 [32], P('dp'), may hold values from 512 to 2048, as said below
- latents: bfloat16 [32, 256, 1280], P('dp'), may hold values from -6 to 6
- byte_table: bfloat16 [262, 768], replicated, may hold values from -6 to 6
- pos_table: bfloat16 [2048, 768], replicated, may hold values from -3 to 3
- gain_in: float32 [768], replicated, may hold values from 0.25 to 1.75
- gain_lat: float32 [1280], replicated, may hold values from 0.25 to 1.75
- gain_mlp: float32 [1280], replicated, may hold values from 0.25 to 1.75
- w_query: bfloat16 [1280, 256], P(None, 'mp'), may hold values from -0.15625 to 0.15625
- w_key: bfloat16 [768, 256], P(None, 'mp'), may hold values from -0.21875 to 0.21875
- w_value: bfloat16 [768, 1280], P(None, 'mp'), may hold values from -0.21875 to 0.21875
- w_out: bfloat16 [1280, 1280], P('mp'), may hold values from -4 to 4
- w_one: bfloat16 [1280, 1280], P(None, 'mp'), may hold values from -0.15625 to 0.15625
- w_two: bfloat16 [1280, 1280], P('mp'), may hold values from -0.15625 to 0.15625
- out_grad: bfloat16 [32, 256, 1280], P('dp'), may hold values from -6 to 6
Outputs:
- latents_out: bfloat16 [32, 256, 1280], P('dp')
- latent_grad: float32 [32, 256, 1280], P('dp')
- byte_grad: float32 [262, 768], P(None, 'mp')
- pos_grad: float32 [2048, 768], P('dp', 'mp')
- gain_in_grad: float32 [768], P('mp')
- gain_lat_grad: float32 [1280], P('mp')
- gain_mlp_grad: float32 [1280], P('mp')
- w_query_grad: float32 [1280, 256], P('dp', 'mp')
- w_key_grad: float32 [768, 256], P('dp', 'mp')
- w_value_grad: float32 [768, 1280], P('dp', 'mp')
- w_out_grad: float32 [1280, 1280], P('mp', 'dp')
- w_one_grad: float32 [1280, 1280], P('dp', 'mp')
- w_two_grad: float32 [1280, 1280], P('mp', 'dp')
The draws below stay inside these ranges and needn't reach their ends.
Inputs may be any that keep to these rules, and one draw needn't show every extreme that they name: The lengths[i] live slots of item i come first; later slots are padding. In every draw some item is full.
All inputs are finite; a program needn't handle non-finite values.
Results may differ from the reference program's by a relative error of at most 0.012.
The reference program's roundings to bfloat16 on the way count: a program that leaves them out, or rounds other values in their place, can miss the bound.
Values sent between devices are 32-bit elements; how exact they have to be, the bound alone decides.
No kernel may reach another device: no remote copies, remote signals or barrier semaphores. Data moves between devices by JAX's collectives and lax.ppermute only.
A program may use at most 320 MiB of HBM per device.

```python
import jax
import jax.numpy as jnp
from jax import lax

DIN = 768
DLAT = 1280
QK = 256
HEADS = 8
LATENTS = 256
SLOTS = 2048
VOCAB = 262
HEAD_DIM = 160
QK_DIM = 32
ITEMS = 32


def draw_lengths(key, part):
    key = jax.random.fold_in(key, 11)
    draw_key, pick_key = jax.random.split(key)
    drawn_len = jax.random.randint(draw_key, (ITEMS,), SLOTS // 4, SLOTS + 1)
    fullest = jax.random.randint(pick_key, (), 0, ITEMS)
    return jnp.where(jnp.arange(ITEMS) == fullest, SLOTS, drawn_len).astype(jnp.int32)


def plant(drawn, stream_key, smallest, largest):
    spot = [jax.random.randint(jax.random.fold_in(stream_key, axis), (), 0, length) for axis, length in enumerate(drawn.shape)]
    widest = drawn.shape.index(max(drawn.shape))
    beside = spot[:widest] + [(spot[widest] + 1) % drawn.shape[widest]] + spot[widest + 1:]
    return drawn.at[tuple(spot)].set(smallest).at[tuple(beside)].set(largest)


def block_scale(key, shape, cuts, low, high):
    gain, own = 1.0, jax.random.fold_in(key, 6)
    for position, blocks in cuts:
        heights = jnp.exp(jax.random.uniform(jax.random.fold_in(own, position), (blocks,), jnp.float32, low / len(cuts), high / len(cuts)))
        gain = gain * jnp.repeat(heights, shape[position] // blocks).reshape([-1 if axis == position else 1 for axis in range(len(shape))])
    return gain


def normal_values(stream_key, dims, spread, most, cuts=(), kind=jnp.bfloat16):
    values = spread * jax.random.normal(stream_key, dims, jnp.float32)
    if cuts:
        values = values * block_scale(stream_key, dims, cuts, -0.22, 0.18)
    return jnp.clip(values, -most, most).astype(kind)


def setup_inputs(seed: int = 0) -> dict:
    seeds = jax.random.split(jax.random.key(seed), 16)
    return {
        "byte_ids": plant(jax.random.randint(seeds[0], (ITEMS, SLOTS), 0, VOCAB), jax.random.fold_in(seeds[0], 1), 0, VOCAB - 1).astype(jnp.int32),
        "lengths": draw_lengths(jax.random.fold_in(seeds[15], 71), 0),
        "latents": normal_values(seeds[2], (ITEMS, LATENTS, DLAT), 1.0, 6.0, ((0, 8),)),
        "byte_table": normal_values(seeds[3], (VOCAB, DIN), 1.0, 6.0),
        "pos_table": normal_values(seeds[4], (SLOTS, DIN), 0.5, 3.0),
        "gain_in": jnp.clip(1.0 + 0.15 * jax.random.normal(seeds[5], (DIN,), jnp.float32), 0.25, 1.75),
        "gain_lat": jnp.clip(1.0 + 0.15 * jax.random.normal(seeds[6], (DLAT,), jnp.float32), 0.25, 1.75),
        "gain_mlp": jnp.clip(1.0 + 0.15 * jax.random.normal(seeds[7], (DLAT,), jnp.float32), 0.25, 1.75),
        "w_query": normal_values(seeds[8], (DLAT, QK), DLAT ** -0.5, 0.15625, ((1, 4),)),
        "w_key": normal_values(seeds[9], (DIN, QK), DIN ** -0.5, 0.21875, ((1, 4),)),
        "w_value": normal_values(seeds[10], (DIN, DLAT), DIN ** -0.5, 0.21875, ((1, 4),)),
        "w_out": normal_values(seeds[11], (DLAT, DLAT), 2 ** -0.5, 4.0, ((0, 4),)),
        "w_one": normal_values(seeds[12], (DLAT, DLAT), DLAT ** -0.5, 0.15625, ((1, 4),)),
        "w_two": normal_values(seeds[13], (DLAT, DLAT), DLAT ** -0.5, 0.15625, ((0, 4),)),
        "out_grad": normal_values(seeds[14], (ITEMS, LATENTS, DLAT), 1.0, 6.0, ((0, 8),)),
    }


@jax.custom_vjp
def low(v):
    return lax.optimization_barrier(v.astype(jnp.bfloat16)).astype(jnp.float32)

@jax.custom_vjp
def low_back(v):
    return v

def low_keep(v):
    return (low(v), None)

def low_pass(kept, grad):
    return (grad,)

def back_keep(v):
    return (v, None)

def back_low(kept, grad):
    return (low(grad),)
low.defvjp(low_keep, low_pass)
low_back.defvjp(back_keep, back_low)
EPSILON = 1e-05
MASKED = -1e+30
HIGH = lax.Precision.HIGHEST

def normalize(tensor, gain_vec):
    centered = tensor - lax.optimization_barrier(jnp.mean(tensor, axis=-1, keepdims=True))
    inv_std = lax.rsqrt(lax.optimization_barrier(jnp.mean(centered * centered, axis=-1, keepdims=True)) + EPSILON)
    return centered * inv_std * gain_vec

def product(former, latter):
    return jnp.dot(former, latter, precision=HIGH)

def exact_gelu(tensor):
    return jax.nn.gelu(tensor, approximate=False)

def item_forward(parameters, latent_rows, item_ids, item_length):
    byte_table, pos_table, gain_in, gain_lat, gain_mlp, w_query, w_key, w_value, w_out, w_one, w_two = parameters
    inputs = jnp.take(byte_table, item_ids, axis=0) + pos_table
    normed_in = low(normalize(inputs, gain_in))
    key_rows = low_back(low(product(normed_in, w_key)))
    value_rows = low_back(low(product(normed_in, w_value)))
    normed_lat = low(normalize(latent_rows, gain_lat))
    queries = low_back(low(product(normed_lat, w_query)))
    query_heads = queries.reshape(LATENTS, HEADS, QK_DIM)
    key_heads = key_rows.reshape(SLOTS, HEADS, QK_DIM)
    value_heads = value_rows.reshape(SLOTS, HEADS, HEAD_DIM)
    raw_scores = jnp.einsum('qhd,khd->hqk', query_heads, key_heads, precision=HIGH) * QK_DIM ** (-0.5)
    raw_scores = low_back(raw_scores)
    live_keys = jnp.arange(SLOTS, dtype=jnp.int32) < item_length
    scores = jnp.where(live_keys[None, None, :], raw_scores, MASKED)
    row_max = lax.optimization_barrier(jnp.max(scores, axis=-1, keepdims=True))
    raised = jnp.exp(scores - row_max)
    chances = raised / lax.optimization_barrier(jnp.sum(raised, axis=-1, keepdims=True))
    weights = low(chances)
    attended = jnp.einsum('hqk,khd->qhd', weights, value_heads, precision=HIGH).reshape(LATENTS, DLAT)
    attended = low_back(low(attended))
    mixed = low_back(product(attended, w_out))
    hidden = latent_rows + mixed
    normed_mlp = low(normalize(hidden, gain_mlp))
    up_proj = low_back(product(normed_mlp, w_one))
    activated = low(exact_gelu(up_proj))
    return hidden + product(activated, w_two)

def reference(byte_ids, lengths, latents, byte_table, pos_table, gain_in, gain_lat, gain_mlp, w_query, w_key, w_value, w_out, w_one, w_two, out_grad):
    parameters = tuple((p.astype(jnp.float32) for p in (byte_table, pos_table, gain_in, gain_lat, gain_mlp, w_query, w_key, w_value, w_out, w_one, w_two)))

    def scan_step(totals, item):
        item_ids, item_length, item_rows, upstream = item

        def forward_item(tables, latent_rows):
            return item_forward(tables, latent_rows, item_ids, item_length)
        result, pullback = jax.vjp(forward_item, parameters, item_rows.astype(jnp.float32))
        param_grads, row_grad = pullback(upstream.astype(jnp.float32))
        totals = tuple((a + b for a, b in zip(totals, param_grads)))
        return (totals, (result.astype(jnp.bfloat16), row_grad))
    zero_grads = tuple((jnp.zeros_like(p) for p in parameters))
    totals, (outputs, latent_grad) = lax.scan(scan_step, zero_grads, (byte_ids, lengths, latents, out_grad))
    return (outputs, latent_grad, totals[0], totals[1], totals[2], totals[3], totals[4], totals[5], totals[6], totals[7], totals[8], totals[9], totals[10])
```

```python
import jax
import jax.numpy as jnp
from jax import lax
from jax.experimental import pallas as pl
from jax.experimental.pallas import tpu as pltpu
from jax.sharding import PartitionSpec as P

HEADS = 8


EPSILON = 1e-05
MASKED = -1e30


def norm_parts(tensor):
    centered = tensor - jnp.mean(tensor, axis=-1, keepdims=True)
    inv_std = lax.rsqrt(jnp.mean(centered * centered, axis=-1, keepdims=True) + EPSILON)
    return (centered * inv_std, inv_std)


def norm_back(upstream, unit_rows, inv_std, gain_vec):
    scaled = upstream * gain_vec
    row_mean = jnp.mean(scaled, axis=-1, keepdims=True)
    row_cross = jnp.mean(scaled * unit_rows, axis=-1, keepdims=True)
    return inv_std * (scaled - row_mean - unit_rows * row_cross)


def exact_gelu(tensor):
    return jax.nn.gelu(tensor, approximate=False)


def contract(form, first_op, second_op):
    return jnp.einsum(form, first_op, second_op, preferred_element_type=jnp.float32)


def swap(tensor, axis, bit):
    return lax.ppermute(tensor, axis, [(i, i ^ bit) for i in range(lax.axis_size(axis))])


def arrange_kernel(place_ref, own_ref, core_ref, far_ref, far_core_ref, out_ref):
    place = place_ref[0]
    for step, ref in enumerate((own_ref, core_ref, far_ref, far_core_ref)):
        out_ref[place ^ step] = ref[...].astype(out_ref.dtype)


def gather_mp(own):
    rows, cols = own.shape
    core = swap(own, "mp", 1)
    far = swap(own, "mp", 2)
    far_core = swap(far, "mp", 1)
    place = lax.axis_index("mp").astype(jnp.int32).reshape(1)
    return pl.pallas_call(
        arrange_kernel,
        out_shape=jax.ShapeDtypeStruct((4, rows, cols), jnp.bfloat16),
        in_specs=[pl.BlockSpec(memory_space=pltpu.SMEM)] + [pl.BlockSpec(memory_space=pltpu.VMEM)] * 4,
        out_specs=pl.BlockSpec(memory_space=pltpu.VMEM),
        compiler_params=pltpu.CompilerParams(vmem_limit_bytes=40 * 2**20),
    )(place, own, core, far, far_core)


def scatter_sum(blocks, axis):
    count = blocks.shape[0]
    place = lax.axis_index(axis)
    bit = 1
    while count > 1:
        split = blocks.reshape(count // 2, 2, *blocks.shape[1:])
        mine = (place // bit) % 2
        send = lax.dynamic_index_in_dim(split, 1 - mine, 1, False)
        keep = lax.dynamic_index_in_dim(split, mine, 1, False)
        blocks = keep + swap(send, axis, bit)
        count //= 2
        bit *= 2
    return blocks[0]


def sum_dp(tensor):
    bit = 1
    while bit < lax.axis_size("dp"):
        tensor = tensor + swap(tensor, "dp", bit)
        bit *= 2
    return tensor


def body(
    byte_ids,
    lengths,
    latents,
    byte_table,
    pos_table,
    gain_in,
    gain_lat,
    gain_mlp,
    w_query,
    w_key,
    w_value,
    w_out,
    w_one,
    w_two,
    out_grad,
):
    item_count, slot_count = byte_ids.shape
    vocab_size, width_in = byte_table.shape
    width_lat = latents.shape[2]
    local_heads = HEADS // lax.axis_size("mp")
    qk_cols = w_query.shape[1]
    qk_size = qk_cols // local_heads
    val_cols = w_value.shape[1]
    head_size = val_cols // local_heads
    factor = qk_size ** (-0.5)
    mp_place = lax.axis_index("mp")
    f32, bf16 = jnp.float32, jnp.bfloat16

    def whole_rows(own):
        stacked = gather_mp(own.astype(f32))
        return stacked.reshape(-1, own.shape[1])

    w_out_all = whole_rows(w_out)
    w_one_rows = whole_rows(w_one.T)
    w_two_all = whole_rows(w_two)
    w_query_rows = whole_rows(w_query.T)

    one_hot = byte_ids[:, :, None] == lax.iota(jnp.int32, vocab_size)[None, None, :]
    byte_hits = one_hot.astype(bf16)
    inputs = contract("isv,vd->isd", byte_hits, byte_table) + pos_table.astype(f32)[None]
    unit_in, inv_in = norm_parts(inputs)
    normed_in = (unit_in * gain_in).astype(bf16)
    unit_low = unit_in.astype(bf16)
    w_kv = jnp.concatenate([w_key, w_value], axis=1)
    kv_rows = contract("isd,dc->isc", normed_in, w_kv).astype(bf16)
    key_rows, value_rows = kv_rows[..., :qk_cols], kv_rows[..., qk_cols:]
    lat_rows = latents.astype(f32)
    unit_lat, inv_lat = norm_parts(lat_rows)
    normed_lat = (unit_lat * gain_lat).astype(bf16)
    queries = contract("iqd,dc->iqc", normed_lat, w_query).astype(bf16)
    query_heads = queries.reshape(item_count, -1, local_heads, qk_size)
    key_heads = key_rows.reshape(item_count, slot_count, local_heads, qk_size)
    value_heads = value_rows.reshape(item_count, slot_count, local_heads, head_size)
    live_keys = lax.iota(jnp.int32, slot_count)[None, :] < lengths[:, None]

    def scores_of():
        raw_scores = contract("iqhd,ikhd->ihqk", query_heads, key_heads) * factor
        return jnp.where(live_keys[:, None, None, :], raw_scores, MASKED)

    scores = scores_of()
    row_max = jnp.max(scores, axis=-1, keepdims=True)
    raised = jnp.exp(scores - row_max)
    row_total = jnp.sum(raised, axis=-1, keepdims=True)
    weights = (raised / row_total).astype(bf16)
    log_total = row_max + jnp.log(row_total)
    attended = (
        contract("ihqk,ikhd->iqhd", weights, value_heads).astype(bf16).reshape(item_count, -1, val_cols)
    )
    attended_all = gather_mp(attended.astype(f32).reshape(-1, val_cols)).reshape(4, item_count, -1, val_cols)
    attended_all = attended_all.transpose(1, 2, 0, 3).reshape(item_count, -1, width_lat)
    hidden = lat_rows + contract("iqc,cd->iqd", attended_all, w_out_all)
    unit_mlp, inv_mlp = norm_parts(hidden)
    normed_mlp = (unit_mlp * gain_mlp).astype(bf16)
    up_proj = contract("iqd,cd->iqc", normed_mlp, w_one_rows)
    act_value, gelu_pull = jax.vjp(exact_gelu, up_proj)
    activated = act_value.astype(bf16)
    latents_out = (hidden + contract("iqc,cd->iqd", activated, w_two_all)).astype(bf16)
    act_grad = contract("iqd,cd->iqc", out_grad, w_two_all)
    up_grad = gelu_pull(act_grad)[0].astype(bf16)
    mlp_norm_grad = contract("iqc,cd->iqd", up_grad, w_one_rows)
    gain_mlp_grad = jnp.sum(mlp_norm_grad * unit_mlp, axis=(0, 1))
    hidden_grad = out_grad.astype(f32) + norm_back(mlp_norm_grad, unit_mlp, inv_mlp, gain_mlp)
    mixed_grad = hidden_grad.astype(bf16)
    own_cols = lambda t: lax.dynamic_slice_in_dim(t, mp_place * val_cols, val_cols, 2)
    w_two_grad = contract("iqd,iqc->dc", out_grad, own_cols(activated))
    w_one_grad = contract("iqd,iqc->dc", normed_mlp, own_cols(up_grad))
    w_out_grad = contract("iqd,iqc->dc", mixed_grad, attended)
    dp_size = lax.axis_size("dp")

    def rows_dp(tensor):
        return scatter_sum(tensor.reshape(dp_size, -1, tensor.shape[1]), "dp")

    w_two_grad, w_one_grad, w_out_grad = rows_dp(w_two_grad), rows_dp(w_one_grad), rows_dp(w_out_grad)

    attended_grad = contract("iqd,cd->iqc", mixed_grad, w_out).astype(bf16)
    attended_grad = attended_grad.reshape(item_count, -1, local_heads, head_size)
    recomputed = jnp.exp(scores_of() - log_total)
    weights_grad = contract("iqhd,ikhd->ihqk", attended_grad, value_heads)
    row_delta = jnp.sum(recomputed * weights_grad, axis=-1, keepdims=True)
    scores_grad = (recomputed * (weights_grad - row_delta)).astype(bf16)
    query_grad = (contract("ihqk,ikhd->iqhd", scores_grad, key_heads) * factor).astype(bf16)
    query_grad = query_grad.reshape(item_count, -1, qk_cols)
    key_grad = (contract("ihqk,iqhd->ikhd", scores_grad, query_heads) * factor).astype(bf16)
    key_grad = key_grad.reshape(item_count, slot_count, qk_cols)
    value_grad = contract("ihqk,iqhd->ikhd", recomputed.astype(bf16), attended_grad).astype(bf16)
    value_grad = value_grad.reshape(item_count, slot_count, val_cols)
    w_query_grad = rows_dp(contract("iqd,iqc->dc", normed_lat, query_grad))
    query_all = gather_mp(query_grad.astype(f32).reshape(-1, qk_cols)).reshape(4, item_count, -1, qk_cols)
    query_all = query_all.transpose(1, 2, 0, 3).reshape(item_count, -1, qk_cols * 4)
    lat_norm_grad = contract("iqc,cd->iqd", query_all, w_query_rows)
    gain_lat_grad = jnp.sum(lat_norm_grad * unit_lat, axis=(0, 1))
    latent_grad = hidden_grad + norm_back(lat_norm_grad, unit_lat, inv_lat, gain_lat)
    kv_grad = jnp.concatenate([key_grad, value_grad], axis=2)
    unit_kv = contract("isd,isc->dc", unit_low, kv_grad)
    gain_in_grad = jnp.sum(unit_kv * w_kv.astype(f32), axis=1)
    kv_sum = rows_dp(unit_kv * gain_in[:, None])
    in_norm_grad = contract("isc,dc->isd", kv_grad, w_kv)
    inputs_grad = norm_back(in_norm_grad, unit_low.astype(f32), inv_in, gain_in)
    byte_part = contract("isv,isd->vd", byte_hits, inputs_grad.astype(bf16))
    pos_part = jnp.sum(inputs_grad, axis=0)
    both = jnp.concatenate([pos_part, byte_part, gain_in_grad[None]], axis=0)
    mine = scatter_sum(both.reshape(-1, 4, width_in // 4).transpose(1, 0, 2), "mp")
    pos_mine = rows_dp(mine[:slot_count])
    lat_share = width_lat // 4
    gains = jnp.stack([gain_lat_grad, gain_mlp_grad])
    gains = lax.dynamic_slice_in_dim(gains, mp_place * lat_share, lat_share, 1)
    byte_mine, gains = sum_dp(mine[slot_count:]), sum_dp(gains)
    return (
        latents_out,
        latent_grad,
        byte_mine[:vocab_size],
        pos_mine,
        byte_mine[vocab_size],
        gains[0],
        gains[1],
        w_query_grad,
        kv_sum[:, :qk_cols],
        kv_sum[:, qk_cols:],
        w_out_grad.T,
        w_one_grad,
        w_two_grad.T,
    )


def solution(mesh):
    return jax.shard_map(
        body,
        mesh=mesh,
        in_specs=(
            P("dp", None),
            P("dp"),
            P("dp", None, None),
            P(),
            P(),
            P(),
            P(),
            P(),
            P(None, "mp"),
            P(None, "mp"),
            P(None, "mp"),
            P("mp", None),
            P(None, "mp"),
            P("mp", None),
            P("dp", None, None),
        ),
        out_specs=(
            P("dp", None, None),
            P("dp", None, None),
            P(None, "mp"),
            P("dp", "mp"),
            P("mp"),
            P("mp"),
            P("mp"),
            P("dp", "mp"),
            P("dp", "mp"),
            P("dp", "mp"),
            P("mp", "dp"),
            P("dp", "mp"),
            P("mp", "dp"),
        ),
        check_vma=False,
    )
```

```python
import functools

import jax
import jax.numpy as jnp
from jax import lax
from jax.experimental import pallas as pl
from jax.experimental.pallas import tpu as pltpu
from jax.sharding import PartitionSpec as P

HEADS = 8
EPSILON = 1e-05
MASKED = -1e30
LOG2E = 1.4426950408889634
TILE = 512
COST = 11500000000
f32, bf16 = jnp.float32, jnp.bfloat16
ANYWHERE = pl.BlockSpec(memory_space=pl.ANY)


def dot(left, right):
    return jnp.dot(left, right, preferred_element_type=f32)


def dot_nt(left, right):
    return lax.dot_general(left, right, (((1,), (1,)), ((), ())), preferred_element_type=f32)


def dot_tn(left, right):
    return lax.dot_general(left, right, (((0,), (0,)), ((), ())), preferred_element_type=f32)


def cost(microseconds):
    return pl.CostEstimate(flops=microseconds * COST, bytes_accessed=0, transcendentals=0)


def limits(mebibytes):
    return pltpu.CompilerParams(vmem_limit_bytes=mebibytes * 2**20)


def ignoring(kernel, start, count):
    def inner(*refs):
        return kernel(*refs[:start], *refs[start + count :])

    return inner


def row_norm(rows):
    centered = rows - jnp.mean(rows, axis=-1, keepdims=True)
    inv_std = lax.rsqrt(jnp.mean(centered * centered, axis=-1, keepdims=True) + EPSILON)
    return centered * inv_std, inv_std


def row_norm_back(upstream, unit, inv, gain):
    scaled = upstream * gain
    row_mean = jnp.mean(scaled, axis=-1, keepdims=True)
    row_cross = jnp.mean(scaled * unit, axis=-1, keepdims=True)
    return inv * (scaled - row_mean - unit * row_cross)


def front_kernel(
    lengths, ids_ref, table_ref, pos_ref, pos_mean_ref, gain_ref, w_kv_ref, lat_ref, gain_lat_ref, w_query_ref,
    unit_ref, inv_ref, kv_ref, lse_ref, query_ref, query_t_ref, att_ref,
    x_ref, normed_ref, scores_ref, total_ref, peak_ref,
    *, first, width, heads,
):
    step = pl.program_id(1)
    item = first + pl.program_id(0)
    length = lengths[item]
    lat_count = lat_ref.shape[1]
    qk_cols = w_query_ref.shape[0]
    qk = qk_cols // heads
    val = (w_kv_ref.shape[0] - qk_cols) // heads
    scale = qk**-0.5 * LOG2E
    chunk = 64

    @pl.when(step == 0)
    def _():
        unit_lat, _ = row_norm(lat_ref[0].astype(f32))
        queries = dot_nt((unit_lat * gain_lat_ref[...]).astype(bf16), w_query_ref[...])
        query_ref[0] = queries.astype(bf16)
        query_t_ref[0] = queries.T.astype(bf16)
        peak_ref[...] = jnp.full_like(peak_ref, MASKED)

    @pl.when(step * TILE < length)
    def _():
        cols = pl.ds(pl.multiple_of(step * TILE, TILE), TILE)
        hits = (lax.broadcasted_iota(jnp.int32, (table_ref.shape[1], TILE), 0) == ids_ref[pl.ds(item, 1), cols]).astype(bf16)
        x_ref[...] = dot(table_ref[...], hits)
        mean = x_ref[width : width + 1] + x_ref[width + 1 : width + 2] + x_ref[width + 2 : width + 3]
        mean = mean + pos_mean_ref[:, cols]
        square = jnp.zeros((8, TILE), f32)
        for r in range(0, width, chunk):
            rows = x_ref[r : r + chunk] + pos_ref[r : r + chunk].astype(f32) - mean
            x_ref[r : r + chunk] = rows
            rows = rows * rows
            square += sum(rows[i : i + 8] for i in range(0, chunk, 8))
        inv = lax.rsqrt(jnp.sum(square, axis=0, keepdims=True) * (1.0 / width) + EPSILON)
        inv_ref[0, :, cols] = inv
        for r in range(0, width, chunk):
            unit = x_ref[r : r + chunk] * inv
            unit_ref[0, r : r + chunk] = unit.astype(bf16)
            gain = jnp.concatenate([gain_ref[r : r + chunk]] * (TILE // 128), axis=1)
            normed_ref[r : r + chunk] = (unit * gain).astype(bf16)
        kv_ref[0, :, cols] = dot(w_kv_ref[...], normed_ref[...]).astype(bf16)
        live = step * TILE + lax.broadcasted_iota(jnp.int32, (1, TILE), 1) < length
        for h in range(heads):
            scores = dot(query_ref[0, :, h * qk : (h + 1) * qk], kv_ref[0, h * qk : (h + 1) * qk, cols])
            scores = jnp.where(live, scores, MASKED)
            scores_ref[h, :, cols] = scores
            peak = peak_ref[h]
            for c in range(0, TILE, 128):
                peak = jnp.maximum(peak, scores[:, c : c + 128])
            peak_ref[h] = peak

    @pl.when(step == pl.num_programs(1) - 1)
    def _():
        peaks = [jnp.max(peak_ref[h], axis=1, keepdims=True) for h in range(heads)]
        total_ref[...] = jnp.zeros_like(total_ref)

        def attend(t, sums):
            cols = pl.ds(pl.multiple_of(t * TILE, TILE), TILE)
            new = []
            for h in range(heads):
                raised = jnp.exp2((scores_ref[h, :, cols] - peaks[h]) * scale)
                new.append(sums[h] + sum(raised[:, c : c + 128] for c in range(0, TILE, 128)))
                start = qk_cols + h * val
                total_ref[h] += dot_nt(raised.astype(bf16), kv_ref[0, start : start + val, cols])
            return tuple(new)

        sums = lax.fori_loop(0, pl.cdiv(length, TILE), attend, (jnp.zeros((lat_count, 128), f32),) * heads)
        lane = lax.broadcasted_iota(jnp.int32, (lat_count, 128), 1)
        packed = jnp.zeros((lat_count, 128), f32)
        out = []
        for h in range(heads):
            total = jnp.sum(sums[h], axis=1, keepdims=True)
            out.append(total_ref[h] / total)
            packed = jnp.where(lane == h, peaks[h] * scale + jnp.log2(total), packed)
        att_ref[0] = jnp.concatenate(out, axis=1).T
        lse_ref[0] = packed


def front(first, count, lengths, ids, table, pos, pos_mean, gain, w_kv, latents, gain_lat, w_query, heads):
    slots = ids.shape[1]
    width = pos.shape[0]
    lat_count, lat_width = latents.shape[1:]
    qk_cols = w_query.shape[0]
    kv_cols = w_kv.shape[0]
    val_cols = kv_cols - qk_cols
    whole = lambda a: pl.BlockSpec(a.shape, lambda i, t, *_: (0,) * a.ndim)
    each = lambda *s: pl.BlockSpec((1, *s), lambda i, t, *_: (first + i, 0, 0))
    made = lambda *s: pl.BlockSpec((1, *s), lambda i, t, *_: (i, 0, 0))
    shape = lambda s, d: jax.ShapeDtypeStruct((count, *s), d)

    def live(i, t, lengths):
        return jnp.minimum(t, pl.cdiv(lengths[first + i], TILE) - 1)

    return pl.pallas_call(
        functools.partial(front_kernel, first=first, width=width, heads=heads),
        grid_spec=pltpu.PrefetchScalarGridSpec(
            num_scalar_prefetch=1,
            grid=(count, slots // TILE),
            in_specs=[
                whole(ids), whole(table), pl.BlockSpec((width, TILE), lambda i, t, l: (0, live(i, t, l))), whole(pos_mean),
                whole(gain), whole(w_kv), each(lat_count, lat_width), whole(gain_lat), whole(w_query),
            ],
            out_specs=[
                pl.BlockSpec((1, width, TILE), lambda i, t, l: (i, 0, live(i, t, l))), made(1, slots), made(kv_cols, slots),
                made(lat_count, 128), made(lat_count, qk_cols), made(qk_cols, lat_count), made(val_cols, lat_count),
            ],
            scratch_shapes=[
                pltpu.VMEM((table.shape[0], TILE), f32),
                pltpu.VMEM((width, TILE), bf16),
                pltpu.VMEM((heads, lat_count, slots), f32),
                pltpu.VMEM((heads, lat_count, val_cols // heads), f32),
                pltpu.VMEM((heads, lat_count, 128), f32),
            ],
        ),
        out_shape=[
            shape((width, slots), bf16), shape((1, slots), f32), shape((kv_cols, slots), bf16), shape((lat_count, 128), f32),
            shape((lat_count, qk_cols), bf16), shape((qk_cols, lat_count), bf16),
            shape((val_cols, lat_count), f32),
        ],
        compiler_params=limits(56),
        cost_estimate=cost(18),
        name="front",
    )(lengths, ids, table, pos, pos_mean, gain, w_kv, latents, gain_lat, w_query)


def tables_kernel(byte_ref, pos_ref, gain_ref, w_key_ref, w_value_ref, table_ref, pos_t_ref, mean_ref, gains_ref, w_kv_ref, w_back_ref, pad_ref):
    vocab, width = byte_ref.shape

    @pl.when(pl.program_id(0) == 0)
    def _():
        gain = gain_ref[...]
        gains_ref[...] = jnp.broadcast_to(gain, (128, width)).T
        first = w_key_ref.shape[0]
        w_kv_ref[:first] = w_key_ref[...]
        w_kv_ref[first:] = w_value_ref[...]
        scaled = w_kv_ref[...].astype(f32) * gain
        w_back_ref[...] = (scaled - jnp.mean(scaled, axis=1, keepdims=True)).T.astype(bf16)
        pad_ref[...] = jnp.zeros_like(pad_ref)
        pad_ref[:vocab] = byte_ref[...].astype(f32)
        table = pad_ref[...].T
        table_ref[:width] = table[:, : table_ref.shape[1]].astype(bf16)
        mean = jnp.mean(table, axis=0, keepdims=True)[:, : table_ref.shape[1]]
        high = mean.astype(bf16)
        rest = mean - high.astype(f32)
        middle = rest.astype(bf16)
        low = (rest - middle.astype(f32)).astype(bf16)
        more = table_ref.shape[0] - width
        row = lax.broadcasted_iota(jnp.int32, (more, table_ref.shape[1]), 0)
        rows = jnp.zeros(row.shape, f32)
        for place, value in enumerate((high, middle, low)):
            rows = jnp.where(row == place, value.astype(f32), rows)
        table_ref[width:] = rows.astype(bf16)

    pos = pos_ref[...].astype(f32).T
    pos_t_ref[...] = pos.astype(bf16)
    mean_ref[...] = jnp.mean(pos, axis=0, keepdims=True)


def tables_of(byte_table, pos_table, gain, w_key_t, w_value_t):
    vocab, width = byte_table.shape
    slots = pos_table.shape[0]
    kv_cols = w_key_t.shape[0] + w_value_t.shape[0]
    vocab_rows = vocab + -vocab % 16
    whole = lambda a: pl.BlockSpec(a.shape, lambda t: (0,) * a.ndim)
    shapes = [
        ((width + 16, vocab_rows), bf16), ((width, slots), bf16), ((1, slots), f32), ((width, 128), f32), ((kv_cols, width), bf16),
        ((width, kv_cols), bf16),
    ]
    shapes = [jax.ShapeDtypeStruct(*s) for s in shapes]
    specs = [whole(a) for a in shapes]
    specs[1] = pl.BlockSpec((width, TILE), lambda t: (0, t))
    specs[2] = pl.BlockSpec((1, TILE), lambda t: (0, t))
    return pl.pallas_call(
        tables_kernel,
        grid=(slots // TILE,),
        in_specs=[
            whole(byte_table), pl.BlockSpec((TILE, width), lambda t: (t, 0)), whole(gain), whole(w_key_t), whole(w_value_t),
        ],
        out_specs=specs,
        out_shape=shapes,
        scratch_shapes=[pltpu.VMEM((vocab + -vocab % 128, width), f32)],
        compiler_params=limits(40),
        cost_estimate=cost(8),
        name="tables",
    )(byte_table, pos_table, gain, w_key_t, w_value_t)


def back_kernel(
    lengths, ids_ref, w_ref, query_in_ref, byte_in_ref, unit_kv_in_ref, *refs,
    first, heads, groups,
):
    step, item = pl.program_id(0), pl.program_id(1)
    length = lengths[item]
    tile = step + first
    made = [refs[9 * g : 9 * g + 9] for g in range(groups)]
    (
        pos_ref, query_out_ref, byte_ref, unit_kv_ref,
        unit_ref, inv_ref, kv_ref, lse_ref, query_ref, query_t_ref, att_grad_ref, att_grad_t_ref, delta_ref, kv_grad_ref, low_ref,
    ) = refs[9 * groups :]
    width, kv_cols = w_ref.shape
    qk_cols = query_ref.shape[1]
    qk, val = qk_cols // heads, (kv_cols - qk_cols) // heads
    factor = qk**-0.5
    scale = factor * LOG2E
    chunk = 64

    @pl.when((step == 0) & (item == 0))
    def _():
        query_out_ref[...] = query_in_ref[...]
        byte_ref[...] = byte_in_ref[...]
        unit_kv_ref[...] = unit_kv_in_ref[...]

    @pl.when(item == 0)
    def _():
        pos_ref[...] = jnp.zeros_like(pos_ref)

    for g in range(groups):

        @pl.when((tile * TILE < length) & (item // (pl.num_programs(1) // groups) == g))
        def _():
            copies = (unit_ref, inv_ref, kv_ref, lse_ref, query_ref, query_t_ref, att_grad_ref, att_grad_t_ref, delta_ref)
            for target, ref in zip(copies, made[g]):
                target[...] = ref[0]

    @pl.when(tile * TILE < length)
    def _():
        live = tile * TILE + lax.broadcasted_iota(jnp.int32, (1, TILE), 1) < length
        cross = jnp.zeros((8, TILE), f32)
        for h in range(heads):
            keys = slice(h * qk, (h + 1) * qk)
            values = slice(qk_cols + h * val, qk_cols + (h + 1) * val)
            cols = slice(h * val, (h + 1) * val)
            scores = dot(query_ref[:, keys], kv_ref[keys])
            chances = jnp.exp2(scores * scale - lse_ref[:, h : h + 1])
            chances = jnp.where(live, chances, 0.0)
            weights_grad = dot(att_grad_ref[:, cols], kv_ref[values])
            scores_grad = (chances * (weights_grad - delta_ref[:, h : h + 1])).astype(bf16)
            query_out_ref[item, :, keys] += dot_nt(scores_grad, kv_ref[keys])
            kv_grad_ref[keys] = (dot(query_t_ref[keys], scores_grad) * factor).astype(bf16)
            kv_grad_ref[values] = dot(att_grad_t_ref[cols], chances.astype(bf16)).astype(bf16)
        for r in range(0, kv_cols, chunk):
            rows = kv_grad_ref[r : r + chunk].astype(f32) * kv_ref[r : r + chunk].astype(f32)
            cross += sum(rows[i : i + 8] for i in range(0, chunk, 8))
        inv = inv_ref[...]
        cross = jnp.sum(cross, axis=0, keepdims=True) * (1.0 / width) * inv
        back = dot(w_ref[...], kv_grad_ref[...])
        for r in range(0, width, chunk):
            rows = slice(r, r + chunk)
            grads = back[rows] * inv - unit_ref[rows].astype(f32) * cross
            pos_ref[rows] += grads
            low_ref[rows] = grads.astype(bf16)
        hits = (lax.broadcasted_iota(jnp.int32, (byte_ref.shape[1], TILE), 0) == ids_ref[pl.ds(item, 1)]).astype(bf16)
        byte_ref[...] += dot_nt(low_ref[...], hits)
        unit_kv_ref[...] += dot_nt(unit_ref[...], kv_grad_ref[...])


def back(first, count, lengths, ids, made, w_back, sums, heads, tokens):
    items = ids.shape[0]
    groups = len(made)
    size = items // groups
    width, kv_cols = w_back.shape
    lat_count, qk_cols = made[0][4].shape[1:]
    val_cols = kv_cols - qk_cols
    whole = lambda a: pl.BlockSpec(a.shape, lambda t, i, *_: (0,) * a.ndim)
    clip = lambda i, g: jnp.clip(i - g * size, 0, size - 1)
    tiles = lambda g, *s: pl.BlockSpec((1, *s, TILE), lambda t, i, *_: (clip(i, g), 0, t + first))
    each = lambda g, *s: pl.BlockSpec((1, *s), lambda t, i, *_: (clip(i, g), 0, 0))
    shape = lambda s: jax.ShapeDtypeStruct(s, f32)
    kernel = functools.partial(back_kernel, first=first, heads=heads, groups=groups)
    operands = (ids, w_back, *sums, *(a for nine in made for a in nine))
    return pl.pallas_call(
        ignoring(kernel, 1 + len(operands), len(tokens)),
        grid_spec=pltpu.PrefetchScalarGridSpec(
            num_scalar_prefetch=1,
            grid=(count, items),
            in_specs=[
                pl.BlockSpec((items, TILE), lambda t, i, *_: (0, t + first)),
                *(whole(a) for a in (w_back, *sums)),
                *(
                    spec
                    for g in range(groups)
                    for spec in (
                        tiles(g, width), tiles(g, 1), tiles(g, kv_cols), each(g, lat_count, 128), each(g, lat_count, qk_cols),
                        each(g, qk_cols, lat_count), each(g, lat_count, val_cols), each(g, val_cols, lat_count), each(g, lat_count, 128),
                    )
                ),
                *([ANYWHERE] * len(tokens)),
            ],
            out_specs=[pl.BlockSpec((width, TILE), lambda t, i, *_: (0, t)), *(whole(a) for a in sums)],
            scratch_shapes=[
                pltpu.VMEM((width, TILE), bf16), pltpu.VMEM((1, TILE), f32), pltpu.VMEM((kv_cols, TILE), bf16),
                pltpu.VMEM((lat_count, 128), f32), pltpu.VMEM((lat_count, qk_cols), bf16),
                pltpu.VMEM((qk_cols, lat_count), bf16), pltpu.VMEM((lat_count, val_cols), bf16),
                pltpu.VMEM((val_cols, lat_count), bf16), pltpu.VMEM((lat_count, 128), f32),
                pltpu.VMEM((kv_cols, TILE), bf16), pltpu.VMEM((width, TILE), bf16),
            ],
        ),
        out_shape=[shape((width, count * TILE)), *(shape(a.shape) for a in sums)],
        compiler_params=limits(56),
        cost_estimate=cost(12 * count),
        name="back",
    )(lengths, *operands, *tokens)


def assemble_kernel(place_ref, own_ref, *refs):
    *far_refs, out_ref = refs
    side, corner = place_ref[0] // 2, place_ref[1] % 4
    rows = own_ref.shape[0]
    quarter = rows // 4

    def put(start, ref):
        out_ref[pl.ds(pl.multiple_of(start, 16), ref.shape[0])] = ref[...].astype(bf16)

    put(side * rows, own_ref)
    for step, ref in enumerate(far_refs):
        put((1 - side) * rows + (corner ^ step) * quarter, ref)


def assemble(place, own, far, tokens=()):
    rows, width = own.shape
    operands = (own, *far)
    return pl.pallas_call(
        ignoring(assemble_kernel, 1 + len(operands), len(tokens)),
        in_specs=[
            pl.BlockSpec(memory_space=pltpu.SMEM), *([pl.BlockSpec(memory_space=pltpu.VMEM)] * len(operands)),
            *([ANYWHERE] * len(tokens)),
        ],
        out_specs=pl.BlockSpec(memory_space=pltpu.VMEM),
        out_shape=jax.ShapeDtypeStruct((2 * rows, width), bf16),
        compiler_params=limits(40),
        cost_estimate=cost(2),
        name="assemble",
    )(place, *operands, *tokens)


def packed(block):
    rows, cols = block.shape
    parts = [block[:, c : c + 128] for c in range(0, cols - 64, 128)]
    last = block[:, cols - 64 :]
    return jnp.concatenate([*parts, jnp.concatenate([last[: rows // 2], last[rows // 2 :]], axis=1)], axis=0)


def unpacked(block, cols):
    rows = block.shape[0] * 128 // cols
    count = cols // 128
    last = block[count * rows :]
    parts = [block[c * rows : (c + 1) * rows] for c in range(count)]
    return jnp.concatenate([*parts, jnp.concatenate([last[:, :64], last[:, 64:]], axis=0)], axis=1)


def put_blocks(keep_ref, send_ref, total, dp_place):
    count = keep_ref.shape[0]
    size = total.shape[0] // count // 2
    for ref, flip in ((keep_ref, 0), (send_ref, 1)):
        for j in range(count):
            target = lax.rem(dp_place // 2 + j, count) * 2 + (dp_place % 2 ^ flip)
            ref[j] = packed(total[pl.ds(pl.multiple_of(target * size, 8), size)])


def call(kernel, grid, inputs, outputs, scratch=(), tokens=(), name=None, time=1, limit=56):
    whole = lambda a: (a, a.shape, lambda *_: (0,) * a.ndim)
    inputs = [i if isinstance(i, tuple) else whole(i) for i in inputs]
    specs = [pl.BlockSpec(block, index) if block else pl.BlockSpec(memory_space=pltpu.SMEM) for _, block, index in inputs]
    return pl.pallas_call(
        ignoring(kernel, len(inputs), len(tokens)),
        grid=grid,
        in_specs=[*specs, *([ANYWHERE] * len(tokens))],
        out_specs=[pl.BlockSpec(block, index) for _, _, block, index in outputs],
        out_shape=[jax.ShapeDtypeStruct(shape, kind) for shape, kind, _, _ in outputs],
        scratch_shapes=list(scratch),
        compiler_params=limits(limit),
        cost_estimate=cost(time),
        name=name,
    )(*(a for a, _, _ in inputs), *tokens)


def scalars(place):
    return place, None, None


def each(array):
    return array, (1, *array.shape[1:]), lambda i: (i, *(0,) * (array.ndim - 1))


def part(array, first):
    return array, (1, *array.shape[1:]), lambda i: (first + i, *(0,) * (array.ndim - 1))


def new(shape, kind=f32):
    return shape, kind, (1, *shape[1:]), lambda i: (i, *(0,) * (len(shape) - 1))


def kept(shape, kind=f32):
    return shape, kind, shape, lambda i: (0,) * len(shape)


def mix(place, own, far, w_out, tokens=()):
    count, rows, lat_count = own.shape

    def kernel(place_ref, own_ref, far_ref, w_ref, out_ref, att_ref):
        side = place_ref[0] // 2
        for ref, at in ((own_ref, side), (far_ref, 1 - side)):
            att_ref[pl.ds(pl.multiple_of(at * rows, 16), rows)] = ref[0].astype(bf16)
        out_ref[0] = dot_tn(att_ref[...], w_ref[...])

    return call(
        kernel, (count,), [scalars(place), each(own), each(far), w_out], [new((count, lat_count, w_out.shape[1]))],
        [pltpu.VMEM((2 * rows, lat_count), bf16)], tokens, "mix", 3,
    )[0]


def feed(place, first, latents, out_grad, mixed, crossed, gain, w_one, w_two, tokens=()):
    count, lat_count, width = mixed.shape
    rows = w_one.shape[0] // 2

    def kernel(
        place_ref, lat_ref, grad_ref, mixed_ref, crossed_ref, gain_ref, w_one_ref, w_two_ref,
        hidden_ref, normed_ref, activated_ref, share_ref, own_ref, up_own_ref, parts_ref,
    ):
        side = place_ref[0] // 2

        def own(tensor):
            parts_ref[0] = tensor[:, :rows]
            parts_ref[1] = tensor[:, rows:]
            return parts_ref[side]

        hidden = lat_ref[0].astype(f32) + (mixed_ref[0] + crossed_ref[0])
        hidden_ref[0] = hidden
        unit, _ = row_norm(hidden)
        normed = (unit * gain_ref[...]).astype(bf16)
        normed_ref[0] = normed
        up = dot_nt(normed, w_one_ref[...])
        below = 0.5 * (1.0 + lax.erf(up * 0.5**0.5))
        activated = (up * below).astype(bf16)
        activated_ref[0] = activated
        own_ref[0] = own(activated)
        slope = below + up * (jnp.exp(-0.5 * up * up) * 0.3989422804014327)
        up_grad = (dot_nt(grad_ref[0], w_two_ref[...]) * slope).astype(bf16)
        up_own_ref[0] = own(up_grad)
        share_ref[0] = dot(up_grad, w_one_ref[...])

    full, low = (count, lat_count, width), (count, lat_count, rows)
    return call(
        kernel, (count,),
        [scalars(place), part(latents, first), part(out_grad, first), each(mixed), each(crossed), gain, w_one, w_two],
        [new(full), new(full, bf16), new((count, lat_count, 2 * rows), bf16), new(full), new(low, bf16), new(low, bf16)],
        [pltpu.VMEM((2, lat_count, rows), bf16)], tokens, "feed", 6,
    )


def split_grad(blocks, width, rows):
    return kept((blocks // 2, width // blocks * rows // 128, 128))


def feed_weights(place, out_grad, fed, blocks, tokens=()):
    items, lat_count, width = out_grad.shape
    groups = len(fed)
    size = items // groups
    rows = fed[0][1].shape[2]

    def kernel(place_ref, grad_ref, *refs):
        item = pl.program_id(0)
        keep_one, send_one, keep_two, send_two, one_sum, two_sum = refs[3 * groups :]

        @pl.when(item == 0)
        def _():
            one_sum[...] = jnp.zeros_like(one_sum)
            two_sum[...] = jnp.zeros_like(two_sum)

        for g in range(groups):

            @pl.when(item // size == g)
            def _():
                normed_ref, activated_ref, up_grad_ref = refs[3 * g : 3 * g + 3]
                two_sum[...] += dot_tn(grad_ref[0], activated_ref[0])
                one_sum[...] += dot_tn(normed_ref[0], up_grad_ref[0])

        @pl.when(item == items - 1)
        def _():
            put_blocks(keep_two, send_two, two_sum, place_ref[1])
            put_blocks(keep_one, send_one, one_sum, place_ref[1])

    def of(array, g):
        return array, (1, *array.shape[1:]), lambda i: (jnp.clip(i - g * size, 0, size - 1), 0, 0)

    return call(
        kernel, (items,), [scalars(place), each(out_grad), *(of(a, g) for g in range(groups) for a in fed[g])],
        [split_grad(blocks, width, rows)] * 4, [pltpu.VMEM((width, rows), f32)] * 2, tokens, "feed_weights", 6,
    )


def unmix(place, first, out_grad, hidden, share, crossed, gain, w_out, att, before, blocks, heads, tokens=()):
    count, lat_count, width = hidden.shape
    rows = w_out.shape[0]
    val = rows // heads

    def kernel(place_ref, grad_ref, hidden_ref, share_ref, crossed_ref, gain_ref, w_ref, att_ref, gain_in_ref, sum_in_ref, *refs):
        item = pl.program_id(0)
        hidden_grad_ref, att_grad_ref, att_grad_t_ref, delta_ref, gain_grad_ref, sum_ref, *split = refs

        @pl.when(item == 0)
        def _():
            gain_grad_ref[...] = gain_in_ref[...]
            sum_ref[...] = sum_in_ref[...]

        unit, inv = row_norm(hidden_ref[0])
        norm_grad = share_ref[0] + crossed_ref[0]
        gain_grad_ref[...] += jnp.sum(norm_grad * unit, axis=0, keepdims=True)
        hidden_grad = grad_ref[0].astype(f32) + row_norm_back(norm_grad, unit, inv, gain_ref[...])
        hidden_grad_ref[0] = hidden_grad
        mixed_grad = hidden_grad.astype(bf16)
        att = att_ref[0].T
        sum_ref[...] += dot_tn(mixed_grad, att.astype(bf16))
        att_grad = dot_nt(mixed_grad, w_ref[...])
        att_grad_ref[0] = att_grad.astype(bf16)
        att_grad_t_ref[0] = att_grad.T.astype(bf16)
        product = att_grad.astype(bf16).astype(f32) * att
        lane = lax.broadcasted_iota(jnp.int32, delta_ref.shape[1:], 1)
        delta = jnp.zeros(delta_ref.shape[1:], f32)
        for h in range(heads):
            delta = jnp.where(lane == h, jnp.sum(product[:, h * val : (h + 1) * val], axis=1, keepdims=True), delta)
        delta_ref[0] = delta
        if split:

            @pl.when(item == count - 1)
            def _():
                put_blocks(*split, sum_ref, place_ref[1])

    full = (count, lat_count, width)
    return call(
        kernel, (count,),
        [
            scalars(place), part(out_grad, first), each(hidden), each(share), each(crossed), gain, w_out, each(att), *before,
        ],
        [
            new(full), new((count, lat_count, rows), bf16), new((count, rows, lat_count), bf16), new((count, lat_count, 128)),
            kept((1, width)), kept((width, rows)), *([split_grad(blocks, width, rows)] * 2 if first else []),
        ],
        [], tokens, "unmix", 6,
    )


def branch(activated, w_two, tokens=()):
    count, lat_count, _ = activated.shape

    def kernel(activated_ref, w_ref, out_ref):
        out_ref[0] = dot(activated_ref[0], w_ref[...])

    return call(
        kernel, (count,), [each(activated), w_two], [new((count, lat_count, w_two.shape[1]))], [], tokens, "branch", 2
    )[0]


def latent(place, first, query_grad, latents, hidden_grad, gain, w_query, hidden, shares, before, blocks, tokens=()):
    count, lat_count, width = hidden.shape
    rows = w_query[0].shape[0]

    def kernel(
        place_ref, own_ref, core_ref, far_ref, far_core_ref, lat_ref, hidden_grad_ref, gain_ref, w_own, w_core, w_far, w_far_core,
        hidden_ref, share_ref, crossed_ref, gain_in_ref, sum_in_ref, grad_ref, out_ref, gain_grad_ref, sum_ref, *refs,
    ):
        *split, w_ref, parts_ref = refs
        item = pl.program_id(0)
        place = place_ref[0]

        @pl.when(item == 0)
        def _():
            for step, ref in enumerate((w_own, w_core, w_far, w_far_core)):
                w_ref[pl.ds(pl.multiple_of((place ^ step) * rows, rows), rows)] = ref[...].astype(bf16)
            gain_grad_ref[...] = gain_in_ref[...]
            sum_ref[...] = sum_in_ref[...]

        for step, ref in enumerate((own_ref, core_ref, far_ref, far_core_ref)):
            parts_ref[place ^ step] = ref[0].astype(bf16)
        unit, inv = row_norm(lat_ref[0].astype(f32))
        gain = gain_ref[...]
        sum_ref[...] += dot_tn((unit * gain).astype(bf16), own_ref[0].astype(bf16))
        norm_grad = dot(jnp.concatenate([parts_ref[j] for j in range(4)], axis=1), w_ref[...])
        gain_grad_ref[...] += jnp.sum(norm_grad * unit, axis=0, keepdims=True)
        grad_ref[0] = hidden_grad_ref[0] + row_norm_back(norm_grad, unit, inv, gain)
        out_ref[0] = (hidden_ref[0] + (share_ref[0] + crossed_ref[0])).astype(bf16)
        if split:

            @pl.when(item == count - 1)
            def _():
                put_blocks(*split, sum_ref, place_ref[1])

    full = (count, lat_count, width)
    return call(
        kernel, (count,),
        [
            scalars(place), *(part(q, first) for q in query_grad), part(latents, first), each(hidden_grad), gain, *w_query,
            each(hidden), *(each(a) for a in shares), *before,
        ],
        [
            new(full), new(full, bf16), kept((1, width)), kept((width, rows)),
            *([split_grad(blocks, width, rows)] * 2 if first else []),
        ],
        [pltpu.VMEM((4 * rows, width), bf16), pltpu.VMEM((4, lat_count, rows), bf16)], tokens, "latent", 6,
    )


def swap(tensor, axis, bit):
    return lax.ppermute(tensor, axis, [(i, i ^ bit) for i in range(lax.axis_size(axis))])


def ring(tensor):
    count = lax.axis_size("dp")
    return lax.ppermute(tensor, "dp", [(i, (i + 2) % count) for i in range(count)])


def shift(tensor, distance):
    count = lax.axis_size("dp")
    return lax.ppermute(tensor, "dp", [(i, (i + 2 * distance) % count) for i in range(count)])


def gather_mp(own):
    far = swap(own, "mp", 2)
    return own, swap(own, "mp", 1), far, swap(far, "mp", 1)


def ring_sum(blocks):
    total = blocks[-1]
    for j in range(blocks.shape[0] - 2, -1, -1):
        total = blocks[j] + ring(total)
    return total


def sum_dp(tensor):
    bit = 1
    while bit < lax.axis_size("dp"):
        tensor = tensor + swap(tensor, "dp", bit)
        bit *= 2
    return tensor


def split_blocks(blocks, dp_place):
    count = blocks.shape[0] // 2
    pairs = blocks.reshape(count, 2, *blocks.shape[1:])
    pairs = jnp.concatenate([pairs, pairs])
    pairs = lax.dynamic_slice_in_dim(pairs, dp_place // 2, count, 0)
    side = dp_place % 2
    return lax.dynamic_index_in_dim(pairs, side, 1, False), lax.dynamic_index_in_dim(pairs, 1 - side, 1, False)


def stage(always, work):
    shapes = jax.eval_shape(work)
    return lax.cond(always, work, lambda: jax.tree.map(lambda s: jnp.zeros(s.shape, s.dtype), shapes))


def body(
    byte_ids, lengths, latents, byte_table, pos_table, gain_in, gain_lat, gain_mlp,
    w_query, w_key, w_value, w_out, w_one, w_two, out_grad,
):
    items, slots = byte_ids.shape
    vocab, width = byte_table.shape
    lat_count, lat_width = latents.shape[1:]
    mp, dp = lax.axis_size("mp"), lax.axis_size("dp")
    mp_place, dp_place = lax.axis_index("mp"), lax.axis_index("dp")
    place = jnp.stack([mp_place, dp_place]).astype(jnp.int32)
    heads = HEADS // mp
    qk_cols = w_query.shape[1]
    val_cols = w_value.shape[1]
    corner = dp_place % 4

    shards = [w_out, w_one.T, w_two]
    quarter = val_cols // 4
    always = lengths[0] > 0
    over_y = lambda w: swap(lax.dynamic_slice_in_dim(w, corner * quarter, quarter, 0).astype(f32), "mp", 2)
    over_x, over_z, over_both = (lambda a, bits=bits: swap(a, "dp", bits) for bits in (1, 2, 3))
    core = lambda a: swap(a, "mp", 1)
    half = items // 2

    def first_stage():
        return over_y(shards[0]), tables_of(byte_table, pos_table, gain_in[None], w_key.T, w_value.T)

    out, (*tables, w_back) = stage(always, first_stage)

    def front_of(first):
        return front(first, half, lengths, byte_ids, *tables, latents, gain_lat[None], w_query.T, heads)

    def second_stage():
        return front_of(0), [over_x(out), over_z(out)], over_y(shards[1]), over_y(shards[2])

    (*made_a, att_a), crossed_out, one, two = stage(always, second_stage)

    def third_stage():
        return front_of(half), over_both(out), [over_x(one), over_z(one), over_both(one)], swap(att_a, "mp", 2)

    (*made_b, att_b), last_out, crossed_one, far_a = stage(always, third_stage)
    far_b = swap(att_b, "mp", 2)
    crossed_two = [over_x(two), over_z(two), over_both(two)]
    w_out_whole = assemble(place, shards[0], [out, *crossed_out, last_out])
    mixed_a = mix(place, att_a, far_a, w_out_whole)
    w_one_whole = assemble(place, shards[1], [one, *crossed_one], [mixed_a])
    w_two_whole = assemble(place, shards[2], [two, *crossed_two], [w_one_whole])
    mixed_b = mix(place, att_b, far_b, w_out_whole, [w_two_whole])
    gain = gain_mlp[None]
    weights = (gain, w_one_whole, w_two_whole)
    hidden_a, normed_a, activated_a, share_a, act_a, up_a = feed(
        place, 0, latents, out_grad, mixed_a, core(mixed_a), *weights, [mixed_b]
    )
    hidden_b, normed_b, activated_b, share_b, act_b, up_b = feed(
        place, half, latents, out_grad, mixed_b, core(mixed_b), *weights, [share_a]
    )
    keep_one, send_one, keep_two, send_two = feed_weights(
        place, out_grad, [(normed_a, act_a, up_a), (normed_b, act_b, up_b)], dp
    )
    zeros = [jnp.zeros((1, lat_width), f32), jnp.zeros((lat_width, val_cols), f32)]
    crossed_a, crossed_b = core(share_a), core(share_b)

    def unmix_stage():
        grads_a = unmix(place, 0, out_grad, hidden_a, share_a, crossed_a, gain, w_out, att_a, zeros, dp, heads)
        grads_b = unmix(place, half, out_grad, hidden_b, share_b, crossed_b, gain, w_out, att_b, grads_a[4:], dp, heads)
        return grads_a[:4], grads_b[:5], grads_b[6:], swap(send_two, "dp", 1)

    (hidden_grad_a, *grads_a), (hidden_grad_b, *grads_b, gain_mlp_grad), (keep_out, send_out), cross_two = stage(
        always, unmix_stage
    )
    made = [(*made_a, *grads_a), (*made_b, *grads_b)]
    byte_cols = vocab + -vocab % 128
    kv_cols = qk_cols + val_cols
    sums = [jnp.zeros(s, f32) for s in ((items, lat_count, qk_cols), (width, byte_cols), (width, kv_cols))]

    def back_of(first, count, sums):
        return back(first, count, lengths, byte_ids, made, w_back, sums, heads, [])

    def spread_z(blocks):
        return [blocks[0]] + [shift(blocks[j], j) for j in range(1, blocks.shape[0])]

    def sum_mp(whole):
        whole = whole.reshape(2, 2, width // mp, -1)
        far, near = mp_place // 2, mp_place % 2
        pick = lambda a, i, axis: lax.dynamic_index_in_dim(a, i, axis, False)
        whole = pick(whole, near, 1) + swap(pick(whole, 1 - near, 1), "mp", 1)
        return pick(whole, far, 0) + swap(pick(whole, 1 - far, 0), "mp", 2)

    two_blocks = keep_two + cross_two

    def back_stage_a():
        return back_of(0, 2, sums), swap(send_one, "dp", 1), spread_z(two_blocks)

    (pos_a, *sums), cross_one, two_parts = stage(always, back_stage_a)
    one_blocks = keep_one + cross_one

    def back_stage_b():
        return back_of(2, 1, sums), swap(send_out, "dp", 1), spread_z(one_blocks)

    (pos_b, *sums), cross_out, one_parts = stage(always, back_stage_b)
    out_blocks = keep_out + cross_out

    def back_stage_c():
        return back_of(3, 1, sums), spread_z(out_blocks)

    (pos_c, *sums), out_parts = stage(always, back_stage_c)
    pos_parts = [pos_a, pos_b, pos_c]
    two_sum, one_sum, out_sum = sum(two_parts), sum(one_parts), sum(out_parts)
    query_grad, byte_part, unit_kv = sums
    query_grad = (query_grad * (qk_cols // heads) ** -0.5).astype(bf16).astype(f32)
    w_query_all = gather_mp(w_query.T.astype(f32))
    query_all = gather_mp(query_grad)
    zeros = [jnp.zeros((1, lat_width), f32), jnp.zeros((lat_width, qk_cols), f32)]
    branch_a, branch_b = branch(activated_a, w_two_whole), branch(activated_b, w_two_whole)
    latent_grad_a, out_a, *before = latent(
        place, 0, query_all, latents, hidden_grad_a, gain_lat[None], w_query_all, hidden_a, (branch_a, core(branch_a)), zeros, dp
    )
    latent_grad_b, out_b, gain_lat_grad, _, keep_query, send_query = latent(
        place, half, query_all, latents, hidden_grad_b, gain_lat[None], w_query_all, hidden_b, (branch_b, core(branch_b)),
        before, dp,
    )
    latent_grad, latents_out = jnp.concatenate([latent_grad_a, latent_grad_b]), jnp.concatenate([out_a, out_b])
    w_kv = jnp.concatenate([w_key, w_value], axis=1)
    query_sum = ring_sum(keep_query + swap(send_query, "dp", 1))
    gain_part = jnp.sum(unit_kv * w_kv.astype(f32), axis=1, keepdims=True)
    keep_kv, send_kv = split_blocks((unit_kv * gain_in[:, None]).reshape(dp, -1, w_kv.shape[1]), dp_place)
    kv_sum = ring_sum(keep_kv + swap(send_kv, "dp", 1))
    byte_part = lax.dynamic_update_slice(byte_part, gain_part, (0, vocab))

    pos_mine = jnp.concatenate([sum_mp(p) for p in pos_parts], axis=1)
    keep_pos, send_pos = split_blocks(pos_mine.reshape(-1, dp, slots // dp).swapaxes(0, 1), dp_place)
    pos_sum = ring_sum(keep_pos + swap(send_pos, "dp", 1))
    byte_mine = sum_dp(sum_mp(byte_part))
    gains = jnp.concatenate([gain_lat_grad, gain_mlp_grad])
    gains = sum_dp(lax.dynamic_slice_in_dim(gains, mp_place * val_cols, val_cols, 1))
    return (
        latents_out, latent_grad, byte_mine[:, :vocab].T, pos_sum.T, byte_mine[:, vocab], gains[0], gains[1],
        unpacked(query_sum, qk_cols), kv_sum[:, :qk_cols], kv_sum[:, qk_cols:], unpacked(out_sum, val_cols).T,
        unpacked(one_sum, val_cols), unpacked(two_sum, val_cols).T,
    )


def solution(mesh):
    return jax.shard_map(
        body,
        mesh=mesh,
        in_specs=(
            P("dp", None),
            P("dp"),
            P("dp", None, None),
            P(),
            P(),
            P(),
            P(),
            P(),
            P(None, "mp"),
            P(None, "mp"),
            P(None, "mp"),
            P("mp", None),
            P(None, "mp"),
            P("mp", None),
            P("dp", None, None),
        ),
        out_specs=(
            P("dp", None, None),
            P("dp", None, None),
            P(None, "mp"),
            P("dp", "mp"),
            P("mp"),
            P("mp"),
            P("mp"),
            P("dp", "mp"),
            P("dp", "mp"),
            P("dp", "mp"),
            P("mp", "dp"),
            P("dp", "mp"),
            P("mp", "dp"),
        ),
        check_vma=False,
    )
```

```python
import functools

import jax
import jax.numpy as jnp
from jax import lax
from jax.experimental import pallas as pl
from jax.experimental.pallas import tpu as pltpu
from jax.sharding import PartitionSpec as P

HEADS = 8
EPSILON = 1e-05
MASKED = -1e30
LOG2E = 1.4426950408889634
TILE = 512
COST = 11500000000
f32, bf16 = jnp.float32, jnp.bfloat16
ANYWHERE = pl.BlockSpec(memory_space=pl.ANY)


def dot(left, right):
    return jnp.dot(left, right, preferred_element_type=f32)


def dot_nt(left, right):
    return lax.dot_general(left, right, (((1,), (1,)), ((), ())), preferred_element_type=f32)


def dot_tn(left, right):
    return lax.dot_general(left, right, (((0,), (0,)), ((), ())), preferred_element_type=f32)


def cost(microseconds):
    return pl.CostEstimate(flops=microseconds * COST, bytes_accessed=0, transcendentals=0)


def limits(mebibytes):
    return pltpu.CompilerParams(vmem_limit_bytes=mebibytes * 2**20)


def ignoring(kernel, start, count):
    def inner(*refs):
        return kernel(*refs[:start], *refs[start + count :])

    return inner


def row_norm(rows):
    centered = rows - jnp.mean(rows, axis=-1, keepdims=True)
    inv_std = lax.rsqrt(jnp.mean(centered * centered, axis=-1, keepdims=True) + EPSILON)
    return centered * inv_std, inv_std


def row_norm_back(upstream, unit, inv, gain):
    scaled = upstream * gain
    row_mean = jnp.mean(scaled, axis=-1, keepdims=True)
    row_cross = jnp.mean(scaled * unit, axis=-1, keepdims=True)
    return inv * (scaled - row_mean - unit * row_cross)


def front_kernel(
    lengths, ids_ref, table_ref, pos_ref, pos_mean_ref, gain_ref, w_kv_ref, lat_ref, gain_lat_ref, w_query_ref,
    unit_ref, inv_ref, kv_ref, lse_ref, query_ref, query_t_ref, att_ref,
    x_ref, normed_ref, scores_ref, total_ref, peak_ref,
    *, first, width, heads,
):
    step = pl.program_id(1)
    item = first + pl.program_id(0)
    length = lengths[item]
    lat_count = lat_ref.shape[1]
    qk_cols = w_query_ref.shape[0]
    qk = qk_cols // heads
    val = (w_kv_ref.shape[0] - qk_cols) // heads
    scale = qk**-0.5 * LOG2E
    chunk = 64

    @pl.when(step == 0)
    def _():
        unit_lat, _ = row_norm(lat_ref[0].astype(f32))
        queries = dot_nt((unit_lat * gain_lat_ref[...]).astype(bf16), w_query_ref[...])
        query_ref[0] = queries.astype(bf16)
        query_t_ref[0] = queries.T.astype(bf16)
        peak_ref[...] = jnp.full_like(peak_ref, MASKED)

    @pl.when(step * TILE < length)
    def _():
        cols = pl.ds(pl.multiple_of(step * TILE, TILE), TILE)
        hits = (lax.broadcasted_iota(jnp.int32, (table_ref.shape[1], TILE), 0) == ids_ref[pl.ds(item, 1), cols]).astype(bf16)
        x_ref[...] = dot(table_ref[...], hits)
        mean = x_ref[width : width + 1] + x_ref[width + 1 : width + 2] + x_ref[width + 2 : width + 3]
        mean = mean + pos_mean_ref[:, cols]
        square = jnp.zeros((8, TILE), f32)
        for r in range(0, width, chunk):
            rows = x_ref[r : r + chunk] + pos_ref[r : r + chunk].astype(f32) - mean
            x_ref[r : r + chunk] = rows
            rows = rows * rows
            square += sum(rows[i : i + 8] for i in range(0, chunk, 8))
        inv = lax.rsqrt(jnp.sum(square, axis=0, keepdims=True) * (1.0 / width) + EPSILON)
        inv_ref[0, :, cols] = inv
        for r in range(0, width, chunk):
            unit = x_ref[r : r + chunk] * inv
            unit_ref[0, r : r + chunk] = unit.astype(bf16)
            gain = jnp.concatenate([gain_ref[r : r + chunk]] * (TILE // 128), axis=1)
            normed_ref[r : r + chunk] = (unit * gain).astype(bf16)
        kv_ref[0, :, cols] = dot(w_kv_ref[...], normed_ref[...]).astype(bf16)
        live = step * TILE + lax.broadcasted_iota(jnp.int32, (1, TILE), 1) < length
        for h in range(heads):
            scores = dot(query_ref[0, :, h * qk : (h + 1) * qk], kv_ref[0, h * qk : (h + 1) * qk, cols])
            scores = jnp.where(live, scores, MASKED)
            scores_ref[h, :, cols] = scores
            peak = peak_ref[h]
            for c in range(0, TILE, 128):
                peak = jnp.maximum(peak, scores[:, c : c + 128])
            peak_ref[h] = peak

    @pl.when(step == pl.num_programs(1) - 1)
    def _():
        peaks = [jnp.max(peak_ref[h], axis=1, keepdims=True) for h in range(heads)]
        total_ref[...] = jnp.zeros_like(total_ref)

        def attend(t, sums):
            cols = pl.ds(pl.multiple_of(t * TILE, TILE), TILE)
            new = []
            for h in range(heads):
                raised = jnp.exp2((scores_ref[h, :, cols] - peaks[h]) * scale)
                new.append(sums[h] + sum(raised[:, c : c + 128] for c in range(0, TILE, 128)))
                start = qk_cols + h * val
                total_ref[h] += dot_nt(raised.astype(bf16), kv_ref[0, start : start + val, cols])
            return tuple(new)

        sums = lax.fori_loop(0, pl.cdiv(length, TILE), attend, (jnp.zeros((lat_count, 128), f32),) * heads)
        lane = lax.broadcasted_iota(jnp.int32, (lat_count, 128), 1)
        packed = jnp.zeros((lat_count, 128), f32)
        out = []
        for h in range(heads):
            total = jnp.sum(sums[h], axis=1, keepdims=True)
            out.append(total_ref[h] / total)
            packed = jnp.where(lane == h, peaks[h] * scale + jnp.log2(total), packed)
        att_ref[0] = jnp.concatenate(out, axis=1).T
        lse_ref[0] = packed


def front(first, count, lengths, ids, table, pos, pos_mean, gain, w_kv, latents, gain_lat, w_query, heads):
    slots = ids.shape[1]
    width = pos.shape[0]
    lat_count, lat_width = latents.shape[1:]
    qk_cols = w_query.shape[0]
    kv_cols = w_kv.shape[0]
    val_cols = kv_cols - qk_cols
    whole = lambda a: pl.BlockSpec(a.shape, lambda i, t, *_: (0,) * a.ndim)
    each = lambda *s: pl.BlockSpec((1, *s), lambda i, t, *_: (first + i, 0, 0))
    made = lambda *s: pl.BlockSpec((1, *s), lambda i, t, *_: (i, 0, 0))
    shape = lambda s, d: jax.ShapeDtypeStruct((count, *s), d)

    def live(i, t, lengths):
        return jnp.minimum(t, pl.cdiv(lengths[first + i], TILE) - 1)

    return pl.pallas_call(
        functools.partial(front_kernel, first=first, width=width, heads=heads),
        grid_spec=pltpu.PrefetchScalarGridSpec(
            num_scalar_prefetch=1,
            grid=(count, slots // TILE),
            in_specs=[
                whole(ids), whole(table), pl.BlockSpec((width, TILE), lambda i, t, l: (0, live(i, t, l))), whole(pos_mean),
                whole(gain), whole(w_kv), each(lat_count, lat_width), whole(gain_lat), whole(w_query),
            ],
            out_specs=[
                pl.BlockSpec((1, width, TILE), lambda i, t, l: (i, 0, live(i, t, l))), made(1, slots), made(kv_cols, slots),
                made(lat_count, 128), made(lat_count, qk_cols), made(qk_cols, lat_count), made(val_cols, lat_count),
            ],
            scratch_shapes=[
                pltpu.VMEM((table.shape[0], TILE), f32),
                pltpu.VMEM((width, TILE), bf16),
                pltpu.VMEM((heads, lat_count, slots), f32),
                pltpu.VMEM((heads, lat_count, val_cols // heads), f32),
                pltpu.VMEM((heads, lat_count, 128), f32),
            ],
        ),
        out_shape=[
            shape((width, slots), bf16), shape((1, slots), f32), shape((kv_cols, slots), bf16), shape((lat_count, 128), f32),
            shape((lat_count, qk_cols), bf16), shape((qk_cols, lat_count), bf16),
            shape((val_cols, lat_count), f32),
        ],
        compiler_params=limits(56),
        cost_estimate=cost(18),
        name="front",
    )(lengths, ids, table, pos, pos_mean, gain, w_kv, latents, gain_lat, w_query)


def tables_kernel(
    place_ref, byte_ref, pos_ref, gain_ref, w_key_ref, w_value_ref, w_one_ref, w_two_ref, table_ref, pos_t_ref, mean_ref, gains_ref, w_kv_ref, w_back_ref,
    w_rows_ref, one_ref, two_ref, pad_ref,
):
    vocab, width = byte_ref.shape

    @pl.when(pl.program_id(0) == 0)
    def _():
        rows = one_ref.shape[0]
        quarter = pl.ds(pl.multiple_of(place_ref[1] % 4 * rows, 16), rows)
        one_ref[...] = w_one_ref[quarter].astype(f32)
        two_ref[...] = w_two_ref[quarter].astype(f32)
        gain = gain_ref[...]
        gains_ref[...] = jnp.broadcast_to(gain, (128, width)).T
        first = w_key_ref.shape[0]
        w_kv_ref[:first] = w_key_ref[...]
        w_kv_ref[first:] = w_value_ref[...]
        w_rows_ref[...] = w_kv_ref[...].astype(f32).T.astype(bf16)
        scaled = w_kv_ref[...].astype(f32) * gain
        w_back_ref[...] = (scaled - jnp.mean(scaled, axis=1, keepdims=True)).T.astype(bf16)
        pad_ref[...] = jnp.zeros_like(pad_ref)
        pad_ref[:vocab] = byte_ref[...].astype(f32)
        table = pad_ref[...].T
        table_ref[:width] = table[:, : table_ref.shape[1]].astype(bf16)
        mean = jnp.mean(table, axis=0, keepdims=True)[:, : table_ref.shape[1]]
        high = mean.astype(bf16)
        rest = mean - high.astype(f32)
        middle = rest.astype(bf16)
        low = (rest - middle.astype(f32)).astype(bf16)
        more = table_ref.shape[0] - width
        row = lax.broadcasted_iota(jnp.int32, (more, table_ref.shape[1]), 0)
        rows = jnp.zeros(row.shape, f32)
        for place, value in enumerate((high, middle, low)):
            rows = jnp.where(row == place, value.astype(f32), rows)
        table_ref[width:] = rows.astype(bf16)

    pos = pos_ref[...].astype(f32).T
    pos_t_ref[...] = pos.astype(bf16)
    mean_ref[...] = jnp.mean(pos, axis=0, keepdims=True)


def tables_of(place, byte_table, pos_table, gain, w_key_t, w_value_t, w_one_t, w_two):
    vocab, width = byte_table.shape
    slots = pos_table.shape[0]
    kv_cols = w_key_t.shape[0] + w_value_t.shape[0]
    vocab_rows = vocab + -vocab % 16
    whole = lambda a: pl.BlockSpec(a.shape, lambda t: (0,) * a.ndim)
    shapes = [
        ((width + 16, vocab_rows), bf16), ((width, slots), bf16), ((1, slots), f32), ((width, 128), f32), ((kv_cols, width), bf16),
        ((width, kv_cols), bf16), ((width, kv_cols), bf16), *([((w_two.shape[0] // 4, w_two.shape[1]), f32)] * 2),
    ]
    shapes = [jax.ShapeDtypeStruct(*s) for s in shapes]
    specs = [whole(a) for a in shapes]
    specs[1] = pl.BlockSpec((width, TILE), lambda t: (0, t))
    specs[2] = pl.BlockSpec((1, TILE), lambda t: (0, t))
    return pl.pallas_call(
        tables_kernel,
        grid=(slots // TILE,),
        in_specs=[
            pl.BlockSpec(memory_space=pltpu.SMEM), whole(byte_table), pl.BlockSpec((TILE, width), lambda t: (t, 0)), whole(gain),
            whole(w_key_t), whole(w_value_t), whole(w_one_t), whole(w_two),
        ],
        out_specs=specs,
        out_shape=shapes,
        scratch_shapes=[pltpu.VMEM((vocab + -vocab % 128, width), f32)],
        compiler_params=limits(40),
        cost_estimate=cost(8),
        name="tables",
    )(place, byte_table, pos_table, gain, w_key_t, w_value_t, w_one_t, w_two)


def back_kernel(
    lengths, place_ref, ids_ref, w_ref, w_rows_ref, gain_ref, *refs,
    first, heads, groups, last, vocab,
):
    step, item = pl.program_id(0), pl.program_id(1)
    length = lengths[item]
    tile = step + first
    sums_in, refs = (refs[:3], refs[3:]) if first else ((), refs)
    made = [refs[9 * g : 9 * g + 9] for g in range(groups)]
    refs = refs[9 * groups :]
    pos_ref, query_out_ref, *refs = refs
    if last:
        keep_ref, send_ref, *refs, byte_ref, unit_kv_ref = refs
    else:
        byte_ref, unit_kv_ref, *refs = refs
    (
        unit_ref, inv_ref, kv_ref, lse_ref, query_ref, query_t_ref, att_grad_ref, att_grad_t_ref, delta_ref, kv_grad_ref, low_ref,
    ) = refs
    width, kv_cols = w_ref.shape
    qk_cols = query_ref.shape[1]
    qk, val = qk_cols // heads, (kv_cols - qk_cols) // heads
    factor = qk**-0.5
    scale = factor * LOG2E
    chunk = 64
    share = pos_ref.shape[1]

    def order(block):
        distance = place_ref[0] ^ block
        return distance % 2 * 2 + distance // 2

    @pl.when((step == 0) & (item == 0))
    def _():
        for i, ref in enumerate((query_out_ref, byte_ref, unit_kv_ref)):
            ref[...] = sums_in[i][...] if first else jnp.zeros_like(ref)

    @pl.when(item == 0)
    def _():
        pos_ref[:, :, :TILE] = jnp.zeros((4, share, TILE), f32)

    for g in range(groups):

        @pl.when((tile * TILE < length) & (item // (pl.num_programs(1) // groups) == g))
        def _():
            copies = (unit_ref, inv_ref, kv_ref, lse_ref, query_ref, query_t_ref, att_grad_ref, att_grad_t_ref, delta_ref)
            for target, ref in zip(copies, made[g]):
                target[...] = ref[0]

    @pl.when(tile * TILE < length)
    def _():
        live = tile * TILE + lax.broadcasted_iota(jnp.int32, (1, TILE), 1) < length
        cross = jnp.zeros((8, TILE), f32)
        for h in range(heads):
            keys = slice(h * qk, (h + 1) * qk)
            values = slice(qk_cols + h * val, qk_cols + (h + 1) * val)
            cols = slice(h * val, (h + 1) * val)
            scores = dot(query_ref[:, keys], kv_ref[keys])
            chances = jnp.exp2(scores * scale - lse_ref[:, h : h + 1])
            chances = jnp.where(live, chances, 0.0)
            weights_grad = dot(att_grad_ref[:, cols], kv_ref[values])
            scores_grad = (chances * (weights_grad - delta_ref[:, h : h + 1])).astype(bf16)
            query_out_ref[item, keys] += dot_nt(kv_ref[keys], scores_grad)
            kv_grad_ref[keys] = (dot(query_t_ref[keys], scores_grad) * factor).astype(bf16)
            kv_grad_ref[values] = dot(att_grad_t_ref[cols], chances.astype(bf16)).astype(bf16)
        for r in range(0, kv_cols, chunk):
            rows = kv_grad_ref[r : r + chunk].astype(f32) * kv_ref[r : r + chunk].astype(f32)
            cross += sum(rows[i : i + 8] for i in range(0, chunk, 8))
        inv = inv_ref[...]
        cross = jnp.sum(cross, axis=0, keepdims=True) * (1.0 / width) * inv
        back = dot(w_ref[...], kv_grad_ref[...])
        for r in range(0, width, chunk):
            rows = slice(r, r + chunk)
            grads = back[rows] * inv - unit_ref[rows].astype(f32) * cross
            pos_ref[order(r // share), r % share : r % share + chunk, :TILE] += grads
            low_ref[rows] = grads.astype(bf16)
        hits = (lax.broadcasted_iota(jnp.int32, (byte_ref.shape[1], TILE), 0) == ids_ref[pl.ds(item, 1)]).astype(bf16)
        byte_ref[...] += dot_nt(low_ref[...], hits)
        unit_kv_ref[...] += dot_nt(unit_ref[...], kv_grad_ref[...])

    if last:

        @pl.when((step == pl.num_programs(0) - 1) & (item == pl.num_programs(1) - 1))
        def _():
            query_out_ref[...] = (query_out_ref[...] * factor).astype(bf16).astype(f32)
            lane = lax.broadcasted_iota(jnp.int32, byte_ref.shape, 1)
            gain_grad = jnp.sum(unit_kv_ref[...] * w_rows_ref[...].astype(f32), axis=1, keepdims=True)
            byte_ref[...] = jnp.where(lane == vocab, gain_grad, byte_ref[...])
            for block in range(4):
                pos_ref[order(block), :, TILE:] = byte_ref[block * share : (block + 1) * share]
            unit_kv_ref[...] *= gain_ref[:, :1]
            split_blocks(keep_ref, send_ref, unit_kv_ref, place_ref[1])


def back(place, first, count, lengths, ids, made, w_back, w_rows, gains, sums, heads, vocab):
    items, slots = ids.shape
    last = (first + count) * TILE == slots
    groups = len(made)
    size = items // groups
    width, kv_cols = w_back.shape
    lat_count, qk_cols = made[0][4].shape[1:]
    val_cols = kv_cols - qk_cols
    whole = lambda a: pl.BlockSpec(a.shape, lambda t, i, *_: (0,) * a.ndim)
    clip = lambda i, g: jnp.clip(i - g * size, 0, size - 1)
    tiles = lambda g, *s: pl.BlockSpec((1, *s, TILE), lambda t, i, *_: (clip(i, g), 0, t + first))
    each = lambda g, *s: pl.BlockSpec((1, *s), lambda t, i, *_: (clip(i, g), 0, 0))
    shape = lambda s: jax.ShapeDtypeStruct(s, f32)
    kernel = functools.partial(back_kernel, first=first, heads=heads, groups=groups, last=last, vocab=vocab)
    operands = (ids, w_back, w_rows, gains, *sums, *(a for nine in made for a in nine))
    byte_cols = vocab + -vocab % 128
    query_sum, byte_sum, unit_kv = (shape(a) for a in ((items, qk_cols, lat_count), (width, byte_cols), (width, kv_cols)))
    blocks = lax.axis_size("dp")
    if last:
        assert count == 1
        split = shape((blocks // 2, width // blocks, kv_cols))
        out_shape = [shape((4, width // 4, TILE + byte_sum.shape[1])), query_sum, split, split]
        out_specs = [whole(a) for a in out_shape]
    else:
        out_shape = [shape((4, width // 4, count * TILE)), query_sum, byte_sum, unit_kv]
        out_specs = [pl.BlockSpec((4, width // 4, TILE), lambda t, i, *_: (0, 0, t)), *(whole(a) for a in out_shape[1:])]
    return pl.pallas_call(
        kernel,
        grid_spec=pltpu.PrefetchScalarGridSpec(
            num_scalar_prefetch=2,
            grid=(count, items),
            in_specs=[
                pl.BlockSpec((items, TILE), lambda t, i, *_: (0, t + first)),
                *(whole(a) for a in (w_back, w_rows, gains, *sums)),
                *(
                    spec
                    for g in range(groups)
                    for spec in (
                        tiles(g, width), tiles(g, 1), tiles(g, kv_cols), each(g, lat_count, 128), each(g, lat_count, qk_cols),
                        each(g, qk_cols, lat_count), each(g, lat_count, val_cols), each(g, val_cols, lat_count), each(g, lat_count, 128),
                    )
                ),
            ],
            out_specs=out_specs,
            scratch_shapes=[
                pltpu.VMEM((width, TILE), bf16), pltpu.VMEM((1, TILE), f32), pltpu.VMEM((kv_cols, TILE), bf16),
                pltpu.VMEM((lat_count, 128), f32), pltpu.VMEM((lat_count, qk_cols), bf16),
                pltpu.VMEM((qk_cols, lat_count), bf16), pltpu.VMEM((lat_count, val_cols), bf16),
                pltpu.VMEM((val_cols, lat_count), bf16), pltpu.VMEM((lat_count, 128), f32),
                pltpu.VMEM((kv_cols, TILE), bf16), pltpu.VMEM((width, TILE), bf16),
                *([pltpu.VMEM(a.shape, f32) for a in (byte_sum, unit_kv)] if last else []),
            ],
        ),
        out_shape=out_shape,
        compiler_params=limits(58),
        cost_estimate=cost(12 * count),
        name="back",
    )(lengths, place, *operands)


def assemble_kernel(place_ref, own_ref, *refs):
    *far_refs, out_ref = refs
    side, corner = place_ref[0] // 2, place_ref[1] % 4
    rows = own_ref.shape[0]
    quarter = rows // 4

    def put(start, ref):
        out_ref[pl.ds(pl.multiple_of(start, 16), ref.shape[0])] = ref[...].astype(bf16)

    put(side * rows, own_ref)
    for step, ref in enumerate(far_refs):
        put((1 - side) * rows + (corner ^ step) * quarter, ref)


def assemble(place, own, far, tokens=()):
    rows, width = own.shape
    operands = (own, *far)
    return pl.pallas_call(
        ignoring(assemble_kernel, 1 + len(operands), len(tokens)),
        in_specs=[
            pl.BlockSpec(memory_space=pltpu.SMEM), *([pl.BlockSpec(memory_space=pltpu.VMEM)] * len(operands)),
            *([ANYWHERE] * len(tokens)),
        ],
        out_specs=pl.BlockSpec(memory_space=pltpu.VMEM),
        out_shape=jax.ShapeDtypeStruct((2 * rows, width), bf16),
        compiler_params=limits(40),
        cost_estimate=cost(2),
        name="assemble",
    )(place, *operands, *tokens)


def packed(block):
    rows, cols = block.shape
    parts = [block[:, c : c + 128] for c in range(0, cols - 64, 128)]
    last = block[:, cols - 64 :]
    return jnp.concatenate([*parts, jnp.concatenate([last[: rows // 2], last[rows // 2 :]], axis=1)], axis=0)


def unpacked(block, cols):
    rows = block.shape[0] * 128 // cols
    count = cols // 128
    last = block[count * rows :]
    parts = [block[c * rows : (c + 1) * rows] for c in range(count)]
    return jnp.concatenate([*parts, jnp.concatenate([last[:, :64], last[:, 64:]], axis=0)], axis=1)


def reversed_bits(count):
    order = [0]
    while len(order) < count:
        order = [2 * o for o in order] + [2 * o + 1 for o in order]
    return order


def split_blocks(keep_ref, send_ref, total, dp_place, shape=lambda block: block):
    count = keep_ref.shape[0]
    size = total.shape[0] // count // 2
    for ref, flip in ((keep_ref, 0), (send_ref, 1)):
        for j, distance in enumerate(reversed_bits(count)):
            target = dp_place ^ (2 * distance + flip)
            ref[j] = shape(total[pl.ds(pl.multiple_of(target * size, 8), size)])


def put_blocks(keep_ref, send_ref, total, dp_place):
    split_blocks(keep_ref, send_ref, total, dp_place, packed)


def call(kernel, grid, inputs, outputs, scratch=(), tokens=(), name=None, time=1, limit=56):
    whole = lambda a: (a, a.shape, lambda *_: (0,) * a.ndim)
    inputs = [i if isinstance(i, tuple) else whole(i) for i in inputs]
    specs = [pl.BlockSpec(block, index) if block else pl.BlockSpec(memory_space=pltpu.SMEM) for _, block, index in inputs]
    return pl.pallas_call(
        ignoring(kernel, len(inputs), len(tokens)),
        grid=grid,
        in_specs=[*specs, *([ANYWHERE] * len(tokens))],
        out_specs=[pl.BlockSpec(block, index) for _, _, block, index in outputs],
        out_shape=[jax.ShapeDtypeStruct(shape, kind) for shape, kind, _, _ in outputs],
        scratch_shapes=list(scratch),
        compiler_params=limits(limit),
        cost_estimate=cost(time),
        name=name,
    )(*(a for a, _, _ in inputs), *tokens)


def scalars(place):
    return place, None, None


def each(array):
    return array, (1, *array.shape[1:]), lambda i: (i, *(0,) * (array.ndim - 1))


def part(array, first):
    return array, (1, *array.shape[1:]), lambda i: (first + i, *(0,) * (array.ndim - 1))


def new(shape, kind=f32):
    return shape, kind, (1, *shape[1:]), lambda i: (i, *(0,) * (len(shape) - 1))


def kept(shape, kind=f32):
    return shape, kind, shape, lambda i: (0,) * len(shape)


def mix(place, own, far, w_out, tokens=()):
    count, rows, lat_count = own.shape

    def kernel(place_ref, own_ref, far_ref, w_ref, out_ref, att_ref):
        side = place_ref[0] // 2
        for ref, at in ((own_ref, side), (far_ref, 1 - side)):
            att_ref[pl.ds(pl.multiple_of(at * rows, 16), rows)] = ref[0].astype(bf16)
        out_ref[0] = dot_tn(att_ref[...], w_ref[...])

    return call(
        kernel, (count,), [scalars(place), each(own), each(far), w_out], [new((count, lat_count, w_out.shape[1]))],
        [pltpu.VMEM((2 * rows, lat_count), bf16)], tokens, "mix", 3,
    )[0]


def feed(place, first, latents, out_grad, mixed, crossed, gain, w_one, w_two, tokens=()):
    count, lat_count, width = mixed.shape
    rows = w_one.shape[0] // 2

    def kernel(
        place_ref, lat_ref, grad_ref, mixed_ref, crossed_ref, gain_ref, w_one_ref, w_two_ref,
        hidden_ref, normed_ref, activated_ref, share_ref, own_ref, up_own_ref, parts_ref,
    ):
        side = place_ref[0] // 2

        def own(tensor):
            parts_ref[0] = tensor[:, :rows]
            parts_ref[1] = tensor[:, rows:]
            return parts_ref[side]

        hidden = lat_ref[0].astype(f32) + (mixed_ref[0] + crossed_ref[0])
        hidden_ref[0] = hidden
        unit, _ = row_norm(hidden)
        normed = (unit * gain_ref[...]).astype(bf16)
        normed_ref[0] = normed
        up = dot_nt(normed, w_one_ref[...])
        below = 0.5 * (1.0 + lax.erf(up * 0.5**0.5))
        activated = (up * below).astype(bf16)
        activated_ref[0] = activated
        own_ref[0] = own(activated)
        slope = below + up * (jnp.exp(-0.5 * up * up) * 0.3989422804014327)
        up_grad = (dot_nt(grad_ref[0], w_two_ref[...]) * slope).astype(bf16)
        up_own_ref[0] = own(up_grad)
        share_ref[0] = dot(up_grad, w_one_ref[...])

    full, low = (count, lat_count, width), (count, lat_count, rows)
    return call(
        kernel, (count,),
        [scalars(place), part(latents, first), part(out_grad, first), each(mixed), each(crossed), gain, w_one, w_two],
        [new(full), new(full, bf16), new((count, lat_count, 2 * rows), bf16), new(full), new(low, bf16), new(low, bf16)],
        [pltpu.VMEM((2, lat_count, rows), bf16)], tokens, "feed", 6,
    )


def split_grad(blocks, width, rows):
    return kept((blocks // 2, width // blocks * rows // 128, 128))


def feed_weights(place, out_grad, fed, blocks, tokens=()):
    items, lat_count, width = out_grad.shape
    groups = len(fed)
    size = items // groups
    rows = fed[0][1].shape[2]

    def kernel(place_ref, grad_ref, *refs):
        item = pl.program_id(0)
        keep_one, send_one, keep_two, send_two, one_sum, two_sum = refs[3 * groups :]

        @pl.when(item == 0)
        def _():
            one_sum[...] = jnp.zeros_like(one_sum)
            two_sum[...] = jnp.zeros_like(two_sum)

        for g in range(groups):

            @pl.when(item // size == g)
            def _():
                normed_ref, activated_ref, up_grad_ref = refs[3 * g : 3 * g + 3]
                two_sum[...] += dot_tn(grad_ref[0], activated_ref[0])
                one_sum[...] += dot_tn(normed_ref[0], up_grad_ref[0])

        @pl.when(item == items - 1)
        def _():
            put_blocks(keep_two, send_two, two_sum, place_ref[1])
            put_blocks(keep_one, send_one, one_sum, place_ref[1])

    def of(array, g):
        return array, (1, *array.shape[1:]), lambda i: (jnp.clip(i - g * size, 0, size - 1), 0, 0)

    return call(
        kernel, (items,), [scalars(place), each(out_grad), *(of(a, g) for g in range(groups) for a in fed[g])],
        [split_grad(blocks, width, rows)] * 4, [pltpu.VMEM((width, rows), f32)] * 2, tokens, "feed_weights", 6,
    )


def unmix(place, first, out_grad, hidden, share, crossed, gain, w_out, att, before, blocks, heads, tokens=()):
    count, lat_count, width = hidden.shape
    rows = w_out.shape[0]
    val = rows // heads

    def kernel(place_ref, grad_ref, hidden_ref, share_ref, crossed_ref, gain_ref, w_ref, att_ref, *refs):
        item = pl.program_id(0)
        sums_in, refs = refs[: len(before)], refs[len(before) :]
        hidden_grad_ref, att_grad_ref, att_grad_t_ref, delta_ref, gain_grad_ref, sum_ref, *split = refs

        @pl.when(item == 0)
        def _():
            for i, ref in enumerate((gain_grad_ref, sum_ref)):
                ref[...] = sums_in[i][...] if before else jnp.zeros_like(ref)

        unit, inv = row_norm(hidden_ref[0])
        norm_grad = share_ref[0] + crossed_ref[0]
        gain_grad_ref[...] += jnp.sum(norm_grad * unit, axis=0, keepdims=True)
        hidden_grad = grad_ref[0].astype(f32) + row_norm_back(norm_grad, unit, inv, gain_ref[...])
        hidden_grad_ref[0] = hidden_grad
        mixed_grad = hidden_grad.astype(bf16)
        att = att_ref[0].T
        sum_ref[...] += dot_tn(mixed_grad, att.astype(bf16))
        att_grad = dot_nt(mixed_grad, w_ref[...])
        att_grad_ref[0] = att_grad.astype(bf16)
        att_grad_t_ref[0] = att_grad.T.astype(bf16)
        product = att_grad.astype(bf16).astype(f32) * att
        lane = lax.broadcasted_iota(jnp.int32, delta_ref.shape[1:], 1)
        delta = jnp.zeros(delta_ref.shape[1:], f32)
        for h in range(heads):
            delta = jnp.where(lane == h, jnp.sum(product[:, h * val : (h + 1) * val], axis=1, keepdims=True), delta)
        delta_ref[0] = delta
        if split:

            @pl.when(item == count - 1)
            def _():
                put_blocks(*split, sum_ref, place_ref[1])

    full = (count, lat_count, width)
    return call(
        kernel, (count,),
        [
            scalars(place), part(out_grad, first), each(hidden), each(share), each(crossed), gain, w_out, each(att), *before,
        ],
        [
            new(full), new((count, lat_count, rows), bf16), new((count, rows, lat_count), bf16), new((count, lat_count, 128)),
            kept((1, width)), kept((width, rows)), *([split_grad(blocks, width, rows)] * 2 if first else []),
        ],
        [], tokens, "unmix", 6,
    )


def branch(activated, w_two, tokens=()):
    count, lat_count, _ = activated.shape

    def kernel(activated_ref, w_ref, out_ref):
        out_ref[0] = dot(activated_ref[0], w_ref[...])

    return call(
        kernel, (count,), [each(activated), w_two], [new((count, lat_count, w_two.shape[1]))], [], tokens, "branch", 2
    )[0]


def latent(place, query_grad, latents, hidden_grad, gain, w_query, hidden, shares, crossed, blocks):
    items, lat_count, width = latents.shape
    rows = w_query[0].shape[0]
    groups = len(hidden)
    size = items // groups

    def kernel(
        place_ref, own_ref, core_ref, far_ref, far_core_ref, lat_ref, gain_ref, w_own, w_core, w_far, w_far_core, *refs,
    ):
        group_refs = [refs[4 * g : 4 * g + 4] for g in range(groups)]
        grad_ref, out_ref, gain_grad_ref, keep_ref, send_ref, w_ref, parts_ref, sum_ref, turned_ref = refs[4 * groups :]
        item = pl.program_id(0)
        place = place_ref[0]

        def put(target, refs, value):
            for step, ref in enumerate(refs):
                target[pl.ds(pl.multiple_of((place ^ step) * rows, 16), rows)] = value(ref).astype(bf16)

        @pl.when(item == 0)
        def _():
            put(w_ref, (w_own, w_core, w_far, w_far_core), lambda ref: ref[...])
            gain_grad_ref[...] = jnp.zeros_like(gain_grad_ref)
            sum_ref[...] = jnp.zeros_like(sum_ref)

        put(parts_ref, (own_ref, core_ref, far_ref, far_core_ref), lambda ref: ref[0])
        unit, inv = row_norm(lat_ref[0].astype(f32))
        gain = gain_ref[...]
        sum_ref[...] += dot(own_ref[0].astype(bf16), (unit * gain).astype(bf16))
        norm_grad = dot_tn(parts_ref[...], w_ref[...])
        gain_grad_ref[...] += jnp.sum(norm_grad * unit, axis=0, keepdims=True)
        for g in range(groups):

            @pl.when(item // size == g)
            def _():
                hidden_grad_ref, hidden_ref, share_ref, crossed_ref = group_refs[g]
                grad_ref[0] = hidden_grad_ref[0] + row_norm_back(norm_grad, unit, inv, gain)
                out_ref[0] = (hidden_ref[0] + (share_ref[0] + crossed_ref[0])).astype(bf16)

        @pl.when(item == items - 1)
        def _():
            turned_ref[...] = sum_ref[...].T
            put_blocks(keep_ref, send_ref, turned_ref, place_ref[1])

    def of(array, g):
        return array, (1, *array.shape[1:]), lambda i: (jnp.clip(i - g * size, 0, size - 1), 0, 0)

    return call(
        kernel, (items,),
        [
            scalars(place), *(each(q) for q in query_grad), each(latents), gain, *w_query,
            *(of(a, g) for g in range(groups) for a in (hidden_grad[g], hidden[g], shares[g], crossed[g])),
        ],
        [new(latents.shape), new(latents.shape, bf16), kept((1, width)), *([split_grad(blocks, width, rows)] * 2)],
        [
            pltpu.VMEM((4 * rows, width), bf16), pltpu.VMEM((4 * rows, lat_count), bf16), pltpu.VMEM((rows, width), f32),
            pltpu.VMEM((width, rows), f32),
        ], (), "latent", 16,
    )


def swap(tensor, axis, bit):
    return lax.ppermute(tensor, axis, [(i, i ^ bit) for i in range(lax.axis_size(axis))])


def stage(always, work):
    shapes = jax.eval_shape(work)
    return lax.cond(always, work, lambda: jax.tree.map(lambda s: jnp.zeros(s.shape, s.dtype), shapes))


def body(
    byte_ids, lengths, latents, byte_table, pos_table, gain_in, gain_lat, gain_mlp,
    w_query, w_key, w_value, w_out, w_one, w_two, out_grad,
):
    items, slots = byte_ids.shape
    vocab, width = byte_table.shape
    lat_count, lat_width = latents.shape[1:]
    mp, dp = lax.axis_size("mp"), lax.axis_size("dp")
    mp_place, dp_place = lax.axis_index("mp"), lax.axis_index("dp")
    place = jnp.stack([mp_place, dp_place]).astype(jnp.int32)
    heads = HEADS // mp
    qk_cols = w_query.shape[1]
    val_cols = w_value.shape[1]
    corner, side = dp_place % 4, dp_place % 2

    shards = [w_out, w_one.T, w_two]
    quarter = val_cols // 4
    always = lengths[0] > 0
    over_y = lambda w: swap(lax.dynamic_slice_in_dim(w, corner * quarter, quarter, 0).astype(f32), "mp", 2)
    over_x, over_z, over_both = (lambda a, bits=bits: swap(a, "dp", bits) for bits in (1, 2, 3))
    core = lambda a: swap(a, "mp", 1)
    half = items // 2

    def first_stage():
        weights = (gain_in[None], w_key.T, w_value.T, *shards[1:])
        return over_y(shards[0]), tables_of(place, byte_table, pos_table, *weights)

    out, (*tables, w_back, w_rows, one, two) = stage(always, first_stage)

    def front_of(first):
        return front(first, half, lengths, byte_ids, *tables, latents, gain_lat[None], w_query.T, heads)

    def second_stage():
        return front_of(0), [over_x(out), over_z(out)], over_both(out), swap(one, "mp", 2), swap(two, "mp", 2)

    (*made_a, att_a), crossed_out, last_out, one, two = stage(always, second_stage)

    def third_stage():
        return front_of(half), [over_x(one), over_z(one), over_both(one)], over_x(two), swap(att_a, "mp", 2)

    (*made_b, att_b), crossed_one, cross_two, far_a = stage(always, third_stage)

    def fourth_stage():
        w_out_whole = assemble(place, shards[0], [out, *crossed_out, last_out])
        w_one_whole = assemble(place, shards[1], [one, *crossed_one], [w_out_whole])
        mixed_a = mix(place, att_a, far_a, w_out_whole, [w_one_whole])
        return w_out_whole, w_one_whole, mixed_a, [over_z(two), over_both(two)], swap(att_b, "mp", 2)

    w_out_whole, w_one_whole, mixed_a, crossed_two, far_b = stage(always, fourth_stage)
    w_two_whole = assemble(place, shards[2], [two, cross_two, *crossed_two])
    mixed_b = mix(place, att_b, far_b, w_out_whole, [w_two_whole])
    gain = gain_mlp[None]
    weights = (gain, w_one_whole, w_two_whole)
    hidden_a, normed_a, activated_a, share_a, act_a, up_a = feed(
        place, 0, latents, out_grad, mixed_a, core(mixed_a), *weights, [mixed_b]
    )
    hidden_b, normed_b, activated_b, share_b, act_b, up_b = feed(
        place, half, latents, out_grad, mixed_b, core(mixed_b), *weights, [share_a]
    )
    keep_one, send_one, keep_two, send_two = feed_weights(
        place, out_grad, [(normed_a, act_a, up_a), (normed_b, act_b, up_b)], dp
    )
    w_query_own = w_query.T.astype(f32)
    crossed_a, crossed_b = core(share_a), core(share_b)

    def unmix_stage():
        grads_a = unmix(place, 0, out_grad, hidden_a, share_a, crossed_a, gain, w_out, att_a, [], dp, heads)
        grads_b = unmix(place, half, out_grad, hidden_b, share_b, crossed_b, gain, w_out, att_b, grads_a[4:], dp, heads)
        w_query_parts = core(w_query_own), swap(w_query_own, "mp", 2)
        return grads_a[:4], grads_b[:5], grads_b[6:], swap(send_two, "dp", 1), w_query_parts

    (hidden_grad_a, *grads_a), (hidden_grad_b, *grads_b, gain_mlp_grad), (keep_out, send_out), cross_two, w_query_parts = stage(
        always, unmix_stage
    )
    made = [(*made_a, *grads_a), (*made_b, *grads_b)]
    byte_cols = vocab + -vocab % 128
    bits = [1 << i for i in range(1, dp.bit_length() - 1)]

    def back_of(first, count, sums):
        return back(place, first, count, lengths, byte_ids, made, w_back, w_rows, tables[3], sums, heads, vocab)

    def spread(blocks):
        return [blocks[0]] + [swap(blocks[j], "dp", 2 * d) for j, d in enumerate(reversed_bits(dp // 2)) if d]

    def halve(blocks, bits):
        for bit in bits:
            count = blocks.shape[0] // 2
            blocks = blocks[:count] + swap(blocks[count:], "dp", bit)
        return blocks

    def pick(array, index, axis):
        return lax.dynamic_index_in_dim(array, index, axis, False)

    def both_sides(array, axis, bit):
        mine = dp_place // bit % 2
        return pick(array, mine, axis), pick(array, 1 - mine, axis)

    two_blocks = keep_two + cross_two

    def back_stage_a():
        return back_of(0, 2, []), swap(send_one, "dp", 1), spread(two_blocks), core(w_query_parts[1])

    (pos_a, *sums), cross_one, two_parts, w_query_last = stage(always, back_stage_a)
    w_query_all = [w_query_own, *w_query_parts, w_query_last]
    one_blocks = keep_one + cross_one

    def back_stage_b():
        return back_of(2, 1, sums), swap(send_out, "dp", 1), spread(one_blocks), core(pos_a)

    (pos_b, *sums), cross_out, one_parts, near_a = stage(always, back_stage_b)
    out_blocks = keep_out + cross_out
    send_a = pos_a[1] + near_a[3]

    def back_stage_c():
        return back_of(3, 1, sums), swap(send_a, "mp", 2), spread(out_blocks), core(pos_b)

    (pos_c, query_own, keep_kv, send_kv), far_pos_a, out_parts, near_b = stage(always, back_stage_c)
    send_b = pos_b[1] + near_b[3]
    total = lambda parts: unpacked(sum(parts), val_cols)

    def tail_stage_a():
        branches = [branch(a, w_two_whole) for a in (activated_a, activated_b)]
        transfers = core(pos_c), swap(query_own, "mp", 2), core(query_own), swap(send_b, "mp", 2), swap(send_kv, "dp", 1)
        return branches, transfers, (total(two_parts).T, total(one_parts), total(out_parts).T)

    branches, (near_c, query_far, query_near, far_pos_b, cross_kv), (two_sum, one_sum, out_sum) = stage(always, tail_stage_a)
    send_c = pos_c[1] + near_c[3]
    mine = jnp.concatenate([pos_a[0] + near_a[2] + far_pos_a, pos_b[0] + near_b[2] + far_pos_b], axis=1)
    keep_ab, send_ab = both_sides(mine.reshape(mine.shape[0], -1, 2, slots // dp), 2, 1)
    kv_blocks = keep_kv + cross_kv
    crossed = [core(a) for a in branches]
    query_all = [query_own, query_near, query_far, core(query_far)]

    def tail_stage_b():
        return latent(
            place, query_all, latents, (hidden_grad_a, hidden_grad_b), gain_lat[None], w_query_all, (hidden_a, hidden_b),
            branches, crossed, dp,
        ), swap(send_c, "mp", 2), swap(send_ab, "dp", 1)

    (latent_grad, latents_out, gain_lat_grad, keep_query, send_query), far_pos_c, cross_ab = stage(always, tail_stage_b)
    mine = pos_c[0] + near_c[2] + far_pos_c
    keep_c, send_c = both_sides(mine[:, :TILE].reshape(mine.shape[0], -1, 2, slots // dp), 2, 1)
    gains = jnp.concatenate([gain_lat_grad, gain_mlp_grad])
    gains = lax.dynamic_slice_in_dim(gains, mp_place * val_cols, val_cols, 1).reshape(-1)
    share = width // mp
    gains = jnp.pad(gains, (0, -gains.size % share)).reshape(-1, share).T
    byte_mine = lax.dynamic_update_slice(mine[:, TILE:], gains, (0, vocab + 1))
    keep_byte, send_byte = both_sides(byte_mine.reshape(2, share // 2, byte_cols), 0, 1)

    cross_c, cross_byte, cross_query = swap(send_c, "dp", 1), swap(send_byte, "dp", 1), swap(send_query, "dp", 1)
    kv_blocks = halve(kv_blocks, bits[:1])
    ring = dp_place // 2
    order = reversed_bits(dp // 2)
    pos_blocks = jnp.concatenate([keep_ab + cross_ab, keep_c + cross_c], axis=1).swapaxes(0, 1)
    byte_blocks = (keep_byte + cross_byte).reshape(dp // 2, -1, byte_cols)
    by_distance = lambda blocks: [pick(blocks, ring ^ d, 0) for d in order]
    pos_blocks = halve(jnp.stack(by_distance(pos_blocks)), bits[:1])
    byte_own = sum(spread(by_distance(byte_blocks)))
    kv_sum = halve(kv_blocks, bits[1:])[0]
    pos_sum = halve(pos_blocks, bits[1:])[0]
    query_blocks = halve(keep_query + cross_query, bits[:1])
    byte_all = jnp.stack([byte_own] + [swap(byte_own, "dp", 2 * d) for d in range(1, dp // 2)])
    byte_half = jnp.concatenate([pick(byte_all, ring ^ d, 0) for d in range(dp // 2)])
    query_sum = halve(query_blocks, bits[1:])[0]
    other = swap(byte_half, "dp", 1)
    byte_whole = jnp.where(side == 0, jnp.concatenate([byte_half, other]), jnp.concatenate([other, byte_half]))
    gains = byte_whole[:, vocab + 1 : vocab + 1 + gains.shape[1]].T.reshape(-1)
    return (
        latents_out, latent_grad, byte_whole[:, :vocab].T, pos_sum.T, byte_whole[:, vocab],
        gains[:val_cols], gains[val_cols : 2 * val_cols], unpacked(query_sum, qk_cols),
        kv_sum[:, :qk_cols], kv_sum[:, qk_cols:], out_sum, one_sum, two_sum,
    )


def solution(mesh):
    return jax.shard_map(
        body,
        mesh=mesh,
        in_specs=(
            P("dp", None),
            P("dp"),
            P("dp", None, None),
            P(),
            P(),
            P(),
            P(),
            P(),
            P(None, "mp"),
            P(None, "mp"),
            P(None, "mp"),
            P("mp", None),
            P(None, "mp"),
            P("mp", None),
            P("dp", None, None),
        ),
        out_specs=(
            P("dp", None, None),
            P("dp", None, None),
            P(None, "mp"),
            P("dp", "mp"),
            P("mp"),
            P("mp"),
            P("mp"),
            P("dp", "mp"),
            P("dp", "mp"),
            P("dp", "mp"),
            P("mp", "dp"),
            P("dp", "mp"),
            P("mp", "dp"),
        ),
        check_vma=False,
    )
```

```python
import functools

import jax
import jax.numpy as jnp
from jax import lax
from jax.experimental import pallas as pl
from jax.experimental.pallas import tpu as pltpu
from jax.sharding import PartitionSpec as P

HEADS = 8
EPSILON = 1e-05
MASKED = -1e30
LOG2E = 1.4426950408889634
TILE = 512
COST = 11500000000
f32, bf16 = jnp.float32, jnp.bfloat16
ANYWHERE = pl.BlockSpec(memory_space=pl.ANY)


def dot(left, right):
    return jnp.dot(left, right, preferred_element_type=f32)


def dot_nt(left, right):
    return lax.dot_general(left, right, (((1,), (1,)), ((), ())), preferred_element_type=f32)


def dot_tn(left, right):
    return lax.dot_general(left, right, (((0,), (0,)), ((), ())), preferred_element_type=f32)


def cost(microseconds):
    return pl.CostEstimate(flops=microseconds * COST, bytes_accessed=0, transcendentals=0)


def limits(mebibytes):
    return pltpu.CompilerParams(vmem_limit_bytes=mebibytes * 2**20)


def ignoring(kernel, start, count):
    def inner(*refs):
        return kernel(*refs[:start], *refs[start + count :])

    return inner


def row_norm(rows):
    centered = rows - jnp.mean(rows, axis=-1, keepdims=True)
    inv_std = lax.rsqrt(jnp.mean(centered * centered, axis=-1, keepdims=True) + EPSILON)
    return centered * inv_std, inv_std


def row_norm_back(upstream, unit, inv, gain):
    scaled = upstream * gain
    row_mean = jnp.mean(scaled, axis=-1, keepdims=True)
    row_cross = jnp.mean(scaled * unit, axis=-1, keepdims=True)
    return inv * (scaled - row_mean - unit * row_cross)


def front_kernel(
    lengths, ids_ref, table_ref, pos_ref, pos_mean_ref, gain_ref, w_kv_ref, lat_ref, gain_lat_ref, w_query_ref,
    unit_ref, inv_ref, kv_ref, lse_ref, query_ref, query_t_ref, att_ref,
    x_ref, normed_ref, scores_ref, total_ref, peak_ref,
    *, first, width, heads,
):
    step = pl.program_id(1)
    item = first + pl.program_id(0)
    length = lengths[item]
    lat_count = lat_ref.shape[1]
    qk_cols = w_query_ref.shape[0]
    qk = qk_cols // heads
    val = (w_kv_ref.shape[0] - qk_cols) // heads
    scale = qk**-0.5 * LOG2E
    chunk = 64

    @pl.when(step == 0)
    def _():
        unit_lat, _ = row_norm(lat_ref[0].astype(f32))
        queries = dot_nt((unit_lat * gain_lat_ref[...]).astype(bf16), w_query_ref[...])
        query_ref[0] = queries.astype(bf16)
        query_t_ref[0] = queries.T.astype(bf16)
        peak_ref[...] = jnp.full_like(peak_ref, MASKED)

    @pl.when(step * TILE < length)
    def _():
        cols = pl.ds(pl.multiple_of(step * TILE, TILE), TILE)
        hits = (lax.broadcasted_iota(jnp.int32, (table_ref.shape[1], TILE), 0) == ids_ref[pl.ds(item, 1), cols]).astype(bf16)
        x_ref[...] = dot(table_ref[...], hits)
        mean = x_ref[width : width + 1] + x_ref[width + 1 : width + 2] + x_ref[width + 2 : width + 3]
        mean = mean + pos_mean_ref[:, cols]
        square = jnp.zeros((8, TILE), f32)
        for r in range(0, width, chunk):
            rows = x_ref[r : r + chunk] + pos_ref[r : r + chunk].astype(f32) - mean
            x_ref[r : r + chunk] = rows
            rows = rows * rows
            square += sum(rows[i : i + 8] for i in range(0, chunk, 8))
        inv = lax.rsqrt(jnp.sum(square, axis=0, keepdims=True) * (1.0 / width) + EPSILON)
        inv_ref[0, :, cols] = inv
        for r in range(0, width, chunk):
            unit = x_ref[r : r + chunk] * inv
            unit_ref[0, r : r + chunk] = unit.astype(bf16)
            gain = jnp.concatenate([gain_ref[r : r + chunk]] * (TILE // 128), axis=1)
            normed_ref[r : r + chunk] = (unit * gain).astype(bf16)
        kv_ref[0, :, cols] = dot(w_kv_ref[...], normed_ref[...]).astype(bf16)
        live = step * TILE + lax.broadcasted_iota(jnp.int32, (1, TILE), 1) < length
        for h in range(heads):
            scores = dot(query_ref[0, :, h * qk : (h + 1) * qk], kv_ref[0, h * qk : (h + 1) * qk, cols])
            scores = jnp.where(live, scores, MASKED)
            scores_ref[h, :, cols] = scores
            peak = peak_ref[h]
            for c in range(0, TILE, 128):
                peak = jnp.maximum(peak, scores[:, c : c + 128])
            peak_ref[h] = peak

    @pl.when(step == pl.num_programs(1) - 1)
    def _():
        peaks = [jnp.max(peak_ref[h], axis=1, keepdims=True) for h in range(heads)]
        total_ref[...] = jnp.zeros_like(total_ref)

        def attend(t, sums):
            cols = pl.ds(pl.multiple_of(t * TILE, TILE), TILE)
            new = []
            for h in range(heads):
                raised = jnp.exp2((scores_ref[h, :, cols] - peaks[h]) * scale)
                new.append(sums[h] + sum(raised[:, c : c + 128] for c in range(0, TILE, 128)))
                start = qk_cols + h * val
                total_ref[h] += dot_nt(raised.astype(bf16), kv_ref[0, start : start + val, cols])
            return tuple(new)

        sums = lax.fori_loop(0, pl.cdiv(length, TILE), attend, (jnp.zeros((lat_count, 128), f32),) * heads)
        lane = lax.broadcasted_iota(jnp.int32, (lat_count, 128), 1)
        packed = jnp.zeros((lat_count, 128), f32)
        out = []
        for h in range(heads):
            total = jnp.sum(sums[h], axis=1, keepdims=True)
            out.append(total_ref[h] / total)
            packed = jnp.where(lane == h, peaks[h] * scale + jnp.log2(total), packed)
        att_ref[0] = jnp.concatenate(out, axis=1).T
        lse_ref[0] = packed


def front(first, count, lengths, ids, table, pos, pos_mean, gain, w_kv, latents, gain_lat, w_query, heads):
    slots = ids.shape[1]
    width = pos.shape[0]
    lat_count, lat_width = latents.shape[1:]
    qk_cols = w_query.shape[0]
    kv_cols = w_kv.shape[0]
    val_cols = kv_cols - qk_cols
    whole = lambda a: pl.BlockSpec(a.shape, lambda i, t, *_: (0,) * a.ndim)
    each = lambda *s: pl.BlockSpec((1, *s), lambda i, t, *_: (first + i, 0, 0))
    made = lambda *s: pl.BlockSpec((1, *s), lambda i, t, *_: (i, 0, 0))
    shape = lambda s, d: jax.ShapeDtypeStruct((count, *s), d)

    def live(i, t, lengths):
        return jnp.minimum(t, pl.cdiv(lengths[first + i], TILE) - 1)

    return pl.pallas_call(
        functools.partial(front_kernel, first=first, width=width, heads=heads),
        grid_spec=pltpu.PrefetchScalarGridSpec(
            num_scalar_prefetch=1,
            grid=(count, slots // TILE),
            in_specs=[
                whole(ids), whole(table), pl.BlockSpec((width, TILE), lambda i, t, l: (0, live(i, t, l))), whole(pos_mean),
                whole(gain), whole(w_kv), each(lat_count, lat_width), whole(gain_lat), whole(w_query),
            ],
            out_specs=[
                pl.BlockSpec((1, width, TILE), lambda i, t, l: (i, 0, live(i, t, l))), made(1, slots), made(kv_cols, slots),
                made(lat_count, 128), made(lat_count, qk_cols), made(qk_cols, lat_count), made(val_cols, lat_count),
            ],
            scratch_shapes=[
                pltpu.VMEM((table.shape[0], TILE), f32),
                pltpu.VMEM((width, TILE), bf16),
                pltpu.VMEM((heads, lat_count, slots), f32),
                pltpu.VMEM((heads, lat_count, val_cols // heads), f32),
                pltpu.VMEM((heads, lat_count, 128), f32),
            ],
        ),
        out_shape=[
            shape((width, slots), bf16), shape((1, slots), f32), shape((kv_cols, slots), bf16), shape((lat_count, 128), f32),
            shape((lat_count, qk_cols), bf16), shape((qk_cols, lat_count), bf16),
            shape((val_cols, lat_count), f32),
        ],
        compiler_params=limits(56),
        cost_estimate=cost(18),
        name="front",
    )(lengths, ids, table, pos, pos_mean, gain, w_kv, latents, gain_lat, w_query)


def tables_kernel(
    place_ref, byte_ref, pos_ref, gain_ref, w_key_ref, w_value_ref, w_one_ref, w_two_ref, table_ref, pos_t_ref, mean_ref, gains_ref, w_kv_ref, w_back_ref,
    w_rows_ref, one_ref, two_ref, pad_ref,
):
    vocab, width = byte_ref.shape

    @pl.when(pl.program_id(0) == 0)
    def _():
        rows = one_ref.shape[0]
        quarter = pl.ds(pl.multiple_of(place_ref[1] % 4 * rows, 16), rows)
        one_ref[...] = w_one_ref[quarter].astype(f32)
        two_ref[...] = w_two_ref[quarter].astype(f32)
        gain = gain_ref[...]
        gains_ref[...] = jnp.broadcast_to(gain, (128, width)).T
        first = w_key_ref.shape[0]
        w_kv_ref[:first] = w_key_ref[...]
        w_kv_ref[first:] = w_value_ref[...]
        w_rows_ref[...] = w_kv_ref[...].astype(f32).T.astype(bf16)
        scaled = w_kv_ref[...].astype(f32) * gain
        w_back_ref[...] = (scaled - jnp.mean(scaled, axis=1, keepdims=True)).T.astype(bf16)
        pad_ref[...] = jnp.zeros_like(pad_ref)
        pad_ref[:vocab] = byte_ref[...].astype(f32)
        table = pad_ref[...].T
        table_ref[:width] = table[:, : table_ref.shape[1]].astype(bf16)
        mean = jnp.mean(table, axis=0, keepdims=True)[:, : table_ref.shape[1]]
        high = mean.astype(bf16)
        rest = mean - high.astype(f32)
        middle = rest.astype(bf16)
        low = (rest - middle.astype(f32)).astype(bf16)
        more = table_ref.shape[0] - width
        row = lax.broadcasted_iota(jnp.int32, (more, table_ref.shape[1]), 0)
        rows = jnp.zeros(row.shape, f32)
        for place, value in enumerate((high, middle, low)):
            rows = jnp.where(row == place, value.astype(f32), rows)
        table_ref[width:] = rows.astype(bf16)

    pos = pos_ref[...].astype(f32).T
    pos_t_ref[...] = pos.astype(bf16)
    mean_ref[...] = jnp.mean(pos, axis=0, keepdims=True)


def tables_of(place, byte_table, pos_table, gain, w_key_t, w_value_t, w_one_t, w_two):
    vocab, width = byte_table.shape
    slots = pos_table.shape[0]
    kv_cols = w_key_t.shape[0] + w_value_t.shape[0]
    vocab_rows = vocab + -vocab % 16
    whole = lambda a: pl.BlockSpec(a.shape, lambda t: (0,) * a.ndim)
    shapes = [
        ((width + 16, vocab_rows), bf16), ((width, slots), bf16), ((1, slots), f32), ((width, 128), f32), ((kv_cols, width), bf16),
        ((width, kv_cols), bf16), ((width, kv_cols), bf16), *([((w_two.shape[0] // 4, w_two.shape[1]), f32)] * 2),
    ]
    shapes = [jax.ShapeDtypeStruct(*s) for s in shapes]
    specs = [whole(a) for a in shapes]
    specs[1] = pl.BlockSpec((width, TILE), lambda t: (0, t))
    specs[2] = pl.BlockSpec((1, TILE), lambda t: (0, t))
    return pl.pallas_call(
        tables_kernel,
        grid=(slots // TILE,),
        in_specs=[
            pl.BlockSpec(memory_space=pltpu.SMEM), whole(byte_table), pl.BlockSpec((TILE, width), lambda t: (t, 0)), whole(gain),
            whole(w_key_t), whole(w_value_t), whole(w_one_t), whole(w_two),
        ],
        out_specs=specs,
        out_shape=shapes,
        scratch_shapes=[pltpu.VMEM((vocab + -vocab % 128, width), f32)],
        compiler_params=limits(40),
        cost_estimate=cost(8),
        name="tables",
    )(place, byte_table, pos_table, gain, w_key_t, w_value_t, w_one_t, w_two)


def back_kernel(
    lengths, place_ref, ids_ref, w_ref, w_rows_ref, gain_ref, *refs,
    first, heads, groups, last, vocab,
):
    step, item = pl.program_id(0), pl.program_id(1)
    length = lengths[item]
    tile = step + first
    sums_in, refs = (refs[:3], refs[3:]) if first else ((), refs)
    made = [refs[9 * g : 9 * g + 9] for g in range(groups)]
    refs = refs[9 * groups :]
    pos_ref, query_out_ref, *refs = refs
    if last:
        keep_ref, send_ref, *refs, byte_ref, unit_kv_ref = refs
    else:
        byte_ref, unit_kv_ref, *refs = refs
    (
        unit_ref, inv_ref, kv_ref, lse_ref, query_ref, query_t_ref, att_grad_ref, att_grad_t_ref, delta_ref, kv_grad_ref, low_ref,
    ) = refs
    width, kv_cols = w_ref.shape
    qk_cols = query_ref.shape[1]
    qk, val = qk_cols // heads, (kv_cols - qk_cols) // heads
    factor = qk**-0.5
    scale = factor * LOG2E
    chunk = 64
    share = pos_ref.shape[1]

    def order(block):
        distance = place_ref[0] ^ block
        return distance % 2 * 2 + distance // 2

    @pl.when((step == 0) & (item == 0))
    def _():
        for i, ref in enumerate((query_out_ref, byte_ref, unit_kv_ref)):
            ref[...] = sums_in[i][...] if first else jnp.zeros_like(ref)

    @pl.when(item == 0)
    def _():
        pos_ref[:, :, :TILE] = jnp.zeros((4, share, TILE), f32)

    for g in range(groups):

        @pl.when((tile * TILE < length) & (item // (pl.num_programs(1) // groups) == g))
        def _():
            copies = (unit_ref, inv_ref, kv_ref, lse_ref, query_ref, query_t_ref, att_grad_ref, att_grad_t_ref, delta_ref)
            for target, ref in zip(copies, made[g]):
                target[...] = ref[0]

    @pl.when(tile * TILE < length)
    def _():
        live = tile * TILE + lax.broadcasted_iota(jnp.int32, (1, TILE), 1) < length
        cross = jnp.zeros((8, TILE), f32)
        for h in range(heads):
            keys = slice(h * qk, (h + 1) * qk)
            values = slice(qk_cols + h * val, qk_cols + (h + 1) * val)
            cols = slice(h * val, (h + 1) * val)
            scores = dot(query_ref[:, keys], kv_ref[keys])
            chances = jnp.exp2(scores * scale - lse_ref[:, h : h + 1])
            chances = jnp.where(live, chances, 0.0)
            weights_grad = dot(att_grad_ref[:, cols], kv_ref[values])
            scores_grad = (chances * (weights_grad - delta_ref[:, h : h + 1])).astype(bf16)
            query_out_ref[item, keys] += dot_nt(kv_ref[keys], scores_grad)
            kv_grad_ref[keys] = (dot(query_t_ref[keys], scores_grad) * factor).astype(bf16)
            kv_grad_ref[values] = dot(att_grad_t_ref[cols], chances.astype(bf16)).astype(bf16)
        for r in range(0, kv_cols, chunk):
            rows = kv_grad_ref[r : r + chunk].astype(f32) * kv_ref[r : r + chunk].astype(f32)
            cross += sum(rows[i : i + 8] for i in range(0, chunk, 8))
        inv = inv_ref[...]
        cross = jnp.sum(cross, axis=0, keepdims=True) * (1.0 / width) * inv
        back = dot(w_ref[...], kv_grad_ref[...])
        for r in range(0, width, chunk):
            rows = slice(r, r + chunk)
            grads = back[rows] * inv - unit_ref[rows].astype(f32) * cross
            pos_ref[order(r // share), r % share : r % share + chunk, :TILE] += grads
            low_ref[rows] = grads.astype(bf16)
        hits = (lax.broadcasted_iota(jnp.int32, (byte_ref.shape[1], TILE), 0) == ids_ref[pl.ds(item, 1)]).astype(bf16)
        byte_ref[...] += dot_nt(low_ref[...], hits)
        unit_kv_ref[...] += dot_nt(unit_ref[...], kv_grad_ref[...])

    if last:

        @pl.when((step == pl.num_programs(0) - 1) & (item == pl.num_programs(1) - 1))
        def _():
            query_out_ref[...] = (query_out_ref[...] * factor).astype(bf16).astype(f32)
            lane = lax.broadcasted_iota(jnp.int32, byte_ref.shape, 1)
            gain_grad = jnp.sum(unit_kv_ref[...] * w_rows_ref[...].astype(f32), axis=1, keepdims=True)
            byte_ref[...] = jnp.where(lane == vocab, gain_grad, byte_ref[...])
            for block in range(4):
                pos_ref[order(block), :, TILE:] = byte_ref[block * share : (block + 1) * share]
            unit_kv_ref[...] *= gain_ref[:, :1]
            split_blocks(keep_ref, send_ref, unit_kv_ref, place_ref[1])


def back(place, first, count, lengths, ids, made, w_back, w_rows, gains, sums, heads, vocab):
    items, slots = ids.shape
    last = (first + count) * TILE == slots
    groups = len(made)
    size = items // groups
    width, kv_cols = w_back.shape
    lat_count, qk_cols = made[0][4].shape[1:]
    val_cols = kv_cols - qk_cols
    whole = lambda a: pl.BlockSpec(a.shape, lambda t, i, *_: (0,) * a.ndim)
    clip = lambda i, g: jnp.clip(i - g * size, 0, size - 1)
    tiles = lambda g, *s: pl.BlockSpec((1, *s, TILE), lambda t, i, *_: (clip(i, g), 0, t + first))
    each = lambda g, *s: pl.BlockSpec((1, *s), lambda t, i, *_: (clip(i, g), 0, 0))
    shape = lambda s: jax.ShapeDtypeStruct(s, f32)
    kernel = functools.partial(back_kernel, first=first, heads=heads, groups=groups, last=last, vocab=vocab)
    operands = (ids, w_back, w_rows, gains, *sums, *(a for nine in made for a in nine))
    byte_cols = vocab + -vocab % 128
    query_sum, byte_sum, unit_kv = (shape(a) for a in ((items, qk_cols, lat_count), (width, byte_cols), (width, kv_cols)))
    blocks = lax.axis_size("dp")
    if last:
        assert count == 1
        split = shape((blocks // 2, width // blocks, kv_cols))
        out_shape = [shape((4, width // 4, TILE + byte_sum.shape[1])), query_sum, split, split]
        out_specs = [whole(a) for a in out_shape]
    else:
        out_shape = [shape((4, width // 4, count * TILE)), query_sum, byte_sum, unit_kv]
        out_specs = [pl.BlockSpec((4, width // 4, TILE), lambda t, i, *_: (0, 0, t)), *(whole(a) for a in out_shape[1:])]
    return pl.pallas_call(
        kernel,
        grid_spec=pltpu.PrefetchScalarGridSpec(
            num_scalar_prefetch=2,
            grid=(count, items),
            in_specs=[
                pl.BlockSpec((items, TILE), lambda t, i, *_: (0, t + first)),
                *(whole(a) for a in (w_back, w_rows, gains, *sums)),
                *(
                    spec
                    for g in range(groups)
                    for spec in (
                        tiles(g, width), tiles(g, 1), tiles(g, kv_cols), each(g, lat_count, 128), each(g, lat_count, qk_cols),
                        each(g, qk_cols, lat_count), each(g, lat_count, val_cols), each(g, val_cols, lat_count), each(g, lat_count, 128),
                    )
                ),
            ],
            out_specs=out_specs,
            scratch_shapes=[
                pltpu.VMEM((width, TILE), bf16), pltpu.VMEM((1, TILE), f32), pltpu.VMEM((kv_cols, TILE), bf16),
                pltpu.VMEM((lat_count, 128), f32), pltpu.VMEM((lat_count, qk_cols), bf16),
                pltpu.VMEM((qk_cols, lat_count), bf16), pltpu.VMEM((lat_count, val_cols), bf16),
                pltpu.VMEM((val_cols, lat_count), bf16), pltpu.VMEM((lat_count, 128), f32),
                pltpu.VMEM((kv_cols, TILE), bf16), pltpu.VMEM((width, TILE), bf16),
                *([pltpu.VMEM(a.shape, f32) for a in (byte_sum, unit_kv)] if last else []),
            ],
        ),
        out_shape=out_shape,
        compiler_params=limits(58),
        cost_estimate=cost(12 * count),
        name="back",
    )(lengths, place, *operands)


def assemble_kernel(place_ref, own_ref, *refs):
    *far_refs, out_ref = refs
    side, corner = place_ref[0] // 2, place_ref[1] % 4
    rows = own_ref.shape[0]
    quarter = rows // 4

    def put(start, ref):
        out_ref[pl.ds(pl.multiple_of(start, 16), ref.shape[0])] = ref[...].astype(bf16)

    put(side * rows, own_ref)
    for step, ref in enumerate(far_refs):
        put((1 - side) * rows + (corner ^ step) * quarter, ref)


def assemble(place, own, far, tokens=()):
    rows, width = own.shape
    operands = (own, *far)
    return pl.pallas_call(
        ignoring(assemble_kernel, 1 + len(operands), len(tokens)),
        in_specs=[
            pl.BlockSpec(memory_space=pltpu.SMEM), *([pl.BlockSpec(memory_space=pltpu.VMEM)] * len(operands)),
            *([ANYWHERE] * len(tokens)),
        ],
        out_specs=pl.BlockSpec(memory_space=pltpu.VMEM),
        out_shape=jax.ShapeDtypeStruct((2 * rows, width), bf16),
        compiler_params=limits(40),
        cost_estimate=cost(2),
        name="assemble",
    )(place, *operands, *tokens)


def packed(block):
    rows, cols = block.shape
    parts = [block[:, c : c + 128] for c in range(0, cols - 127, 128)]
    if cols % 128:
        last = block[:, cols - 64 :]
        parts.append(jnp.concatenate([last[: rows // 2], last[rows // 2 :]], axis=1))
    return jnp.concatenate(parts, axis=0)


def unpacked(block, cols):
    rows = block.shape[0] * 128 // cols
    count = cols // 128
    parts = [block[c * rows : (c + 1) * rows] for c in range(count)]
    if cols % 128:
        last = block[count * rows :]
        parts.append(jnp.concatenate([last[:, :64], last[:, 64:]], axis=0))
    return jnp.concatenate(parts, axis=1)


def reversed_bits(count):
    order = [0]
    while len(order) < count:
        order = [2 * o for o in order] + [2 * o + 1 for o in order]
    return order


def split_blocks(keep_ref, send_ref, total, dp_place, shape=lambda block: block):
    count = keep_ref.shape[0]
    size = total.shape[0] // count // 2
    for ref, flip in ((keep_ref, 0), (send_ref, 1)):
        for j, distance in enumerate(reversed_bits(count)):
            target = dp_place ^ (2 * distance + flip)
            ref[j] = shape(total[pl.ds(pl.multiple_of(target * size, 8), size)])


def put_blocks(keep_ref, send_ref, total, dp_place):
    split_blocks(keep_ref, send_ref, total, dp_place, packed)


def call(kernel, grid, inputs, outputs, scratch=(), tokens=(), name=None, time=1, limit=56):
    whole = lambda a: (a, a.shape, lambda *_: (0,) * a.ndim)
    inputs = [i if isinstance(i, tuple) else whole(i) for i in inputs]
    specs = [pl.BlockSpec(block, index) if block else pl.BlockSpec(memory_space=pltpu.SMEM) for _, block, index in inputs]
    return pl.pallas_call(
        ignoring(kernel, len(inputs), len(tokens)),
        grid=grid,
        in_specs=[*specs, *([ANYWHERE] * len(tokens))],
        out_specs=[pl.BlockSpec(block, index) for _, _, block, index in outputs],
        out_shape=[jax.ShapeDtypeStruct(shape, kind) for shape, kind, _, _ in outputs],
        scratch_shapes=list(scratch),
        compiler_params=limits(limit),
        cost_estimate=cost(time),
        name=name,
    )(*(a for a, _, _ in inputs), *tokens)


def scalars(place):
    return place, None, None


def each(array):
    return array, (1, *array.shape[1:]), lambda i: (i, *(0,) * (array.ndim - 1))


def part(array, first):
    return array, (1, *array.shape[1:]), lambda i: (first + i, *(0,) * (array.ndim - 1))


def among(array, group, size):
    return array, (1, *array.shape[1:]), lambda i: (jnp.clip(i - group * size, 0, size - 1), 0, 0)


def new(shape, kind=f32):
    return shape, kind, (1, *shape[1:]), lambda i: (i, *(0,) * (len(shape) - 1))


def kept(shape, kind=f32):
    return shape, kind, shape, lambda i: (0,) * len(shape)


def mix(place, own, far, w_out, tokens=()):
    count, rows, lat_count = own.shape

    def kernel(place_ref, own_ref, far_ref, w_ref, out_ref, att_ref):
        side = place_ref[0] // 2
        for ref, at in ((own_ref, side), (far_ref, 1 - side)):
            att_ref[pl.ds(pl.multiple_of(at * rows, 16), rows)] = ref[0].astype(bf16)
        out_ref[0] = dot_tn(att_ref[...], w_ref[...])

    return call(
        kernel, (count,), [scalars(place), each(own), each(far), w_out], [new((count, lat_count, w_out.shape[1]))],
        [pltpu.VMEM((2 * rows, lat_count), bf16)], tokens, "mix", 3, 14,
    )[0]


def feed(place, first, latents, out_grad, mixed, crossed, gain, w_one, w_two, tokens=()):
    count, lat_count, width = mixed.shape
    rows = w_one.shape[0] // 2

    def kernel(
        place_ref, lat_ref, grad_ref, mixed_ref, crossed_ref, gain_ref, w_one_ref, w_two_ref,
        hidden_ref, normed_ref, activated_ref, share_ref, own_ref, up_own_ref, parts_ref,
    ):
        side = place_ref[0] // 2

        def own(tensor):
            parts_ref[0] = tensor[:, :rows]
            parts_ref[1] = tensor[:, rows:]
            return parts_ref[side]

        hidden = lat_ref[0].astype(f32) + (mixed_ref[0] + crossed_ref[0])
        hidden_ref[0] = hidden
        unit, _ = row_norm(hidden)
        normed = (unit * gain_ref[...]).astype(bf16)
        normed_ref[0] = normed
        up = dot_nt(normed, w_one_ref[...])
        below = 0.5 * (1.0 + lax.erf(up * 0.5**0.5))
        activated = (up * below).astype(bf16)
        activated_ref[0] = activated
        own_ref[0] = own(activated)
        slope = below + up * (jnp.exp(-0.5 * up * up) * 0.3989422804014327)
        up_grad = (dot_nt(grad_ref[0], w_two_ref[...]) * slope).astype(bf16)
        up_own_ref[0] = own(up_grad)
        share_ref[0] = dot(up_grad, w_one_ref[...])

    full, low = (count, lat_count, width), (count, lat_count, rows)
    return call(
        kernel, (count,),
        [scalars(place), part(latents, first), part(out_grad, first), each(mixed), each(crossed), gain, w_one, w_two],
        [new(full), new(full, bf16), new((count, lat_count, 2 * rows), bf16), new(full), new(low, bf16), new(low, bf16)],
        [pltpu.VMEM((2, lat_count, rows), bf16)], tokens, "feed", 6, 36,
    )


def split_grad(blocks, width, rows):
    return kept((blocks // 2, width // blocks * rows // 128, 128))


def feed_weights(place, out_grad, fed, blocks, tokens=()):
    items, lat_count, width = out_grad.shape
    groups = len(fed)
    size = items // groups
    rows = fed[0][1].shape[2]

    def kernel(place_ref, grad_ref, *refs):
        item = pl.program_id(0)
        keep_one, send_one, keep_two, send_two, one_sum, two_sum = refs[3 * groups :]

        @pl.when(item == 0)
        def _():
            one_sum[...] = jnp.zeros_like(one_sum)
            two_sum[...] = jnp.zeros_like(two_sum)

        for g in range(groups):

            @pl.when(item // size == g)
            def _():
                normed_ref, activated_ref, up_grad_ref = refs[3 * g : 3 * g + 3]
                two_sum[...] += dot_tn(grad_ref[0], activated_ref[0])
                one_sum[...] += dot_tn(normed_ref[0], up_grad_ref[0])

        @pl.when(item == items - 1)
        def _():
            put_blocks(keep_two, send_two, two_sum, place_ref[1])
            put_blocks(keep_one, send_one, one_sum, place_ref[1])

    return call(
        kernel, (items,), [scalars(place), each(out_grad), *(among(a, g, size) for g in range(groups) for a in fed[g])],
        [split_grad(blocks, width, rows)] * 4, [pltpu.VMEM((width, rows), f32)] * 2, tokens, "feed_weights", 6, 26,
    )


def unmix(place, first, out_grad, hidden, share, crossed, gain, w_out, att, before, blocks, heads, tokens=()):
    count, lat_count, width = hidden.shape
    rows = w_out.shape[0]
    val = rows // heads

    def kernel(place_ref, grad_ref, hidden_ref, share_ref, crossed_ref, gain_ref, w_ref, att_ref, *refs):
        item = pl.program_id(0)
        sums_in, refs = refs[: len(before)], refs[len(before) :]
        hidden_grad_ref, att_grad_ref, att_grad_t_ref, delta_ref, gain_grad_ref, sum_ref, *split = refs

        @pl.when(item == 0)
        def _():
            for i, ref in enumerate((gain_grad_ref, sum_ref)):
                ref[...] = sums_in[i][...] if before else jnp.zeros_like(ref)

        unit, inv = row_norm(hidden_ref[0])
        norm_grad = share_ref[0] + crossed_ref[0]
        gain_grad_ref[...] += jnp.sum(norm_grad * unit, axis=0, keepdims=True)
        hidden_grad = grad_ref[0].astype(f32) + row_norm_back(norm_grad, unit, inv, gain_ref[...])
        hidden_grad_ref[0] = hidden_grad
        mixed_grad = hidden_grad.astype(bf16)
        att = att_ref[0].T
        sum_ref[...] += dot_tn(mixed_grad, att.astype(bf16))
        att_grad = dot_nt(mixed_grad, w_ref[...])
        att_grad_ref[0] = att_grad.astype(bf16)
        att_grad_t_ref[0] = att_grad.T.astype(bf16)
        product = att_grad.astype(bf16).astype(f32) * att
        lane = lax.broadcasted_iota(jnp.int32, delta_ref.shape[1:], 1)
        delta = jnp.zeros(delta_ref.shape[1:], f32)
        for h in range(heads):
            delta = jnp.where(lane == h, jnp.sum(product[:, h * val : (h + 1) * val], axis=1, keepdims=True), delta)
        delta_ref[0] = delta
        if split:

            @pl.when(item == count - 1)
            def _():
                put_blocks(*split, sum_ref, place_ref[1])

    full = (count, lat_count, width)
    return call(
        kernel, (count,),
        [
            scalars(place), part(out_grad, first), each(hidden), each(share), each(crossed), gain, w_out, each(att), *before,
        ],
        [
            new(full), new((count, lat_count, rows), bf16), new((count, rows, lat_count), bf16), new((count, lat_count, 128)),
            kept((1, width)), kept((width, rows)), *([split_grad(blocks, width, rows)] * 2 if first else []),
        ],
        [], tokens, "unmix", 6, 32,
    )


def branch(activated, w_two):
    count, lat_count, _ = activated[0].shape
    groups = len(activated)
    width = w_two.shape[1]

    def kernel(*refs):
        *group_refs, w_ref, out_ref = refs
        for g in range(groups):

            @pl.when(pl.program_id(0) // count == g)
            def _():
                out_ref[0] = dot(group_refs[g][0], w_ref[...])

    return call(
        kernel, (count * groups,), [*(among(a, g, count) for g, a in enumerate(activated)), w_two],
        [new((count * groups, lat_count, width))], [], (), "branch", 4, 20,
    )[0]


def latent(place, query_grad, latents, hidden_grad, gain, w_query, hidden, share, crossed, blocks):
    items, lat_count, width = latents.shape
    rows = w_query[0].shape[0]
    groups = len(hidden)
    size = items // groups

    def kernel(
        place_ref, own_ref, core_ref, far_ref, far_core_ref, lat_ref, share_ref, crossed_ref, gain_ref,
        w_own, w_core, w_far, w_far_core, *refs,
    ):
        group_refs = [refs[2 * g : 2 * g + 2] for g in range(groups)]
        grad_ref, out_ref, gain_grad_ref, keep_ref, send_ref, w_ref, parts_ref, sum_ref, turned_ref = refs[2 * groups :]
        item = pl.program_id(0)
        place = place_ref[0]

        def put(target, refs, value):
            for step, ref in enumerate(refs):
                target[pl.ds(pl.multiple_of((place ^ step) * rows, 16), rows)] = value(ref).astype(bf16)

        @pl.when(item == 0)
        def _():
            put(w_ref, (w_own, w_core, w_far, w_far_core), lambda ref: ref[...])
            gain_grad_ref[...] = jnp.zeros_like(gain_grad_ref)
            sum_ref[...] = jnp.zeros_like(sum_ref)

        put(parts_ref, (own_ref, core_ref, far_ref, far_core_ref), lambda ref: ref[0])
        unit, inv = row_norm(lat_ref[0].astype(f32))
        gain = gain_ref[...]
        sum_ref[...] += dot(own_ref[0].astype(bf16), (unit * gain).astype(bf16))
        norm_grad = dot_tn(parts_ref[...], w_ref[...])
        gain_grad_ref[...] += jnp.sum(norm_grad * unit, axis=0, keepdims=True)
        for g in range(groups):

            @pl.when(item // size == g)
            def _():
                hidden_grad_ref, hidden_ref = group_refs[g]
                grad_ref[0] = hidden_grad_ref[0] + row_norm_back(norm_grad, unit, inv, gain)
                out_ref[0] = (hidden_ref[0] + (share_ref[0] + crossed_ref[0])).astype(bf16)

        @pl.when(item == items - 1)
        def _():
            turned_ref[...] = sum_ref[...].T
            put_blocks(keep_ref, send_ref, turned_ref, place_ref[1])

    return call(
        kernel, (items,),
        [
            scalars(place), *(each(q) for q in query_grad), each(latents), each(share), each(crossed), gain, *w_query,
            *(among(a, g, size) for g in range(groups) for a in (hidden_grad[g], hidden[g])),
        ],
        [new(latents.shape), new(latents.shape, bf16), kept((1, width)), *([split_grad(blocks, width, rows)] * 2)],
        [
            pltpu.VMEM((4 * rows, width), bf16), pltpu.VMEM((4 * rows, lat_count), bf16), pltpu.VMEM((rows, width), f32),
            pltpu.VMEM((width, rows), f32),
        ], (), "latent", 16, 36,
    )


def at(array, index):
    return array, (1, *array.shape[1:]), lambda *_: (index, *(0,) * (array.ndim - 1))


def pos_blocks(columns, slots):
    return [
        (packed(columns[:, c : c + slots]), packed(columns[:, c + slots : c + 2 * slots]))
        for c in range(0, columns.shape[1], 2 * slots)
    ]


def first_sums(place, pos_a, near_a, far_a, pos_b, near_b, far_b, pos_c, near_c, slots):
    share = far_a.shape[0]
    count = (far_a.shape[1] + far_b.shape[1]) // slots // 2

    def kernel(
        place_ref, pos_a_ref, near_a_ref, far_a_ref, pos_b_ref, near_b_ref, far_b_ref, pos_c_ref, near_c_ref, out_ref, keep_ref,
        send_ref,
    ):
        side = place_ref[1] % 2
        out_ref[...] = pos_c_ref[0] + near_c_ref[0]
        blocks = pos_blocks(pos_a_ref[0] + near_a_ref[0] + far_a_ref[...], slots)
        blocks += pos_blocks(pos_b_ref[0] + near_b_ref[0] + far_b_ref[...], slots)
        for i, (low, high) in enumerate(blocks):
            keep_ref[i] = jnp.where(side == 0, low, high)
            send_ref[i] = jnp.where(side == 0, high, low)

    split = kept((count, share * slots // 128, 128))
    return call(
        kernel, (1,),
        [
            scalars(place), at(pos_a, 0), at(near_a, 2), far_a, at(pos_b, 0), at(near_b, 2), far_b, at(pos_c, 1), at(near_c, 3),
        ],
        [kept(pos_c.shape[1:]), split, split], [], (), "first_sums", 4, 40,
    )


def second_sums(place, pos, near, far, gain_lat, gain_mlp, slots, vocab):
    share, cols = far.shape
    own = gain_lat.shape[1] // 4
    count = TILE // slots // 2
    rows = share * slots // 128
    byte_rows = share // 2 * (cols - TILE) // 128
    first = vocab + 1 + -(vocab + 1) % 8

    def kernel(place_ref, pos_ref, near_ref, far_ref, lat_ref, mlp_ref, keep_ref, send_ref, byte_ref, gains_ref):
        side = place_ref[1] % 2
        mine = pos_ref[0] + near_ref[0] + far_ref[...]
        byte_ref[...] = mine[:, TILE:]
        gains = jnp.concatenate([lat_ref[...], mlp_ref[...], jnp.zeros((6, lat_ref.shape[1]), f32)], axis=0)
        gains_ref[...] = gains.T
        gains = gains_ref[pl.ds(pl.multiple_of(place_ref[0] * own, 8), own)]
        byte_ref[:, first : first + 8] = gains[:share]
        byte_ref[: own - share, first + 8 : first + 16] = gains[share:]
        blocks = pos_blocks(mine[:, :TILE], slots)
        blocks.append((packed(byte_ref[: share // 2]), packed(byte_ref[share // 2 :])))
        start = 0
        for low, high in blocks:
            stretch = slice(start, start + low.shape[0])
            keep_ref[stretch] = jnp.where(side == 0, low, high)
            send_ref[stretch] = jnp.where(side == 0, high, low)
            start += low.shape[0]

    split = kept((count * rows + byte_rows, 128))
    return call(
        kernel, (1,), [scalars(place), at(pos, 0), at(near, 2), far, gain_lat, gain_mlp], [split, split],
        [pltpu.VMEM((share, cols - TILE), f32), pltpu.VMEM((gain_lat.shape[1], 8), f32)], (), "second_sums", 3, 40,
    )


def third_sums(place, keep_ab, cross_ab, keep, cross, byte_rows, half):
    before, rows, _ = keep_ab.shape
    last = (keep.shape[0] - byte_rows) // rows
    count = before + last
    size, part = byte_rows // count, half // count

    def kernel(place_ref, keep_ab_ref, cross_ab_ref, keep_ref, cross_ref, pos_keep_ref, pos_send_ref, byte_ref):
        ring = place_ref[1] // 2
        sums = [keep_ab_ref[i] + cross_ab_ref[i] for i in range(before)]
        total = keep_ref[...] + cross_ref[...]
        sums += [total[i * rows : (i + 1) * rows] for i in range(last)]
        for i in range(count // 2):
            pos_keep_ref[i] = jnp.where(ring % 2 == 0, sums[2 * i], sums[2 * i + 1])
            pos_send_ref[i] = jnp.where(ring % 2 == 0, sums[2 * i + 1], sums[2 * i])
        total = total[last * rows :]
        for j in range(count):
            distance = ring ^ j
            place, bits = 0, count.bit_length() - 1
            for b in range(bits):
                place += (distance >> b & 1) << (bits - 1 - b)
            byte_ref[place] = jnp.concatenate(
                [total[c + j * part : c + (j + 1) * part] for c in range(0, byte_rows, half)], axis=0
            )

    split = kept((count // 2, rows, 128))
    return call(
        kernel, (1,), [scalars(place), keep_ab, cross_ab, keep, cross], [split, split, kept((count, size, 128))], [], (),
        "third_sums", 3, 40,
    )


def next_sums(place, keep, cross, bit, parts=()):
    count, rows, _ = keep.shape

    def kernel(place_ref, keep_ref, cross_ref, *refs):
        part_refs, (pos_keep_ref, pos_send_ref, *sum_ref) = refs[: len(parts)], refs[len(parts) :]
        mine = place_ref[1] // bit % 2
        sums = [keep_ref[i] + cross_ref[i] for i in range(count)]
        for i in range(count // 2):
            pos_keep_ref[i] = jnp.where(mine == 0, sums[2 * i], sums[2 * i + 1])
            pos_send_ref[i] = jnp.where(mine == 0, sums[2 * i + 1], sums[2 * i])
        if parts:
            sum_ref[0][...] = sum(ref[0] if len(ref.shape) == 3 else ref[...] for ref in part_refs)

    split = kept((count // 2, rows, 128))
    return call(
        kernel, (1,), [scalars(place), keep, cross, *parts], [split, split, *([kept(parts[1].shape)] if parts else [])], [], (),
        "next_sums", 2, 40,
    )


def last_sums(place, keep, cross, parts, share):
    count = len(parts)
    size = parts[0].shape[0]
    rows = keep.shape[1]
    half = share // 2
    part = half // count
    lanes = size // part

    def kernel(place_ref, keep_ref, cross_ref, *refs):
        part_refs, (pos_ref, byte_ref, held_ref) = refs[:count], refs[count:]
        pos_ref[...] = unpacked(keep_ref[0] + cross_ref[0], pos_ref.shape[1])
        for distance, ref in enumerate(part_refs):
            held_ref[place_ref[1] // 2 ^ distance] = ref[...]
        byte_ref[...] = jnp.concatenate(
            [held_ref[j, c * part : (c + 1) * part] for c in range(lanes) for j in range(count)], axis=0
        )

    return call(
        kernel, (1,), [scalars(place), keep, cross, *parts], [kept((share, rows * 128 // share)), kept((count * size, 128))],
        [pltpu.VMEM((count, size, 128), f32)], (), "last_sums", 2, 40,
    )


def byte_sums(place, own, other, share, vocab, gain_cols):
    cols = own.shape[0] * 128 // (share // 2)
    first = vocab + 1 + -(vocab + 1) % 8

    def kernel(place_ref, own_ref, other_ref, table_ref, gain_ref, gains_ref):
        side = place_ref[1] % 2
        low = jnp.where(side == 0, own_ref[...], other_ref[...])
        high = jnp.where(side == 0, other_ref[...], own_ref[...])
        turned = jnp.concatenate([unpacked(low, cols), unpacked(high, cols)], axis=0).T
        table_ref[...] = turned[:vocab]
        gain_ref[...] = turned[vocab : vocab + 1]
        gains_ref[...] = jnp.concatenate([turned[first : first + 2], turned[first + 8 : first + 10, : gain_cols - share]], axis=1)

    return call(
        kernel, (1,), [scalars(place), own, other], [kept((vocab, share)), kept((1, share)), kept((2, gain_cols))], [], (),
        "byte_sums", 2, 40,
    )


def swap(tensor, axis, bit):
    return lax.ppermute(tensor, axis, [(i, i ^ bit) for i in range(lax.axis_size(axis))])


def stage(always, work):
    shapes = jax.eval_shape(work)
    return lax.cond(always, work, lambda: jax.tree.map(lambda s: jnp.zeros(s.shape, s.dtype), shapes))


def body(
    byte_ids, lengths, latents, byte_table, pos_table, gain_in, gain_lat, gain_mlp,
    w_query, w_key, w_value, w_out, w_one, w_two, out_grad,
):
    items, slots = byte_ids.shape
    vocab, width = byte_table.shape
    lat_count, lat_width = latents.shape[1:]
    mp, dp = lax.axis_size("mp"), lax.axis_size("dp")
    mp_place, dp_place = lax.axis_index("mp"), lax.axis_index("dp")
    place = jnp.stack([mp_place, dp_place]).astype(jnp.int32)
    heads = HEADS // mp
    qk_cols = w_query.shape[1]
    val_cols = w_value.shape[1]
    corner, side = dp_place % 4, dp_place % 2

    shards = [w_out, w_one.T, w_two]
    quarter = val_cols // 4
    always = lengths[0] > 0
    over_y = lambda w: swap(lax.dynamic_slice_in_dim(w, corner * quarter, quarter, 0).astype(f32), "mp", 2)
    over_x, over_z, over_both = (lambda a, bits=bits: swap(a, "dp", bits) for bits in (1, 2, 3))
    core = lambda a: swap(a, "mp", 1)
    half = items // 2

    def first_stage():
        weights = (gain_in[None], w_key.T, w_value.T, *shards[1:])
        return over_y(shards[0]), tables_of(place, byte_table, pos_table, *weights)

    out, (*tables, w_back, w_rows, one, two) = stage(always, first_stage)

    def front_of(first):
        return front(first, half, lengths, byte_ids, *tables, latents, gain_lat[None], w_query.T, heads)

    def second_stage():
        return front_of(0), [over_x(out), over_z(out)], over_both(out), swap(one, "mp", 2), swap(two, "mp", 2)

    (*made_a, att_a), crossed_out, last_out, one, two = stage(always, second_stage)

    def third_stage():
        return front_of(half), [over_x(one), over_z(one), over_both(one)], swap(att_a, "mp", 2)

    (*made_b, att_b), crossed_one, far_a = stage(always, third_stage)

    def fourth_stage():
        w_out_whole = assemble(place, shards[0], [out, *crossed_out, last_out])
        w_one_whole = assemble(place, shards[1], [one, *crossed_one], [w_out_whole])
        mixed_a = mix(place, att_a, far_a, w_out_whole, [w_one_whole])
        return w_out_whole, w_one_whole, mixed_a, [over_x(two), over_z(two), over_both(two)], swap(att_b, "mp", 2)

    w_out_whole, w_one_whole, mixed_a, crossed_two, far_b = stage(always, fourth_stage)
    w_two_whole = assemble(place, shards[2], [two, *crossed_two])
    mixed_b = mix(place, att_b, far_b, w_out_whole, [w_two_whole])
    gain = gain_mlp[None]
    weights = (gain, w_one_whole, w_two_whole)
    hidden_a, normed_a, activated_a, share_a, act_a, up_a = feed(
        place, 0, latents, out_grad, mixed_a, core(mixed_a), *weights, [mixed_b]
    )
    hidden_b, normed_b, activated_b, share_b, act_b, up_b = feed(
        place, half, latents, out_grad, mixed_b, core(mixed_b), *weights, [share_a]
    )
    keep_one, send_one, keep_two, send_two = feed_weights(
        place, out_grad, [(normed_a, act_a, up_a), (normed_b, act_b, up_b)], dp
    )
    w_query_own = w_query.T.astype(f32)
    crossed_a, crossed_b = core(share_a), core(share_b)

    def unmix_stage():
        grads_a = unmix(place, 0, out_grad, hidden_a, share_a, crossed_a, gain, w_out, att_a, [], dp, heads)
        grads_b = unmix(place, half, out_grad, hidden_b, share_b, crossed_b, gain, w_out, att_b, grads_a[4:], dp, heads)
        w_query_parts = core(w_query_own), swap(w_query_own, "mp", 2)
        return grads_a[:4], grads_b[:5], grads_b[6:], swap(send_two, "dp", 1), w_query_parts

    (hidden_grad_a, *grads_a), (hidden_grad_b, *grads_b, gain_mlp_grad), (keep_out, send_out), cross_two, w_query_parts = stage(
        always, unmix_stage
    )
    made = [(*made_a, *grads_a), (*made_b, *grads_b)]
    byte_cols = vocab + -vocab % 128
    bits = [1 << i for i in range(1, dp.bit_length() - 1)]

    def back_of(first, count, sums):
        return back(place, first, count, lengths, byte_ids, made, w_back, w_rows, tables[3], sums, heads, vocab)

    def halve(blocks, bits):
        for bit in bits:
            count = blocks.shape[0] // 2
            blocks = blocks[:count] + swap(blocks[count:], "dp", bit)
        return blocks

    two_blocks = keep_two + cross_two

    def back_stage_a():
        transfers = swap(send_one, "dp", 1), halve(two_blocks, bits[:1]), core(w_query_parts[1])
        return back_of(0, 2, []), transfers

    (pos_a, *sums), (cross_one, two_blocks, w_query_last) = stage(always, back_stage_a)
    w_query_all = [w_query_own, *w_query_parts, w_query_last]

    def back_stage_b():
        transfers = swap(send_out, "dp", 1), core(pos_a), halve(two_blocks, bits[1:]), halve(keep_one + cross_one, bits[:1])
        return back_of(2, 1, sums), transfers

    (pos_b, *sums), (cross_out, near_a, two_blocks, one_blocks) = stage(always, back_stage_b)

    def back_stage_c():
        far_pos_a = swap(pos_a[1] + near_a[3], "mp", 2)
        transfers = core(pos_b), halve(one_blocks, bits[1:]), halve(keep_out + cross_out, bits[:1])
        return back_of(3, 1, sums), far_pos_a, transfers

    (pos_c, query_own, keep_kv, send_kv), far_pos_a, (near_b, one_blocks, out_blocks) = stage(always, back_stage_c)

    def tail_stage_a():
        transfers = (
            core(pos_c), swap(query_own, "mp", 2), core(query_own), swap(pos_b[1] + near_b[3], "mp", 2), swap(send_kv, "dp", 1),
        )
        return branch((activated_a, activated_b), w_two_whole), transfers, halve(out_blocks, bits[1:])

    share_out, (near_c, query_far, query_near, far_pos_b, cross_kv), out_blocks = stage(always, tail_stage_a)
    slot_share, share = slots // dp, width // mp

    def tail_stage_b():
        send_c, keep_ab, send_ab = first_sums(
            place, pos_a, near_a, far_pos_a, pos_b, near_b, far_pos_b, pos_c, near_c, slot_share
        )
        query_all = [query_own, query_near, query_far, core(query_far)]
        latent_out = latent(
            place, query_all, latents, (hidden_grad_a, hidden_grad_b), gain_lat[None], w_query_all, (hidden_a, hidden_b),
            share_out, core(share_out), dp,
        )
        kv_blocks = halve(keep_kv + cross_kv, bits[:1])
        return latent_out, swap(send_c, "mp", 2), keep_ab, swap(send_ab, "dp", 1), kv_blocks

    latent_out, far_pos_c, keep_ab, cross_ab, kv_blocks = stage(always, tail_stage_b)
    latent_grad, latents_out, gain_lat_grad, keep_query, send_query = latent_out
    keep_c, send_c = second_sums(place, pos_c, near_c, far_pos_c, gain_lat_grad, gain_mlp_grad, slot_share, vocab)
    cross_c, cross_query = swap(send_c, "dp", 1), swap(send_query, "dp", 1)
    byte_rows = share // 2 * byte_cols // 128
    pos_keep, pos_send, byte_blocks = third_sums(place, keep_ab, cross_ab, keep_c, cross_c, byte_rows, share // 2)
    cross = swap(pos_send, "dp", bits[0])
    kv_sum = halve(kv_blocks, bits[1:])[0]
    query_blocks = halve(keep_query + cross_query, bits[:1])
    byte_parts = [byte_blocks[:1]] + [swap(byte_blocks[j], "dp", 2 * d) for j, d in enumerate(reversed_bits(dp // 2)) if d]
    for k, bit in enumerate(bits[1:]):
        pos_keep, pos_send, *byte_own = next_sums(place, pos_keep, cross, bit, [] if k else byte_parts)
        byte_sum = byte_sum if k else byte_own[0]
        cross = swap(pos_send, "dp", bit)
    query_sum = halve(query_blocks, bits[1:])[0]
    byte_parts = [byte_sum] + [swap(byte_sum, "dp", 2 * d) for d in range(1, dp // 2)]
    pos_sum, byte_half = last_sums(place, pos_keep, cross, byte_parts, share)
    byte_grad, gain_in_grad, gains = byte_sums(place, byte_half, swap(byte_half, "dp", 1), share, vocab, val_cols)
    two_sum, one_sum, out_sum = (unpacked(a[0], val_cols) for a in (two_blocks, one_blocks, out_blocks))
    return (
        latents_out, latent_grad, byte_grad, pos_sum.T, gain_in_grad[0], gains[0], gains[1],
        unpacked(query_sum, qk_cols), kv_sum[:, :qk_cols], kv_sum[:, qk_cols:], out_sum.T, one_sum, two_sum.T,
    )


def solution(mesh):
    return jax.shard_map(
        body,
        mesh=mesh,
        in_specs=(
            P("dp", None),
            P("dp"),
            P("dp", None, None),
            P(),
            P(),
            P(),
            P(),
            P(),
            P(None, "mp"),
            P(None, "mp"),
            P(None, "mp"),
            P("mp", None),
            P(None, "mp"),
            P("mp", None),
            P("dp", None, None),
        ),
        out_specs=(
            P("dp", None, None),
            P("dp", None, None),
            P(None, "mp"),
            P("dp", "mp"),
            P("mp"),
            P("mp"),
            P("mp"),
            P("dp", "mp"),
            P("dp", "mp"),
            P("dp", "mp"),
            P("mp", "dp"),
            P("dp", "mp"),
            P("mp", "dp"),
        ),
        check_vma=False,
    )
```

```python
import functools

import jax
import jax.numpy as jnp
from jax import lax
from jax.experimental import pallas as pl
from jax.experimental.pallas import tpu as pltpu
from jax.sharding import PartitionSpec as P

HEADS = 8
EPSILON = 1e-05
MASKED = -1e30
LOG2E = 1.4426950408889634
TILE = 512
COST = 11500000000
f32, bf16 = jnp.float32, jnp.bfloat16
ANYWHERE = pl.BlockSpec(memory_space=pl.ANY)


def dot(left, right):
    return jnp.dot(left, right, preferred_element_type=f32)


def dot_nt(left, right):
    return lax.dot_general(left, right, (((1,), (1,)), ((), ())), preferred_element_type=f32)


def dot_tn(left, right):
    return lax.dot_general(left, right, (((0,), (0,)), ((), ())), preferred_element_type=f32)


def cost(microseconds):
    return pl.CostEstimate(flops=microseconds * COST, bytes_accessed=0, transcendentals=0)


def limits(mebibytes):
    return pltpu.CompilerParams(vmem_limit_bytes=mebibytes * 2**20)


def ignoring(kernel, start, count):
    def inner(*refs):
        return kernel(*refs[:start], *refs[start + count :])

    return inner


def row_norm(rows):
    centered = rows - jnp.mean(rows, axis=-1, keepdims=True)
    inv_std = lax.rsqrt(jnp.mean(centered * centered, axis=-1, keepdims=True) + EPSILON)
    return centered * inv_std, inv_std


def row_norm_back(upstream, unit, inv, gain):
    scaled = upstream * gain
    row_mean = jnp.mean(scaled, axis=-1, keepdims=True)
    row_cross = jnp.mean(scaled * unit, axis=-1, keepdims=True)
    return inv * (scaled - row_mean - unit * row_cross)


def front_kernel(
    lengths, ids_ref, table_ref, pos_ref, pos_mean_ref, gain_ref, w_kv_ref, lat_ref, gain_lat_ref, w_query_ref,
    unit_ref, inv_ref, kv_ref, lse_ref, query_ref, query_t_ref, att_ref,
    x_ref, normed_ref, scores_ref, total_ref, peak_ref,
    *, first, width, heads,
):
    step = pl.program_id(1)
    item = first + pl.program_id(0)
    length = lengths[item]
    lat_count = lat_ref.shape[1]
    qk_cols = w_query_ref.shape[0]
    qk = qk_cols // heads
    val = (w_kv_ref.shape[0] - qk_cols) // heads
    scale = qk**-0.5 * LOG2E
    chunk = 64

    @pl.when(step == 0)
    def _():
        unit_lat, _ = row_norm(lat_ref[0].astype(f32))
        queries = dot_nt((unit_lat * gain_lat_ref[...]).astype(bf16), w_query_ref[...])
        query_ref[0] = queries.astype(bf16)
        query_t_ref[0] = queries.T.astype(bf16)
        peak_ref[...] = jnp.full_like(peak_ref, MASKED)

    @pl.when(step * TILE < length)
    def _():
        cols = pl.ds(pl.multiple_of(step * TILE, TILE), TILE)
        hits = (lax.broadcasted_iota(jnp.int32, (table_ref.shape[1], TILE), 0) == ids_ref[pl.ds(item, 1), cols]).astype(bf16)
        x_ref[...] = dot(table_ref[...], hits)
        mean = x_ref[width : width + 1] + x_ref[width + 1 : width + 2] + x_ref[width + 2 : width + 3]
        mean = mean + pos_mean_ref[:, cols]
        square = jnp.zeros((8, TILE), f32)
        for r in range(0, width, chunk):
            rows = x_ref[r : r + chunk] + pos_ref[r : r + chunk].astype(f32) - mean
            x_ref[r : r + chunk] = rows
            rows = rows * rows
            square += sum(rows[i : i + 8] for i in range(0, chunk, 8))
        inv = lax.rsqrt(jnp.sum(square, axis=0, keepdims=True) * (1.0 / width) + EPSILON)
        inv_ref[0, :, cols] = inv
        for r in range(0, width, chunk):
            unit = x_ref[r : r + chunk] * inv
            unit_ref[0, r : r + chunk] = unit.astype(bf16)
            gain = jnp.concatenate([gain_ref[r : r + chunk]] * (TILE // 128), axis=1)
            normed_ref[r : r + chunk] = (unit * gain).astype(bf16)
        kv_ref[0, :, cols] = dot(w_kv_ref[...], normed_ref[...]).astype(bf16)
        live = step * TILE + lax.broadcasted_iota(jnp.int32, (1, TILE), 1) < length
        for h in range(heads):
            scores = dot(query_ref[0, :, h * qk : (h + 1) * qk], kv_ref[0, h * qk : (h + 1) * qk, cols])
            scores = jnp.where(live, scores, MASKED)
            scores_ref[h, :, cols] = scores
            peak = peak_ref[h]
            for c in range(0, TILE, 128):
                peak = jnp.maximum(peak, scores[:, c : c + 128])
            peak_ref[h] = peak

    @pl.when(step == pl.num_programs(1) - 1)
    def _():
        peaks = [jnp.max(peak_ref[h], axis=1, keepdims=True) for h in range(heads)]
        total_ref[...] = jnp.zeros_like(total_ref)

        def attend(t, sums):
            cols = pl.ds(pl.multiple_of(t * TILE, TILE), TILE)
            new = []
            for h in range(heads):
                raised = jnp.exp2((scores_ref[h, :, cols] - peaks[h]) * scale)
                new.append(sums[h] + sum(raised[:, c : c + 128] for c in range(0, TILE, 128)))
                start = qk_cols + h * val
                total_ref[h] += dot_nt(raised.astype(bf16), kv_ref[0, start : start + val, cols])
            return tuple(new)

        sums = lax.fori_loop(0, pl.cdiv(length, TILE), attend, (jnp.zeros((lat_count, 128), f32),) * heads)
        lane = lax.broadcasted_iota(jnp.int32, (lat_count, 128), 1)
        packed = jnp.zeros((lat_count, 128), f32)
        out = []
        for h in range(heads):
            total = jnp.sum(sums[h], axis=1, keepdims=True)
            out.append(total_ref[h] / total)
            packed = jnp.where(lane == h, peaks[h] * scale + jnp.log2(total), packed)
        att_ref[0] = jnp.concatenate(out, axis=1).T
        lse_ref[0] = packed


def front(first, count, lengths, ids, table, pos, pos_mean, gain, w_kv, latents, gain_lat, w_query, heads):
    slots = ids.shape[1]
    width = pos.shape[0]
    lat_count, lat_width = latents.shape[1:]
    qk_cols = w_query.shape[0]
    kv_cols = w_kv.shape[0]
    val_cols = kv_cols - qk_cols
    whole = lambda a: pl.BlockSpec(a.shape, lambda i, t, *_: (0,) * a.ndim)
    each = lambda *s: pl.BlockSpec((1, *s), lambda i, t, *_: (first + i, 0, 0))
    made = lambda *s: pl.BlockSpec((1, *s), lambda i, t, *_: (i, 0, 0))
    shape = lambda s, d: jax.ShapeDtypeStruct((count, *s), d)

    def live(i, t, lengths):
        return jnp.minimum(t, pl.cdiv(lengths[first + i], TILE) - 1)

    return pl.pallas_call(
        functools.partial(front_kernel, first=first, width=width, heads=heads),
        grid_spec=pltpu.PrefetchScalarGridSpec(
            num_scalar_prefetch=1,
            grid=(count, slots // TILE),
            in_specs=[
                whole(ids), whole(table), pl.BlockSpec((width, TILE), lambda i, t, l: (0, live(i, t, l))), whole(pos_mean),
                whole(gain), whole(w_kv), each(lat_count, lat_width), whole(gain_lat), whole(w_query),
            ],
            out_specs=[
                pl.BlockSpec((1, width, TILE), lambda i, t, l: (i, 0, live(i, t, l))), made(1, slots), made(kv_cols, slots),
                made(lat_count, 128), made(lat_count, qk_cols), made(qk_cols, lat_count), made(val_cols, lat_count),
            ],
            scratch_shapes=[
                pltpu.VMEM((table.shape[0], TILE), f32),
                pltpu.VMEM((width, TILE), bf16),
                pltpu.VMEM((heads, lat_count, slots), f32),
                pltpu.VMEM((heads, lat_count, val_cols // heads), f32),
                pltpu.VMEM((heads, lat_count, 128), f32),
            ],
        ),
        out_shape=[
            shape((width, slots), bf16), shape((1, slots), f32), shape((kv_cols, slots), bf16), shape((lat_count, 128), f32),
            shape((lat_count, qk_cols), bf16), shape((qk_cols, lat_count), bf16),
            shape((val_cols, lat_count), f32),
        ],
        compiler_params=limits(56),
        cost_estimate=cost(18),
        name="front",
    )(lengths, ids, table, pos, pos_mean, gain, w_kv, latents, gain_lat, w_query)


def tables_kernel(
    place_ref, byte_ref, pos_ref, gain_ref, w_key_ref, w_value_ref, w_one_ref, w_two_ref, table_ref, pos_t_ref, mean_ref, gains_ref, w_kv_ref, w_back_ref,
    w_rows_ref, one_ref, two_ref, pad_ref,
):
    vocab, width = byte_ref.shape

    @pl.when(pl.program_id(0) == 0)
    def _():
        rows = one_ref.shape[0]
        quarter = pl.ds(pl.multiple_of(place_ref[1] % 4 * rows, 16), rows)
        one_ref[...] = w_one_ref[quarter].astype(f32)
        two_ref[...] = w_two_ref[quarter].astype(f32)
        gain = gain_ref[...]
        gains_ref[...] = jnp.broadcast_to(gain, (128, width)).T
        first = w_key_ref.shape[0]
        w_kv_ref[:first] = w_key_ref[...]
        w_kv_ref[first:] = w_value_ref[...]
        w_rows_ref[...] = w_kv_ref[...].astype(f32).T.astype(bf16)
        scaled = w_kv_ref[...].astype(f32) * gain
        w_back_ref[...] = (scaled - jnp.mean(scaled, axis=1, keepdims=True)).T.astype(bf16)
        pad_ref[...] = jnp.zeros_like(pad_ref)
        pad_ref[:vocab] = byte_ref[...].astype(f32)
        table = pad_ref[...].T
        table_ref[:width] = table[:, : table_ref.shape[1]].astype(bf16)
        mean = jnp.mean(table, axis=0, keepdims=True)[:, : table_ref.shape[1]]
        high = mean.astype(bf16)
        rest = mean - high.astype(f32)
        middle = rest.astype(bf16)
        low = (rest - middle.astype(f32)).astype(bf16)
        more = table_ref.shape[0] - width
        row = lax.broadcasted_iota(jnp.int32, (more, table_ref.shape[1]), 0)
        rows = jnp.zeros(row.shape, f32)
        for place, value in enumerate((high, middle, low)):
            rows = jnp.where(row == place, value.astype(f32), rows)
        table_ref[width:] = rows.astype(bf16)

    pos = pos_ref[...].astype(f32).T
    pos_t_ref[...] = pos.astype(bf16)
    mean_ref[...] = jnp.mean(pos, axis=0, keepdims=True)


def tables_of(place, byte_table, pos_table, gain, w_key_t, w_value_t, w_one_t, w_two):
    vocab, width = byte_table.shape
    slots = pos_table.shape[0]
    kv_cols = w_key_t.shape[0] + w_value_t.shape[0]
    vocab_rows = vocab + -vocab % 16
    whole = lambda a: pl.BlockSpec(a.shape, lambda t: (0,) * a.ndim)
    shapes = [
        ((width + 16, vocab_rows), bf16), ((width, slots), bf16), ((1, slots), f32), ((width, 128), f32), ((kv_cols, width), bf16),
        ((width, kv_cols), bf16), ((width, kv_cols), bf16), *([((w_two.shape[0] // 4, w_two.shape[1]), f32)] * 2),
    ]
    shapes = [jax.ShapeDtypeStruct(*s) for s in shapes]
    specs = [whole(a) for a in shapes]
    specs[1] = pl.BlockSpec((width, TILE), lambda t: (0, t))
    specs[2] = pl.BlockSpec((1, TILE), lambda t: (0, t))
    return pl.pallas_call(
        tables_kernel,
        grid=(slots // TILE,),
        in_specs=[
            pl.BlockSpec(memory_space=pltpu.SMEM), whole(byte_table), pl.BlockSpec((TILE, width), lambda t: (t, 0)), whole(gain),
            whole(w_key_t), whole(w_value_t), whole(w_one_t), whole(w_two),
        ],
        out_specs=specs,
        out_shape=shapes,
        scratch_shapes=[pltpu.VMEM((vocab + -vocab % 128, width), f32)],
        compiler_params=limits(40),
        cost_estimate=cost(8),
        name="tables",
    )(place, byte_table, pos_table, gain, w_key_t, w_value_t, w_one_t, w_two)


def back_kernel(
    lengths, place_ref, ids_ref, w_ref, w_rows_ref, gain_ref, *refs,
    first, heads, groups, last, vocab,
):
    step, item = pl.program_id(0), pl.program_id(1)
    length = lengths[item]
    tile = step + first
    sums_in, refs = (refs[:3], refs[3:]) if first else ((), refs)
    made = [refs[9 * g : 9 * g + 9] for g in range(groups)]
    refs = refs[9 * groups :]
    pos_ref, query_out_ref, *refs = refs
    if last:
        keep_ref, send_ref, *refs, byte_ref, unit_kv_ref, turned_ref = refs
    else:
        byte_ref, unit_kv_ref, *refs = refs
    (
        unit_ref, inv_ref, kv_ref, lse_ref, query_ref, query_t_ref, att_grad_ref, att_grad_t_ref, delta_ref, kv_grad_ref, low_ref,
    ) = refs
    width, kv_cols = w_ref.shape
    qk_cols = query_ref.shape[1]
    qk, val = qk_cols // heads, (kv_cols - qk_cols) // heads
    factor = qk**-0.5
    scale = factor * LOG2E
    chunk = 64
    share = pos_ref.shape[1]

    def order(block):
        distance = place_ref[0] ^ block
        return distance % 2 * 2 + distance // 2

    @pl.when((step == 0) & (item == 0))
    def _():
        for i, ref in enumerate((query_out_ref, byte_ref, unit_kv_ref)):
            ref[...] = sums_in[i][...] if first else jnp.zeros_like(ref)

    @pl.when(item == 0)
    def _():
        pos_ref[:, :, :TILE] = jnp.zeros((4, share, TILE), f32)

    for g in range(groups):

        @pl.when((tile * TILE < length) & (item // (pl.num_programs(1) // groups) == g))
        def _():
            copies = (unit_ref, inv_ref, kv_ref, lse_ref, query_ref, query_t_ref, att_grad_ref, att_grad_t_ref, delta_ref)
            for target, ref in zip(copies, made[g]):
                target[...] = ref[0]

    @pl.when(tile * TILE < length)
    def _():
        live = tile * TILE + lax.broadcasted_iota(jnp.int32, (1, TILE), 1) < length
        cross = jnp.zeros((8, TILE), f32)
        for h in range(heads):
            keys = slice(h * qk, (h + 1) * qk)
            values = slice(qk_cols + h * val, qk_cols + (h + 1) * val)
            cols = slice(h * val, (h + 1) * val)
            scores = dot(query_ref[:, keys], kv_ref[keys])
            chances = jnp.exp2(scores * scale - lse_ref[:, h : h + 1])
            chances = jnp.where(live, chances, 0.0)
            weights_grad = dot(att_grad_ref[:, cols], kv_ref[values])
            scores_grad = (chances * (weights_grad - delta_ref[:, h : h + 1])).astype(bf16)
            query_out_ref[item, keys] += dot_nt(kv_ref[keys], scores_grad)
            kv_grad_ref[keys] = (dot(query_t_ref[keys], scores_grad) * factor).astype(bf16)
            kv_grad_ref[values] = dot(att_grad_t_ref[cols], chances.astype(bf16)).astype(bf16)
        for r in range(0, kv_cols, chunk):
            rows = kv_grad_ref[r : r + chunk].astype(f32) * kv_ref[r : r + chunk].astype(f32)
            cross += sum(rows[i : i + 8] for i in range(0, chunk, 8))
        inv = inv_ref[...]
        cross = jnp.sum(cross, axis=0, keepdims=True) * (1.0 / width) * inv
        back = dot(w_ref[...], kv_grad_ref[...])
        for r in range(0, width, chunk):
            rows = slice(r, r + chunk)
            grads = back[rows] * inv - unit_ref[rows].astype(f32) * cross
            pos_ref[order(r // share), r % share : r % share + chunk, :TILE] += grads
            low_ref[rows] = grads.astype(bf16)
        hits = (lax.broadcasted_iota(jnp.int32, (byte_ref.shape[0], TILE), 0) == ids_ref[pl.ds(item, 1)]).astype(bf16)
        byte_ref[...] += dot_nt(hits, low_ref[...])
        unit_kv_ref[...] += dot_nt(kv_grad_ref[...], unit_ref[...])

    if last:

        @pl.when((step == pl.num_programs(0) - 1) & (item == pl.num_programs(1) - 1))
        def _():
            query_out_ref[...] = (query_out_ref[...] * factor).astype(bf16).astype(f32)
            turned_ref[...] = unit_kv_ref[...].T
            gain_grad = jnp.sum(turned_ref[...] * w_rows_ref[...].astype(f32), axis=1, keepdims=True)
            spare = pos_ref.shape[2] - TILE - byte_ref.shape[0]
            byte = jnp.concatenate([byte_ref[...], jnp.zeros((spare, width), f32)], axis=0).T
            byte = jnp.where(lax.broadcasted_iota(jnp.int32, byte.shape, 1) == vocab, gain_grad, byte)
            for block in range(4):
                pos_ref[order(block), :, TILE:] = byte[block * share : (block + 1) * share]
            turned_ref[...] *= gain_ref[:, :1]
            split_blocks(keep_ref, send_ref, turned_ref, place_ref[1])


def back(place, first, count, lengths, ids, made, w_back, w_rows, gains, sums, heads, vocab):
    items, slots = ids.shape
    last = (first + count) * TILE == slots
    groups = len(made)
    size = items // groups
    width, kv_cols = w_back.shape
    lat_count, qk_cols = made[0][4].shape[1:]
    val_cols = kv_cols - qk_cols
    whole = lambda a: pl.BlockSpec(a.shape, lambda t, i, *_: (0,) * a.ndim)
    clip = lambda i, g: jnp.clip(i - g * size, 0, size - 1)
    tiles = lambda g, *s: pl.BlockSpec((1, *s, TILE), lambda t, i, *_: (clip(i, g), 0, t + first))
    each = lambda g, *s: pl.BlockSpec((1, *s), lambda t, i, *_: (clip(i, g), 0, 0))
    shape = lambda s: jax.ShapeDtypeStruct(s, f32)
    kernel = functools.partial(back_kernel, first=first, heads=heads, groups=groups, last=last, vocab=vocab)
    operands = (ids, w_back, w_rows, gains, *sums, *(a for nine in made for a in nine))
    byte_cols = vocab + -vocab % 128
    sums_of = (items, qk_cols, lat_count), (vocab + -vocab % 16, width), (kv_cols, width)
    query_sum, byte_sum, unit_kv = (shape(a) for a in sums_of)
    blocks = lax.axis_size("dp")
    if last:
        assert count == 1
        split = shape((blocks // 2, width // blocks, kv_cols))
        out_shape = [shape((4, width // 4, TILE + byte_cols)), query_sum, split, split]
        out_specs = [whole(a) for a in out_shape]
    else:
        out_shape = [shape((4, width // 4, count * TILE)), query_sum, byte_sum, unit_kv]
        out_specs = [pl.BlockSpec((4, width // 4, TILE), lambda t, i, *_: (0, 0, t)), *(whole(a) for a in out_shape[1:])]
    return pl.pallas_call(
        kernel,
        grid_spec=pltpu.PrefetchScalarGridSpec(
            num_scalar_prefetch=2,
            grid=(count, items),
            in_specs=[
                pl.BlockSpec((items, TILE), lambda t, i, *_: (0, t + first)),
                *(whole(a) for a in (w_back, w_rows, gains, *sums)),
                *(
                    spec
                    for g in range(groups)
                    for spec in (
                        tiles(g, width), tiles(g, 1), tiles(g, kv_cols), each(g, lat_count, 128), each(g, lat_count, qk_cols),
                        each(g, qk_cols, lat_count), each(g, lat_count, val_cols), each(g, val_cols, lat_count), each(g, lat_count, 128),
                    )
                ),
            ],
            out_specs=out_specs,
            scratch_shapes=[
                pltpu.VMEM((width, TILE), bf16), pltpu.VMEM((1, TILE), f32), pltpu.VMEM((kv_cols, TILE), bf16),
                pltpu.VMEM((lat_count, 128), f32), pltpu.VMEM((lat_count, qk_cols), bf16),
                pltpu.VMEM((qk_cols, lat_count), bf16), pltpu.VMEM((lat_count, val_cols), bf16),
                pltpu.VMEM((val_cols, lat_count), bf16), pltpu.VMEM((lat_count, 128), f32),
                pltpu.VMEM((kv_cols, TILE), bf16), pltpu.VMEM((width, TILE), bf16),
                *([pltpu.VMEM(s, f32) for s in (*sums_of[1:], (width, kv_cols))] if last else []),
            ],
        ),
        out_shape=out_shape,
        compiler_params=limits(58),
        cost_estimate=cost(12 * count),
        name="back",
    )(lengths, place, *operands)


def assemble_kernel(place_ref, own_ref, *refs):
    *far_refs, out_ref = refs
    side, corner = place_ref[0] // 2, place_ref[1] % 4
    rows = own_ref.shape[0]
    quarter = rows // 4

    def put(start, ref):
        out_ref[pl.ds(pl.multiple_of(start, 16), ref.shape[0])] = ref[...].astype(bf16)

    put(side * rows, own_ref)
    for step, ref in enumerate(far_refs):
        put((1 - side) * rows + (corner ^ step) * quarter, ref)


def assemble(place, own, far, tokens=()):
    rows, width = own.shape
    operands = (own, *far)
    return pl.pallas_call(
        ignoring(assemble_kernel, 1 + len(operands), len(tokens)),
        in_specs=[
            pl.BlockSpec(memory_space=pltpu.SMEM), *([pl.BlockSpec(memory_space=pltpu.VMEM)] * len(operands)),
            *([ANYWHERE] * len(tokens)),
        ],
        out_specs=pl.BlockSpec(memory_space=pltpu.VMEM),
        out_shape=jax.ShapeDtypeStruct((2 * rows, width), bf16),
        compiler_params=limits(40),
        cost_estimate=cost(2),
        name="assemble",
    )(place, *operands, *tokens)


def packed(block):
    rows, cols = block.shape
    parts = [block[:, c : c + 128] for c in range(0, cols - 127, 128)]
    if cols % 128:
        last = block[:, cols - 64 :]
        parts.append(jnp.concatenate([last[: rows // 2], last[rows // 2 :]], axis=1))
    return jnp.concatenate(parts, axis=0)


def unpacked(block, cols):
    rows = block.shape[0] * 128 // cols
    count = cols // 128
    parts = [block[c * rows : (c + 1) * rows] for c in range(count)]
    if cols % 128:
        last = block[count * rows :]
        parts.append(jnp.concatenate([last[:, :64], last[:, 64:]], axis=0))
    return jnp.concatenate(parts, axis=1)


def reversed_bits(count):
    order = [0]
    while len(order) < count:
        order = [2 * o for o in order] + [2 * o + 1 for o in order]
    return order


def split_blocks(keep_ref, send_ref, total, dp_place, shape=lambda block: block):
    count = keep_ref.shape[0]
    size = total.shape[0] // count // 2
    for ref, flip in ((keep_ref, 0), (send_ref, 1)):
        for j, distance in enumerate(reversed_bits(count)):
            target = dp_place ^ (2 * distance + flip)
            ref[j] = shape(total[pl.ds(pl.multiple_of(target * size, 8), size)])


def put_blocks(keep_ref, send_ref, total, dp_place):
    split_blocks(keep_ref, send_ref, total, dp_place, packed)


def call(kernel, grid, inputs, outputs, scratch=(), tokens=(), name=None, time=1, limit=56):
    whole = lambda a: (a, a.shape, lambda *_: (0,) * a.ndim)
    inputs = [i if isinstance(i, tuple) else whole(i) for i in inputs]
    specs = [pl.BlockSpec(block, index) if block else pl.BlockSpec(memory_space=pltpu.SMEM) for _, block, index in inputs]
    return pl.pallas_call(
        ignoring(kernel, len(inputs), len(tokens)),
        grid=grid,
        in_specs=[*specs, *([ANYWHERE] * len(tokens))],
        out_specs=[pl.BlockSpec(block, index) for _, _, block, index in outputs],
        out_shape=[jax.ShapeDtypeStruct(shape, kind) for shape, kind, _, _ in outputs],
        scratch_shapes=list(scratch),
        compiler_params=limits(limit),
        cost_estimate=cost(time),
        name=name,
    )(*(a for a, _, _ in inputs), *tokens)


def scalars(place):
    return place, None, None


def each(array):
    return array, (1, *array.shape[1:]), lambda i: (i, *(0,) * (array.ndim - 1))


def part(array, first):
    return array, (1, *array.shape[1:]), lambda i: (first + i, *(0,) * (array.ndim - 1))


def among(array, group, size):
    return array, (1, *array.shape[1:]), lambda i: (jnp.clip(i - group * size, 0, size - 1), 0, 0)


def new(shape, kind=f32):
    return shape, kind, (1, *shape[1:]), lambda i: (i, *(0,) * (len(shape) - 1))


def kept(shape, kind=f32):
    return shape, kind, shape, lambda i: (0,) * len(shape)


def mix(place, own, far, w_out, tokens=()):
    count, rows, lat_count = own.shape

    def kernel(place_ref, own_ref, far_ref, w_ref, out_ref, att_ref):
        side = place_ref[0] // 2
        for ref, at in ((own_ref, side), (far_ref, 1 - side)):
            att_ref[pl.ds(pl.multiple_of(at * rows, 16), rows)] = ref[0].astype(bf16)
        out_ref[0] = dot_tn(att_ref[...], w_ref[...])

    return call(
        kernel, (count,), [scalars(place), each(own), each(far), w_out], [new((count, lat_count, w_out.shape[1]))],
        [pltpu.VMEM((2 * rows, lat_count), bf16)], tokens, "mix", 3, 14,
    )[0]


def feed(place, first, latents, out_grad, mixed, crossed, gain, w_one, w_two, tokens=()):
    count, lat_count, width = mixed.shape
    rows = w_one.shape[0] // 2

    def kernel(
        place_ref, lat_ref, grad_ref, mixed_ref, crossed_ref, gain_ref, w_one_ref, w_two_ref,
        hidden_ref, normed_ref, activated_ref, share_ref, own_ref, up_own_ref, parts_ref,
    ):
        side = place_ref[0] // 2

        def own(tensor):
            parts_ref[0] = tensor[:, :rows]
            parts_ref[1] = tensor[:, rows:]
            return parts_ref[side]

        hidden = lat_ref[0].astype(f32) + (mixed_ref[0] + crossed_ref[0])
        hidden_ref[0] = hidden
        unit, _ = row_norm(hidden)
        normed = (unit * gain_ref[...]).astype(bf16)
        normed_ref[0] = normed
        up = dot_nt(normed, w_one_ref[...])
        below = 0.5 * (1.0 + lax.erf(up * 0.5**0.5))
        activated = (up * below).astype(bf16)
        activated_ref[0] = activated
        own_ref[0] = own(activated)
        slope = below + up * (jnp.exp(-0.5 * up * up) * 0.3989422804014327)
        up_grad = (dot_nt(grad_ref[0], w_two_ref[...]) * slope).astype(bf16)
        up_own_ref[0] = own(up_grad)
        share_ref[0] = dot(up_grad, w_one_ref[...])

    full, low = (count, lat_count, width), (count, lat_count, rows)
    return call(
        kernel, (count,),
        [scalars(place), part(latents, first), part(out_grad, first), each(mixed), each(crossed), gain, w_one, w_two],
        [new(full), new(full, bf16), new((count, lat_count, 2 * rows), bf16), new(full), new(low, bf16), new(low, bf16)],
        [pltpu.VMEM((2, lat_count, rows), bf16)], tokens, "feed", 6, 36,
    )


def split_grad(blocks, width, rows):
    return kept((blocks // 2, width // blocks * rows // 128, 128))


def feed_weights(place, out_grad, fed, blocks, tokens=()):
    items, lat_count, width = out_grad.shape
    groups = len(fed)
    size = items // groups
    rows = fed[0][1].shape[2]

    def kernel(place_ref, grad_ref, *refs):
        item = pl.program_id(0)
        keep_one, send_one, keep_two, send_two, one_sum, two_sum = refs[3 * groups :]

        @pl.when(item == 0)
        def _():
            one_sum[...] = jnp.zeros_like(one_sum)
            two_sum[...] = jnp.zeros_like(two_sum)

        for g in range(groups):

            @pl.when(item // size == g)
            def _():
                normed_ref, activated_ref, up_grad_ref = refs[3 * g : 3 * g + 3]
                two_sum[...] += dot_tn(grad_ref[0], activated_ref[0])
                one_sum[...] += dot_tn(normed_ref[0], up_grad_ref[0])

        @pl.when(item == items - 1)
        def _():
            put_blocks(keep_two, send_two, two_sum, place_ref[1])
            put_blocks(keep_one, send_one, one_sum, place_ref[1])

    return call(
        kernel, (items,), [scalars(place), each(out_grad), *(among(a, g, size) for g in range(groups) for a in fed[g])],
        [split_grad(blocks, width, rows)] * 4, [pltpu.VMEM((width, rows), f32)] * 2, tokens, "feed_weights", 6, 26,
    )


def unmix(place, first, out_grad, hidden, share, crossed, gain, w_out, att, before, blocks, heads, tokens=()):
    count, lat_count, width = hidden.shape
    rows = w_out.shape[0]
    val = rows // heads

    def kernel(place_ref, grad_ref, hidden_ref, share_ref, crossed_ref, gain_ref, w_ref, att_ref, *refs):
        item = pl.program_id(0)
        sums_in, refs = refs[: len(before)], refs[len(before) :]
        hidden_grad_ref, att_grad_ref, att_grad_t_ref, delta_ref, gain_grad_ref, sum_ref, *split = refs

        @pl.when(item == 0)
        def _():
            for i, ref in enumerate((gain_grad_ref, sum_ref)):
                ref[...] = sums_in[i][...] if before else jnp.zeros_like(ref)

        unit, inv = row_norm(hidden_ref[0])
        norm_grad = share_ref[0] + crossed_ref[0]
        gain_grad_ref[...] += jnp.sum(norm_grad * unit, axis=0, keepdims=True)
        hidden_grad = grad_ref[0].astype(f32) + row_norm_back(norm_grad, unit, inv, gain_ref[...])
        hidden_grad_ref[0] = hidden_grad
        mixed_grad = hidden_grad.astype(bf16)
        att = att_ref[0].T
        sum_ref[...] += dot_tn(mixed_grad, att.astype(bf16))
        att_grad = dot_nt(mixed_grad, w_ref[...])
        att_grad_ref[0] = att_grad.astype(bf16)
        att_grad_t_ref[0] = att_grad.T.astype(bf16)
        product = att_grad.astype(bf16).astype(f32) * att
        lane = lax.broadcasted_iota(jnp.int32, delta_ref.shape[1:], 1)
        delta = jnp.zeros(delta_ref.shape[1:], f32)
        for h in range(heads):
            delta = jnp.where(lane == h, jnp.sum(product[:, h * val : (h + 1) * val], axis=1, keepdims=True), delta)
        delta_ref[0] = delta
        if split:

            @pl.when(item == count - 1)
            def _():
                put_blocks(*split, sum_ref, place_ref[1])

    full = (count, lat_count, width)
    return call(
        kernel, (count,),
        [
            scalars(place), part(out_grad, first), each(hidden), each(share), each(crossed), gain, w_out, each(att), *before,
        ],
        [
            new(full), new((count, lat_count, rows), bf16), new((count, rows, lat_count), bf16), new((count, lat_count, 128)),
            kept((1, width)), kept((width, rows)), *([split_grad(blocks, width, rows)] * 2 if first else []),
        ],
        [], tokens, "unmix", 6, 32,
    )


def branch(activated, w_two, tokens=()):
    count, lat_count, _ = activated[0].shape
    groups = len(activated)
    width = w_two.shape[1]

    def kernel(*refs):
        *group_refs, w_ref, out_ref = refs
        for g in range(groups):

            @pl.when(pl.program_id(0) // count == g)
            def _():
                out_ref[0] = dot(group_refs[g][0], w_ref[...])

    return call(
        kernel, (count * groups,), [*(among(a, g, count) for g, a in enumerate(activated)), w_two],
        [new((count * groups, lat_count, width))], [], tokens, "branch", 4, 20,
    )[0]


def block_output(hidden, share, crossed, tokens=()):
    count = hidden[0].shape[0]
    groups = len(hidden)

    def kernel(*refs):
        *hidden_refs, share_ref, crossed_ref, out_ref = refs
        for g in range(groups):

            @pl.when(pl.program_id(0) // count == g)
            def _():
                out_ref[0] = (hidden_refs[g][0] + (share_ref[0] + crossed_ref[0])).astype(bf16)

    return call(
        kernel, (count * groups,), [*(among(a, g, count) for g, a in enumerate(hidden)), each(share), each(crossed)],
        [new(share.shape, bf16)], [], tokens, "block_output", 4, 20,
    )[0]


def latent(place, query_grad, latents, hidden_grad, gain, w_query, blocks):
    items, lat_count, width = latents.shape
    rows = w_query[0].shape[0]
    groups = len(hidden_grad)
    size = items // groups

    def kernel(
        place_ref, own_ref, core_ref, far_ref, far_core_ref, lat_ref, gain_ref, w_own, w_core, w_far, w_far_core, *refs,
    ):
        grad_ref, gain_grad_ref, keep_ref, send_ref, w_ref, parts_ref, sum_ref, turned_ref = refs[groups:]
        item = pl.program_id(0)
        place = place_ref[0]

        def put(target, refs, value):
            for step, ref in enumerate(refs):
                target[pl.ds(pl.multiple_of((place ^ step) * rows, 16), rows)] = value(ref).astype(bf16)

        @pl.when(item == 0)
        def _():
            put(w_ref, (w_own, w_core, w_far, w_far_core), lambda ref: ref[...])
            gain_grad_ref[...] = jnp.zeros_like(gain_grad_ref)
            sum_ref[...] = jnp.zeros_like(sum_ref)

        put(parts_ref, (own_ref, core_ref, far_ref, far_core_ref), lambda ref: ref[0])
        unit, inv = row_norm(lat_ref[0].astype(f32))
        gain = gain_ref[...]
        sum_ref[...] += dot(own_ref[0].astype(bf16), (unit * gain).astype(bf16))
        norm_grad = dot_tn(parts_ref[...], w_ref[...])
        gain_grad_ref[...] += jnp.sum(norm_grad * unit, axis=0, keepdims=True)
        for g in range(groups):

            @pl.when(item // size == g)
            def _():
                grad_ref[0] = refs[g][0] + row_norm_back(norm_grad, unit, inv, gain)

        @pl.when(item == items - 1)
        def _():
            turned_ref[...] = sum_ref[...].T
            put_blocks(keep_ref, send_ref, turned_ref, place_ref[1])

    return call(
        kernel, (items,),
        [
            scalars(place), *(each(q) for q in query_grad), each(latents), gain, *w_query,
            *(among(a, g, size) for g, a in enumerate(hidden_grad)),
        ],
        [new(latents.shape), kept((1, width)), *([split_grad(blocks, width, rows)] * 2)],
        [
            pltpu.VMEM((4 * rows, width), bf16), pltpu.VMEM((4 * rows, lat_count), bf16), pltpu.VMEM((rows, width), f32),
            pltpu.VMEM((width, rows), f32),
        ], (), "latent", 16, 36,
    )


def at(array, index):
    return array, (1, *array.shape[1:]), lambda *_: (index, *(0,) * (array.ndim - 1))


def pos_blocks(columns, slots):
    return [
        (packed(columns[:, c : c + slots]), packed(columns[:, c + slots : c + 2 * slots]))
        for c in range(0, columns.shape[1], 2 * slots)
    ]


def first_sums(place, pos, near, far, slots):
    share, cols = far.shape

    def kernel(place_ref, pos_ref, near_ref, far_ref, keep_ref, send_ref):
        side = place_ref[1] % 2
        for i, (low, high) in enumerate(pos_blocks(pos_ref[0] + near_ref[0] + far_ref[...], slots)):
            keep_ref[i] = jnp.where(side == 0, low, high)
            send_ref[i] = jnp.where(side == 0, high, low)

    split = kept((cols // slots // 2, share * slots // 128, 128))
    return call(
        kernel, (1,), [scalars(place), at(pos, 0), at(near, 2), far], [split, split], [], (), "first_sums", 3, 40
    )


def second_sums(place, tiles, gain_lat, gain_mlp, slots, vocab):
    share, cols = tiles[-1][2].shape
    own = gain_lat.shape[1] // 4
    count = TILE // slots // 2 * len(tiles)
    rows = share * slots // 128
    byte_rows = share // 2 * (cols - TILE) // 128
    first = vocab + 1 + -(vocab + 1) % 8

    def kernel(place_ref, *refs):
        tile_refs = [refs[3 * t : 3 * t + 3] for t in range(len(tiles))]
        lat_ref, mlp_ref, keep_ref, send_ref, byte_ref, gains_ref = refs[3 * len(tiles) :]
        side = place_ref[1] % 2
        blocks = []
        for pos_ref, near_ref, far_ref in tile_refs:
            mine = pos_ref[0] + near_ref[0] + far_ref[...]
            blocks += pos_blocks(mine[:, :TILE], slots)
        byte_ref[...] = mine[:, TILE:]
        gains = jnp.concatenate([lat_ref[...], mlp_ref[...], jnp.zeros((6, lat_ref.shape[1]), f32)], axis=0)
        gains_ref[...] = gains.T
        gains = gains_ref[pl.ds(pl.multiple_of(place_ref[0] * own, 8), own)]
        byte_ref[:, first : first + 8] = gains[:share]
        byte_ref[: own - share, first + 8 : first + 16] = gains[share:]
        blocks.append((packed(byte_ref[: share // 2]), packed(byte_ref[share // 2 :])))
        start = 0
        for low, high in blocks:
            stretch = slice(start, start + low.shape[0])
            keep_ref[stretch] = jnp.where(side == 0, low, high)
            send_ref[stretch] = jnp.where(side == 0, high, low)
            start += low.shape[0]

    split = kept((count * rows + byte_rows, 128))
    return call(
        kernel, (1,),
        [scalars(place), *(a for pos, near, far in tiles for a in (at(pos, 0), at(near, 2), far)), gain_lat, gain_mlp],
        [split, split], [pltpu.VMEM((share, cols - TILE), f32), pltpu.VMEM((gain_lat.shape[1], 8), f32)], (), "second_sums", 3,
        40,
    )


def third_sums(place, keep_ab, cross_ab, keep, cross, byte_rows, half):
    before, rows, _ = keep_ab.shape
    last = (keep.shape[0] - byte_rows) // rows
    count = before + last
    size, part = byte_rows // count, half // count

    def kernel(place_ref, keep_ab_ref, cross_ab_ref, keep_ref, cross_ref, pos_keep_ref, pos_send_ref, byte_ref):
        ring = place_ref[1] // 2
        sums = [keep_ab_ref[i] + cross_ab_ref[i] for i in range(before)]
        total = keep_ref[...] + cross_ref[...]
        sums += [total[i * rows : (i + 1) * rows] for i in range(last)]
        for i in range(count // 2):
            pos_keep_ref[i] = jnp.where(ring % 2 == 0, sums[2 * i], sums[2 * i + 1])
            pos_send_ref[i] = jnp.where(ring % 2 == 0, sums[2 * i + 1], sums[2 * i])
        total = total[last * rows :]
        for j in range(count):
            distance = ring ^ j
            place, bits = 0, count.bit_length() - 1
            for b in range(bits):
                place += (distance >> b & 1) << (bits - 1 - b)
            byte_ref[place] = jnp.concatenate(
                [total[c + j * part : c + (j + 1) * part] for c in range(0, byte_rows, half)], axis=0
            )

    split = kept((count // 2, rows, 128))
    return call(
        kernel, (1,), [scalars(place), keep_ab, cross_ab, keep, cross], [split, split, kept((count, size, 128))], [], (),
        "third_sums", 3, 40,
    )


def next_sums(place, keep, cross, bit, parts=(), tokens=()):
    count, rows, _ = keep.shape

    def kernel(place_ref, *refs):
        part_refs, (keep_ref, cross_ref, pos_keep_ref, pos_send_ref, *sum_ref) = refs[: len(parts)], refs[len(parts) :]
        mine = place_ref[1] // bit % 2
        sums = [keep_ref[i] + cross_ref[i] for i in range(count)]
        for i in range(count // 2):
            pos_keep_ref[i] = jnp.where(mine == 0, sums[2 * i], sums[2 * i + 1])
            pos_send_ref[i] = jnp.where(mine == 0, sums[2 * i + 1], sums[2 * i])
        if parts:
            sum_ref[0][...] = sum(ref[0] if len(ref.shape) == 3 else ref[...] for ref in part_refs)

    split = kept((count // 2, rows, 128))
    return call(
        kernel, (1,), [scalars(place), *parts, keep, cross], [split, split, *([kept(parts[1].shape)] if parts else [])], [],
        tokens, "next_sums", 2, 40,
    )


def last_sums(place, keep, cross, parts, share):
    count = len(parts)
    size = parts[0].shape[0]
    rows = keep.shape[1]
    half = share // 2
    part = half // count
    lanes = size // part

    def kernel(place_ref, *refs):
        part_refs, (keep_ref, cross_ref, pos_ref, byte_ref, held_ref) = refs[:count], refs[count:]
        pos_ref[...] = unpacked(keep_ref[0] + cross_ref[0], pos_ref.shape[1])
        for distance, ref in enumerate(part_refs):
            held_ref[place_ref[1] // 2 ^ distance] = ref[...]
        byte_ref[...] = jnp.concatenate(
            [held_ref[j, c * part : (c + 1) * part] for c in range(lanes) for j in range(count)], axis=0
        )

    return call(
        kernel, (1,), [scalars(place), *parts, keep, cross], [kept((share, rows * 128 // share)), kept((count * size, 128))],
        [pltpu.VMEM((count, size, 128), f32)], (), "last_sums", 2, 40,
    )


def byte_sums(place, own, other, share, vocab, gain_cols):
    cols = own.shape[0] * 128 // (share // 2)
    first = vocab + 1 + -(vocab + 1) % 8

    def kernel(place_ref, own_ref, other_ref, table_ref, gain_ref, gains_ref):
        side = place_ref[1] % 2
        low = jnp.where(side == 0, own_ref[...], other_ref[...])
        high = jnp.where(side == 0, other_ref[...], own_ref[...])
        turned = jnp.concatenate([unpacked(low, cols), unpacked(high, cols)], axis=0).T
        table_ref[...] = turned[:vocab]
        gain_ref[...] = turned[vocab : vocab + 1]
        gains_ref[...] = jnp.concatenate([turned[first : first + 2], turned[first + 8 : first + 10, : gain_cols - share]], axis=1)

    return call(
        kernel, (1,), [scalars(place), own, other], [kept((vocab, share)), kept((1, share)), kept((2, gain_cols))], [], (),
        "byte_sums", 2, 40,
    )


def finish(sums, cols, tokens=()):
    def kernel(*refs):
        for i, out_ref in enumerate(refs[2 * len(sums) :]):
            out_ref[...] = unpacked(refs[2 * i][0] + refs[2 * i + 1][0], cols)

    rows = sums[0][0].shape[1] * 128 // cols
    return call(
        kernel, (1,), [at(a, 0) for pair in sums for a in pair], [kept((rows, cols))] * len(sums), [], tokens, "finish", 3, 40
    )


def swap(tensor, axis, bit):
    return lax.ppermute(tensor, axis, [(i, i ^ bit) for i in range(lax.axis_size(axis))])


def stage(always, work):
    shapes = jax.eval_shape(work)
    return lax.cond(always, work, lambda: jax.tree.map(lambda s: jnp.zeros(s.shape, s.dtype), shapes))


def body(
    byte_ids, lengths, latents, byte_table, pos_table, gain_in, gain_lat, gain_mlp,
    w_query, w_key, w_value, w_out, w_one, w_two, out_grad,
):
    items, slots = byte_ids.shape
    vocab, width = byte_table.shape
    lat_count, lat_width = latents.shape[1:]
    mp, dp = lax.axis_size("mp"), lax.axis_size("dp")
    mp_place, dp_place = lax.axis_index("mp"), lax.axis_index("dp")
    place = jnp.stack([mp_place, dp_place]).astype(jnp.int32)
    heads = HEADS // mp
    qk_cols = w_query.shape[1]
    val_cols = w_value.shape[1]
    corner, side = dp_place % 4, dp_place % 2

    shards = [w_out, w_one.T, w_two]
    quarter = val_cols // 4
    always = lengths[0] > 0
    over_y = lambda w: swap(lax.dynamic_slice_in_dim(w, corner * quarter, quarter, 0).astype(f32), "mp", 2)
    over_x, over_z, over_both = (lambda a, bits=bits: swap(a, "dp", bits) for bits in (1, 2, 3))
    core = lambda a: swap(a, "mp", 1)
    half = items // 2

    def first_stage():
        weights = (gain_in[None], w_key.T, w_value.T, *shards[1:])
        return over_y(shards[0]), tables_of(place, byte_table, pos_table, *weights)

    out, (*tables, w_back, w_rows, one, two) = stage(always, first_stage)

    def front_of(first):
        return front(first, half, lengths, byte_ids, *tables, latents, gain_lat[None], w_query.T, heads)

    def second_stage():
        return front_of(0), [over_x(out), over_z(out)], over_both(out), swap(one, "mp", 2), swap(two, "mp", 2)

    (*made_a, att_a), crossed_out, last_out, one, two = stage(always, second_stage)

    def third_stage():
        return front_of(half), [over_x(one), over_z(one), over_both(one)], over_both(two), swap(att_a, "mp", 2)

    (*made_b, att_b), crossed_one, last_two, far_a = stage(always, third_stage)

    def fourth_stage():
        w_out_whole = assemble(place, shards[0], [out, *crossed_out, last_out])
        w_one_whole = assemble(place, shards[1], [one, *crossed_one], [w_out_whole])
        mixed_a = mix(place, att_a, far_a, w_out_whole, [w_one_whole])
        return w_out_whole, w_one_whole, mixed_a, [over_x(two), over_z(two)], swap(att_b, "mp", 2)

    w_out_whole, w_one_whole, mixed_a, crossed_two, far_b = stage(always, fourth_stage)
    w_two_whole = assemble(place, shards[2], [two, *crossed_two, last_two])
    mixed_b = mix(place, att_b, far_b, w_out_whole, [w_two_whole])
    gain = gain_mlp[None]
    weights = (gain, w_one_whole, w_two_whole)
    hidden_a, normed_a, activated_a, share_a, act_a, up_a = feed(
        place, 0, latents, out_grad, mixed_a, core(mixed_a), *weights, [mixed_b]
    )
    hidden_b, normed_b, activated_b, share_b, act_b, up_b = feed(
        place, half, latents, out_grad, mixed_b, core(mixed_b), *weights, [share_a]
    )
    keep_one, send_one, keep_two, send_two = feed_weights(
        place, out_grad, [(normed_a, act_a, up_a), (normed_b, act_b, up_b)], dp
    )
    w_query_own = w_query.T.astype(f32)
    crossed_a, crossed_b = core(share_a), core(share_b)

    def unmix_stage():
        grads_a = unmix(place, 0, out_grad, hidden_a, share_a, crossed_a, gain, w_out, att_a, [], dp, heads)
        grads_b = unmix(place, half, out_grad, hidden_b, share_b, crossed_b, gain, w_out, att_b, grads_a[4:], dp, heads)
        w_query_parts = core(w_query_own), swap(w_query_own, "mp", 2)
        share_out = branch((activated_a, activated_b), w_two_whole)
        return grads_a[:4], grads_b[:5], grads_b[6:], swap(send_two, "dp", 1), w_query_parts, share_out

    unmixed_a, unmixed_b, (keep_out, send_out), cross_two, w_query_parts, share_out = stage(always, unmix_stage)
    (hidden_grad_a, *grads_a), (hidden_grad_b, *grads_b, gain_mlp_grad) = unmixed_a, unmixed_b
    made = [(*made_a, *grads_a), (*made_b, *grads_b)]
    byte_cols = vocab + -vocab % 128
    bits = [1 << i for i in range(1, dp.bit_length() - 1)]

    def back_of(first, count, sums):
        return back(place, first, count, lengths, byte_ids, made, w_back, w_rows, tables[3], sums, heads, vocab)

    def halve(blocks, bits):
        for bit in bits:
            count = blocks.shape[0] // 2
            blocks = blocks[:count] + swap(blocks[count:], "dp", bit)
        return blocks

    two_blocks = keep_two + cross_two

    def back_stage_a():
        transfers = swap(send_one, "dp", 1), halve(two_blocks, bits[:1]), core(w_query_parts[1]), core(share_out)
        return back_of(0, 2, []), transfers

    (pos_a, *sums), (cross_one, two_blocks, w_query_last, crossed_out) = stage(always, back_stage_a)
    w_query_all = [w_query_own, *w_query_parts, w_query_last]

    def last_pair(blocks):
        return blocks[:1], swap(blocks[1:], "dp", bits[-1])

    def back_stage_b():
        near_a = core(pos_a)
        two, one = halve(two_blocks, bits[1:-1]), halve(keep_one + cross_one, bits[:1])
        two = last_pair(two)
        cross_out = swap(send_out, "dp", 1)
        return back_of(2, 1, sums), (near_a, two, one, cross_out), pos_a[1] + near_a[3]

    (pos_b, *sums), (near_a, two_pair, one_blocks, cross_out), send_a = stage(always, back_stage_b)

    def back_stage_c():
        near_b = core(pos_b)
        one, out = last_pair(halve(one_blocks, bits[1:-1])), halve(keep_out + cross_out, bits[:1])
        far_a = swap(send_a, "mp", 2)
        return back_of(3, 1, sums), far_a, near_b, one, out

    (pos_c, query_own, keep_kv, send_kv), far_a, near_b, one_pair, out_blocks = stage(always, back_stage_c)
    slot_share, share = slots // dp, width // mp

    def tail_stage_a():
        near_c = core(pos_c)
        out = last_pair(halve(out_blocks, bits[1:-1]))
        cross_kv, query_far = swap(send_kv, "dp", 1), swap(query_own, "mp", 2)
        far_b = swap(pos_b[1] + near_b[3], "mp", 2)
        latents_out = block_output((hidden_a, hidden_b), share_out, crossed_out)
        transfers = near_c, out, cross_kv, query_far, far_b
        return latents_out, first_sums(place, pos_a, near_a, far_a, slot_share), transfers, pos_c[1] + near_c[3]

    latents_out, (keep_a, send_x), transfers, send_c = stage(always, tail_stage_a)
    near_c, out_pair, cross_kv, query_far, far_b = transfers

    def tail_stage_b():
        query_all = [query_own, core(query_own), query_far, core(query_far)]
        kv_blocks = halve(keep_kv + cross_kv, bits[:1])
        cross_a = swap(send_x, "dp", 1)
        far_c = swap(send_c, "mp", 2)
        latent_out = latent(
            place, query_all, latents, (hidden_grad_a, hidden_grad_b), gain_lat[None], w_query_all, dp
        )
        tiles = [(pos_b, near_b, far_b), (pos_c, near_c, far_c)]
        return latent_out, cross_a, kv_blocks, second_sums(place, tiles, latent_out[1], gain_mlp_grad, slot_share, vocab)

    latent_out, cross_a, kv_blocks, (keep_c, send_c) = stage(always, tail_stage_b)
    latent_grad, gain_lat_grad, keep_query, send_query = latent_out
    byte_rows = share // 2 * byte_cols // 128
    cross_c, cross_query = swap(send_c, "dp", 1), swap(send_query, "dp", 1)
    byte_rows = share // 2 * byte_cols // 128
    pos_keep, pos_send, byte_blocks = third_sums(place, keep_a, cross_a, keep_c, cross_c, byte_rows, share // 2)
    cross = swap(pos_send, "dp", bits[0])
    kv_sum = halve(kv_blocks, bits[1:])[0]
    two_sum, one_sum, out_sum = finish([two_pair, one_pair, out_pair], val_cols, [pos_keep])
    query_blocks = halve(keep_query + cross_query, bits[:1])
    byte_parts = [byte_blocks[:1]] + [swap(byte_blocks[j], "dp", 2 * d) for j, d in enumerate(reversed_bits(dp // 2)) if d]
    for k, bit in enumerate(bits[1:]):
        pos_keep, pos_send, *byte_own = next_sums(place, pos_keep, cross, bit, [] if k else byte_parts, [two_sum])
        byte_sum = byte_sum if k else byte_own[0]
        cross = swap(pos_send, "dp", bit)
    query_sum = halve(query_blocks, bits[1:])[0]
    byte_parts = [byte_sum] + [swap(byte_sum, "dp", 2 * d) for d in range(1, dp // 2)]
    pos_sum, byte_half = last_sums(place, pos_keep, cross, byte_parts, share)
    byte_grad, gain_in_grad, gains = byte_sums(place, byte_half, swap(byte_half, "dp", 1), share, vocab, val_cols)
    return (
        latents_out, latent_grad, byte_grad, pos_sum.T, gain_in_grad[0], gains[0], gains[1],
        unpacked(query_sum, qk_cols), kv_sum[:, :qk_cols], kv_sum[:, qk_cols:], out_sum.T, one_sum, two_sum.T,
    )


def solution(mesh):
    return jax.shard_map(
        body,
        mesh=mesh,
        in_specs=(
            P("dp", None),
            P("dp"),
            P("dp", None, None),
            P(),
            P(),
            P(),
            P(),
            P(),
            P(None, "mp"),
            P(None, "mp"),
            P(None, "mp"),
            P("mp", None),
            P(None, "mp"),
            P("mp", None),
            P("dp", None, None),
        ),
        out_specs=(
            P("dp", None, None),
            P("dp", None, None),
            P(None, "mp"),
            P("dp", "mp"),
            P("mp"),
            P("mp"),
            P("mp"),
            P("dp", "mp"),
            P("dp", "mp"),
            P("dp", "mp"),
            P("mp", "dp"),
            P("dp", "mp"),
            P("mp", "dp"),
        ),
        check_vma=False,
    )
```

```python
import functools

import jax
import jax.numpy as jnp
from jax import lax
from jax.experimental import pallas as pl
from jax.experimental.pallas import tpu as pltpu
from jax.sharding import PartitionSpec as P

HEADS = 8
EPSILON = 1e-05
MASKED = -1e30
LOG2E = 1.4426950408889634
TILE = 512
COST = 11500000000
f32, bf16 = jnp.float32, jnp.bfloat16
ANYWHERE = pl.BlockSpec(memory_space=pl.ANY)


def dot(left, right):
    return jnp.dot(left, right, preferred_element_type=f32)


def dot_nt(left, right):
    return lax.dot_general(left, right, (((1,), (1,)), ((), ())), preferred_element_type=f32)


def dot_tn(left, right):
    return lax.dot_general(left, right, (((0,), (0,)), ((), ())), preferred_element_type=f32)


def cost(microseconds):
    return pl.CostEstimate(flops=microseconds * COST, bytes_accessed=0, transcendentals=0)


def limits(mebibytes):
    return pltpu.CompilerParams(vmem_limit_bytes=mebibytes * 2**20)


def ignoring(kernel, start, count):
    def inner(*refs):
        return kernel(*refs[:start], *refs[start + count :])

    return inner


def row_norm(rows):
    centered = rows - jnp.mean(rows, axis=-1, keepdims=True)
    inv_std = lax.rsqrt(jnp.mean(centered * centered, axis=-1, keepdims=True) + EPSILON)
    return centered * inv_std, inv_std


def row_norm_back(upstream, unit, inv, gain):
    scaled = upstream * gain
    row_mean = jnp.mean(scaled, axis=-1, keepdims=True)
    row_cross = jnp.mean(scaled * unit, axis=-1, keepdims=True)
    return inv * (scaled - row_mean - unit * row_cross)


def front_kernel(
    lengths, ids_ref, table_ref, pos_ref, pos_mean_ref, gain_ref, w_kv_ref, lat_ref, gain_lat_ref, w_query_ref,
    unit_ref, inv_ref, kv_ref, lse_ref, query_ref, query_t_ref, att_ref,
    x_ref, normed_ref, scores_ref, total_ref, peak_ref,
    *, first, width, heads,
):
    step = pl.program_id(1)
    item = first + pl.program_id(0)
    length = lengths[item]
    lat_count = lat_ref.shape[1]
    qk_cols = w_query_ref.shape[0]
    qk = qk_cols // heads
    val = (w_kv_ref.shape[0] - qk_cols) // heads
    scale = qk**-0.5 * LOG2E
    chunk = 64

    @pl.when(step == 0)
    def _():
        unit_lat, _ = row_norm(lat_ref[0].astype(f32))
        queries = dot_nt((unit_lat * gain_lat_ref[...]).astype(bf16), w_query_ref[...])
        query_ref[0] = queries.astype(bf16)
        query_t_ref[0] = queries.T.astype(bf16)
        peak_ref[...] = jnp.full_like(peak_ref, MASKED)

    @pl.when(step * TILE < length)
    def _():
        cols = pl.ds(pl.multiple_of(step * TILE, TILE), TILE)
        hits = (lax.broadcasted_iota(jnp.int32, (table_ref.shape[1], TILE), 0) == ids_ref[pl.ds(item, 1), cols]).astype(bf16)
        x_ref[...] = dot(table_ref[...], hits)
        mean = x_ref[width : width + 1] + x_ref[width + 1 : width + 2] + x_ref[width + 2 : width + 3]
        mean = mean + pos_mean_ref[:, cols]
        square = jnp.zeros((8, TILE), f32)
        for r in range(0, width, chunk):
            rows = x_ref[r : r + chunk] + pos_ref[r : r + chunk].astype(f32) - mean
            x_ref[r : r + chunk] = rows
            rows = rows * rows
            square += sum(rows[i : i + 8] for i in range(0, chunk, 8))
        inv = lax.rsqrt(jnp.sum(square, axis=0, keepdims=True) * (1.0 / width) + EPSILON)
        inv_ref[0, :, cols] = inv
        for r in range(0, width, chunk):
            unit = x_ref[r : r + chunk] * inv
            unit_ref[0, r : r + chunk] = unit.astype(bf16)
            gain = jnp.concatenate([gain_ref[r : r + chunk]] * (TILE // 128), axis=1)
            normed_ref[r : r + chunk] = (unit * gain).astype(bf16)
        kv_ref[0, :, cols] = dot(w_kv_ref[...], normed_ref[...]).astype(bf16)
        live = step * TILE + lax.broadcasted_iota(jnp.int32, (1, TILE), 1) < length
        for h in range(heads):
            scores = dot(query_ref[0, :, h * qk : (h + 1) * qk], kv_ref[0, h * qk : (h + 1) * qk, cols])
            scores = jnp.where(live, scores, MASKED)
            scores_ref[h, :, cols] = scores
            peak = peak_ref[h]
            for c in range(0, TILE, 128):
                peak = jnp.maximum(peak, scores[:, c : c + 128])
            peak_ref[h] = peak

    @pl.when(step == pl.num_programs(1) - 1)
    def _():
        peaks = [jnp.max(peak_ref[h], axis=1, keepdims=True) for h in range(heads)]
        total_ref[...] = jnp.zeros_like(total_ref)

        def attend(t, sums):
            cols = pl.ds(pl.multiple_of(t * TILE, TILE), TILE)
            new = []
            for h in range(heads):
                raised = jnp.exp2((scores_ref[h, :, cols] - peaks[h]) * scale)
                new.append(sums[h] + sum(raised[:, c : c + 128] for c in range(0, TILE, 128)))
                start = qk_cols + h * val
                total_ref[h] += dot_nt(raised.astype(bf16), kv_ref[0, start : start + val, cols])
            return tuple(new)

        sums = lax.fori_loop(0, pl.cdiv(length, TILE), attend, (jnp.zeros((lat_count, 128), f32),) * heads)
        lane = lax.broadcasted_iota(jnp.int32, (lat_count, 128), 1)
        packed = jnp.zeros((lat_count, 128), f32)
        out = []
        for h in range(heads):
            total = jnp.sum(sums[h], axis=1, keepdims=True)
            out.append(total_ref[h] / total)
            packed = jnp.where(lane == h, peaks[h] * scale + jnp.log2(total), packed)
        att_ref[0] = jnp.concatenate(out, axis=1).T
        lse_ref[0] = packed


def front(first, count, lengths, ids, table, pos, pos_mean, gain, w_kv, latents, gain_lat, w_query, heads):
    slots = ids.shape[1]
    width = pos.shape[0]
    lat_count, lat_width = latents.shape[1:]
    qk_cols = w_query.shape[0]
    kv_cols = w_kv.shape[0]
    val_cols = kv_cols - qk_cols
    whole = lambda a: pl.BlockSpec(a.shape, lambda i, t, *_: (0,) * a.ndim)
    each = lambda *s: pl.BlockSpec((1, *s), lambda i, t, *_: (first + i, 0, 0))
    made = lambda *s: pl.BlockSpec((1, *s), lambda i, t, *_: (i, 0, 0))
    shape = lambda s, d: jax.ShapeDtypeStruct((count, *s), d)

    def live(i, t, lengths):
        return jnp.minimum(t, pl.cdiv(lengths[first + i], TILE) - 1)

    return pl.pallas_call(
        functools.partial(front_kernel, first=first, width=width, heads=heads),
        grid_spec=pltpu.PrefetchScalarGridSpec(
            num_scalar_prefetch=1,
            grid=(count, slots // TILE),
            in_specs=[
                whole(ids), whole(table), pl.BlockSpec((width, TILE), lambda i, t, l: (0, live(i, t, l))), whole(pos_mean),
                whole(gain), whole(w_kv), each(lat_count, lat_width), whole(gain_lat), whole(w_query),
            ],
            out_specs=[
                pl.BlockSpec((1, width, TILE), lambda i, t, l: (i, 0, live(i, t, l))), made(1, slots), made(kv_cols, slots),
                made(lat_count, 128), made(lat_count, qk_cols), made(qk_cols, lat_count), made(val_cols, lat_count),
            ],
            scratch_shapes=[
                pltpu.VMEM((table.shape[0], TILE), f32),
                pltpu.VMEM((width, TILE), bf16),
                pltpu.VMEM((heads, lat_count, slots), f32),
                pltpu.VMEM((heads, lat_count, val_cols // heads), f32),
                pltpu.VMEM((heads, lat_count, 128), f32),
            ],
        ),
        out_shape=[
            shape((width, slots), bf16), shape((1, slots), f32), shape((kv_cols, slots), bf16), shape((lat_count, 128), f32),
            shape((lat_count, qk_cols), bf16), shape((qk_cols, lat_count), bf16),
            shape((val_cols, lat_count), f32),
        ],
        compiler_params=limits(56),
        cost_estimate=cost(18),
        name="front",
    )(lengths, ids, table, pos, pos_mean, gain, w_kv, latents, gain_lat, w_query)


def tables_kernel(
    place_ref, byte_ref, pos_ref, gain_ref, w_key_ref, w_value_ref, w_one_ref, w_two_ref, table_ref, pos_t_ref, mean_ref, gains_ref, w_kv_ref, w_back_ref,
    w_rows_ref, one_ref, two_ref, pad_ref,
):
    vocab, width = byte_ref.shape

    @pl.when(pl.program_id(0) == 0)
    def _():
        rows = one_ref.shape[0]
        quarter = pl.ds(pl.multiple_of(place_ref[1] % 4 * rows, 16), rows)
        one_ref[...] = w_one_ref[quarter].astype(f32)
        two_ref[...] = w_two_ref[quarter].astype(f32)
        gain = gain_ref[...]
        gains_ref[...] = jnp.broadcast_to(gain, (128, width)).T
        first = w_key_ref.shape[0]
        w_kv_ref[:first] = w_key_ref[...]
        w_kv_ref[first:] = w_value_ref[...]
        w_rows_ref[...] = w_kv_ref[...].astype(f32).T.astype(bf16)
        scaled = w_kv_ref[...].astype(f32) * gain
        w_back_ref[...] = (scaled - jnp.mean(scaled, axis=1, keepdims=True)).T.astype(bf16)
        pad_ref[...] = jnp.zeros_like(pad_ref)
        pad_ref[:vocab] = byte_ref[...].astype(f32)
        table = pad_ref[...].T
        table_ref[:width] = table[:, : table_ref.shape[1]].astype(bf16)
        mean = jnp.mean(table, axis=0, keepdims=True)[:, : table_ref.shape[1]]
        high = mean.astype(bf16)
        rest = mean - high.astype(f32)
        middle = rest.astype(bf16)
        low = (rest - middle.astype(f32)).astype(bf16)
        more = table_ref.shape[0] - width
        row = lax.broadcasted_iota(jnp.int32, (more, table_ref.shape[1]), 0)
        rows = jnp.zeros(row.shape, f32)
        for place, value in enumerate((high, middle, low)):
            rows = jnp.where(row == place, value.astype(f32), rows)
        table_ref[width:] = rows.astype(bf16)

    pos = pos_ref[...].astype(f32).T
    pos_t_ref[...] = pos.astype(bf16)
    mean_ref[...] = jnp.mean(pos, axis=0, keepdims=True)


def tables_of(place, byte_table, pos_table, gain, w_key_t, w_value_t, w_one_t, w_two):
    vocab, width = byte_table.shape
    slots = pos_table.shape[0]
    kv_cols = w_key_t.shape[0] + w_value_t.shape[0]
    vocab_rows = vocab + -vocab % 16
    whole = lambda a: pl.BlockSpec(a.shape, lambda t: (0,) * a.ndim)
    shapes = [
        ((width + 16, vocab_rows), bf16), ((width, slots), bf16), ((1, slots), f32), ((width, 128), f32), ((kv_cols, width), bf16),
        ((width, kv_cols), bf16), ((width, kv_cols), bf16), *([((w_two.shape[0] // 4, w_two.shape[1]), f32)] * 2),
    ]
    shapes = [jax.ShapeDtypeStruct(*s) for s in shapes]
    specs = [whole(a) for a in shapes]
    specs[1] = pl.BlockSpec((width, TILE), lambda t: (0, t))
    specs[2] = pl.BlockSpec((1, TILE), lambda t: (0, t))
    return pl.pallas_call(
        tables_kernel,
        grid=(slots // TILE,),
        in_specs=[
            pl.BlockSpec(memory_space=pltpu.SMEM), whole(byte_table), pl.BlockSpec((TILE, width), lambda t: (t, 0)), whole(gain),
            whole(w_key_t), whole(w_value_t), whole(w_one_t), whole(w_two),
        ],
        out_specs=specs,
        out_shape=shapes,
        scratch_shapes=[pltpu.VMEM((vocab + -vocab % 128, width), f32)],
        compiler_params=limits(40),
        cost_estimate=cost(8),
        name="tables",
    )(place, byte_table, pos_table, gain, w_key_t, w_value_t, w_one_t, w_two)


def back_kernel(
    lengths, place_ref, ids_ref, w_ref, w_rows_ref, gain_ref, *refs,
    first, heads, groups, last, vocab,
):
    step, item = pl.program_id(0), pl.program_id(1)
    length = lengths[item]
    tile = step + first
    sums_in, refs = (refs[:3], refs[3:]) if first else ((), refs)
    made = [refs[9 * g : 9 * g + 9] for g in range(groups)]
    refs = refs[9 * groups :]
    pos_ref, query_out_ref, *refs = refs
    if last:
        keep_ref, send_ref, *refs, byte_ref, unit_kv_ref, turned_ref = refs
    else:
        byte_ref, unit_kv_ref, *refs = refs
    (
        unit_ref, inv_ref, kv_ref, lse_ref, query_ref, query_t_ref, att_grad_ref, att_grad_t_ref, delta_ref, kv_grad_ref, low_ref,
    ) = refs
    width, kv_cols = w_ref.shape
    qk_cols = query_ref.shape[1]
    qk, val = qk_cols // heads, (kv_cols - qk_cols) // heads
    factor = qk**-0.5
    scale = factor * LOG2E
    chunk = 64
    share = pos_ref.shape[1]

    def order(block):
        distance = place_ref[0] ^ block
        return distance % 2 * 2 + distance // 2

    @pl.when((step == 0) & (item == 0))
    def _():
        for i, ref in enumerate((query_out_ref, byte_ref, unit_kv_ref)):
            ref[...] = sums_in[i][...] if first else jnp.zeros_like(ref)

    @pl.when(item == 0)
    def _():
        pos_ref[:, :, :TILE] = jnp.zeros((4, share, TILE), f32)

    for g in range(groups):

        @pl.when((tile * TILE < length) & (item // (pl.num_programs(1) // groups) == g))
        def _():
            copies = (unit_ref, inv_ref, kv_ref, lse_ref, query_ref, query_t_ref, att_grad_ref, att_grad_t_ref, delta_ref)
            for target, ref in zip(copies, made[g]):
                target[...] = ref[0]

    @pl.when(tile * TILE < length)
    def _():
        live = tile * TILE + lax.broadcasted_iota(jnp.int32, (1, TILE), 1) < length
        cross = jnp.zeros((8, TILE), f32)
        for h in range(heads):
            keys = slice(h * qk, (h + 1) * qk)
            values = slice(qk_cols + h * val, qk_cols + (h + 1) * val)
            cols = slice(h * val, (h + 1) * val)
            scores = dot(query_ref[:, keys], kv_ref[keys])
            chances = jnp.exp2(scores * scale - lse_ref[:, h : h + 1])
            chances = jnp.where(live, chances, 0.0)
            weights_grad = dot(att_grad_ref[:, cols], kv_ref[values])
            scores_grad = (chances * (weights_grad - delta_ref[:, h : h + 1])).astype(bf16)
            query_out_ref[item, keys] += dot_nt(kv_ref[keys], scores_grad)
            kv_grad_ref[keys] = (dot(query_t_ref[keys], scores_grad) * factor).astype(bf16)
            kv_grad_ref[values] = dot(att_grad_t_ref[cols], chances.astype(bf16)).astype(bf16)
        for r in range(0, kv_cols, chunk):
            rows = kv_grad_ref[r : r + chunk].astype(f32) * kv_ref[r : r + chunk].astype(f32)
            cross += sum(rows[i : i + 8] for i in range(0, chunk, 8))
        inv = inv_ref[...]
        cross = jnp.sum(cross, axis=0, keepdims=True) * (1.0 / width) * inv
        back = dot(w_ref[...], kv_grad_ref[...])
        for r in range(0, width, chunk):
            rows = slice(r, r + chunk)
            grads = back[rows] * inv - unit_ref[rows].astype(f32) * cross
            pos_ref[order(r // share), r % share : r % share + chunk, :TILE] += grads
            low_ref[rows] = grads.astype(bf16)
        hits = (lax.broadcasted_iota(jnp.int32, (byte_ref.shape[0], TILE), 0) == ids_ref[pl.ds(item, 1)]).astype(bf16)
        byte_ref[...] += dot_nt(hits, low_ref[...])
        unit_kv_ref[...] += dot_nt(kv_grad_ref[...], unit_ref[...])

    if last:

        @pl.when((step == pl.num_programs(0) - 1) & (item == pl.num_programs(1) - 1))
        def _():
            query_out_ref[...] = (query_out_ref[...] * factor).astype(bf16).astype(f32)
            turned_ref[...] = unit_kv_ref[...].T
            gain_grad = jnp.sum(turned_ref[...] * w_rows_ref[...].astype(f32), axis=1, keepdims=True)
            spare = pos_ref.shape[2] - TILE - byte_ref.shape[0]
            byte = jnp.concatenate([byte_ref[...], jnp.zeros((spare, width), f32)], axis=0).T
            byte = jnp.where(lax.broadcasted_iota(jnp.int32, byte.shape, 1) == vocab, gain_grad, byte)
            for block in range(4):
                pos_ref[order(block), :, TILE:] = byte[block * share : (block + 1) * share]
            turned_ref[...] *= gain_ref[:, :1]
            split_blocks(keep_ref, send_ref, turned_ref, place_ref[1])


def back(place, first, count, lengths, ids, made, w_back, w_rows, gains, sums, heads, vocab):
    items, slots = ids.shape
    last = (first + count) * TILE == slots
    groups = len(made)
    size = items // groups
    width, kv_cols = w_back.shape
    lat_count, qk_cols = made[0][4].shape[1:]
    val_cols = kv_cols - qk_cols
    whole = lambda a: pl.BlockSpec(a.shape, lambda t, i, *_: (0,) * a.ndim)
    clip = lambda i, g: jnp.clip(i - g * size, 0, size - 1)
    tiles = lambda g, *s: pl.BlockSpec((1, *s, TILE), lambda t, i, *_: (clip(i, g), 0, t + first))
    each = lambda g, *s: pl.BlockSpec((1, *s), lambda t, i, *_: (clip(i, g), 0, 0))
    shape = lambda s: jax.ShapeDtypeStruct(s, f32)
    kernel = functools.partial(back_kernel, first=first, heads=heads, groups=groups, last=last, vocab=vocab)
    operands = (ids, w_back, w_rows, gains, *sums, *(a for nine in made for a in nine))
    byte_cols = vocab + -vocab % 128
    sums_of = (items, qk_cols, lat_count), (vocab + -vocab % 16, width), (kv_cols, width)
    query_sum, byte_sum, unit_kv = (shape(a) for a in sums_of)
    blocks = lax.axis_size("dp")
    if last:
        assert count == 1
        split = shape((blocks // 2, width // blocks, kv_cols))
        out_shape = [shape((4, width // 4, TILE + byte_cols)), query_sum, split, split]
        out_specs = [whole(a) for a in out_shape]
    else:
        out_shape = [shape((4, width // 4, count * TILE)), query_sum, byte_sum, unit_kv]
        out_specs = [pl.BlockSpec((4, width // 4, TILE), lambda t, i, *_: (0, 0, t)), *(whole(a) for a in out_shape[1:])]
    return pl.pallas_call(
        kernel,
        grid_spec=pltpu.PrefetchScalarGridSpec(
            num_scalar_prefetch=2,
            grid=(count, items),
            in_specs=[
                pl.BlockSpec((items, TILE), lambda t, i, *_: (0, t + first)),
                *(whole(a) for a in (w_back, w_rows, gains, *sums)),
                *(
                    spec
                    for g in range(groups)
                    for spec in (
                        tiles(g, width), tiles(g, 1), tiles(g, kv_cols), each(g, lat_count, 128), each(g, lat_count, qk_cols),
                        each(g, qk_cols, lat_count), each(g, lat_count, val_cols), each(g, val_cols, lat_count), each(g, lat_count, 128),
                    )
                ),
            ],
            out_specs=out_specs,
            scratch_shapes=[
                pltpu.VMEM((width, TILE), bf16), pltpu.VMEM((1, TILE), f32), pltpu.VMEM((kv_cols, TILE), bf16),
                pltpu.VMEM((lat_count, 128), f32), pltpu.VMEM((lat_count, qk_cols), bf16),
                pltpu.VMEM((qk_cols, lat_count), bf16), pltpu.VMEM((lat_count, val_cols), bf16),
                pltpu.VMEM((val_cols, lat_count), bf16), pltpu.VMEM((lat_count, 128), f32),
                pltpu.VMEM((kv_cols, TILE), bf16), pltpu.VMEM((width, TILE), bf16),
                *([pltpu.VMEM(s, f32) for s in (*sums_of[1:], (width, kv_cols))] if last else []),
            ],
        ),
        out_shape=out_shape,
        compiler_params=limits(58),
        cost_estimate=cost(12 * count),
        name="back",
    )(lengths, place, *operands)


def assemble_kernel(place_ref, own_ref, *refs):
    *far_refs, out_ref = refs
    side, corner = place_ref[0] // 2, place_ref[1] % 4
    rows = own_ref.shape[0]
    quarter = rows // 4

    def put(start, ref):
        out_ref[pl.ds(pl.multiple_of(start, 16), ref.shape[0])] = ref[...].astype(bf16)

    put(side * rows, own_ref)
    for step, ref in enumerate(far_refs):
        put((1 - side) * rows + (corner ^ step) * quarter, ref)


def assemble(place, own, far, tokens=()):
    rows, width = own.shape
    operands = (own, *far)
    return pl.pallas_call(
        ignoring(assemble_kernel, 1 + len(operands), len(tokens)),
        in_specs=[
            pl.BlockSpec(memory_space=pltpu.SMEM), *([pl.BlockSpec(memory_space=pltpu.VMEM)] * len(operands)),
            *([ANYWHERE] * len(tokens)),
        ],
        out_specs=pl.BlockSpec(memory_space=pltpu.VMEM),
        out_shape=jax.ShapeDtypeStruct((2 * rows, width), bf16),
        compiler_params=limits(40),
        cost_estimate=cost(2),
        name="assemble",
    )(place, *operands, *tokens)


def packed(block):
    rows, cols = block.shape
    parts = [block[:, c : c + 128] for c in range(0, cols - 127, 128)]
    if cols % 128:
        last = block[:, cols - 64 :]
        parts.append(jnp.concatenate([last[: rows // 2], last[rows // 2 :]], axis=1))
    return jnp.concatenate(parts, axis=0)


def unpacked(block, cols):
    rows = block.shape[0] * 128 // cols
    count = cols // 128
    parts = [block[c * rows : (c + 1) * rows] for c in range(count)]
    if cols % 128:
        last = block[count * rows :]
        parts.append(jnp.concatenate([last[:, :64], last[:, 64:]], axis=0))
    return jnp.concatenate(parts, axis=1)


def reversed_bits(count):
    order = [0]
    while len(order) < count:
        order = [2 * o for o in order] + [2 * o + 1 for o in order]
    return order


def split_blocks(keep_ref, send_ref, total, dp_place, shape=lambda block: block):
    count = keep_ref.shape[0]
    size = total.shape[0] // count // 2
    for ref, flip in ((keep_ref, 0), (send_ref, 1)):
        for j, distance in enumerate(reversed_bits(count)):
            target = dp_place ^ (2 * distance + flip)
            ref[j] = shape(total[pl.ds(pl.multiple_of(target * size, 8), size)])


def put_blocks(keep_ref, send_ref, total, dp_place):
    split_blocks(keep_ref, send_ref, total, dp_place, packed)


def call(kernel, grid, inputs, outputs, scratch=(), tokens=(), name=None, time=1, limit=56):
    whole = lambda a: (a, a.shape, lambda *_: (0,) * a.ndim)
    inputs = [i if isinstance(i, tuple) else whole(i) for i in inputs]
    specs = [pl.BlockSpec(block, index) if block else pl.BlockSpec(memory_space=pltpu.SMEM) for _, block, index in inputs]
    return pl.pallas_call(
        ignoring(kernel, len(inputs), len(tokens)),
        grid=grid,
        in_specs=[*specs, *([ANYWHERE] * len(tokens))],
        out_specs=[pl.BlockSpec(block, index) for _, _, block, index in outputs],
        out_shape=[jax.ShapeDtypeStruct(shape, kind) for shape, kind, _, _ in outputs],
        scratch_shapes=list(scratch),
        compiler_params=limits(limit),
        cost_estimate=cost(time),
        name=name,
    )(*(a for a, _, _ in inputs), *tokens)


def scalars(place):
    return place, None, None


def each(array):
    return array, (1, *array.shape[1:]), lambda i: (i, *(0,) * (array.ndim - 1))


def part(array, first):
    return array, (1, *array.shape[1:]), lambda i: (first + i, *(0,) * (array.ndim - 1))


def among(array, group, size):
    return array, (1, *array.shape[1:]), lambda i: (jnp.clip(i - group * size, 0, size - 1), 0, 0)


def new(shape, kind=f32):
    return shape, kind, (1, *shape[1:]), lambda i: (i, *(0,) * (len(shape) - 1))


def kept(shape, kind=f32):
    return shape, kind, shape, lambda i: (0,) * len(shape)


def mix(place, own, far, w_out, tokens=()):
    count, rows, lat_count = own.shape

    def kernel(place_ref, own_ref, far_ref, w_ref, out_ref, att_ref):
        side = place_ref[0] // 2
        for ref, at in ((own_ref, side), (far_ref, 1 - side)):
            att_ref[pl.ds(pl.multiple_of(at * rows, 16), rows)] = ref[0].astype(bf16)
        out_ref[0] = dot_tn(att_ref[...], w_ref[...])

    return call(
        kernel, (count,), [scalars(place), each(own), each(far), w_out], [new((count, lat_count, w_out.shape[1]))],
        [pltpu.VMEM((2 * rows, lat_count), bf16)], tokens, "mix", 3, 14,
    )[0]


def feed(place, first, latents, out_grad, mixed, crossed, gain, w_one, w_two, tokens=()):
    count, lat_count, width = mixed.shape
    rows = w_one.shape[0] // 2

    def kernel(
        place_ref, lat_ref, grad_ref, mixed_ref, crossed_ref, gain_ref, w_one_ref, w_two_ref,
        hidden_ref, normed_ref, activated_ref, share_ref, own_ref, up_own_ref, parts_ref,
    ):
        side = place_ref[0] // 2

        def own(tensor):
            parts_ref[0] = tensor[:, :rows]
            parts_ref[1] = tensor[:, rows:]
            return parts_ref[side]

        hidden = lat_ref[0].astype(f32) + (mixed_ref[0] + crossed_ref[0])
        hidden_ref[0] = hidden
        unit, _ = row_norm(hidden)
        normed = (unit * gain_ref[...]).astype(bf16)
        normed_ref[0] = normed
        up = dot_nt(normed, w_one_ref[...])
        below = 0.5 * (1.0 + lax.erf(up * 0.5**0.5))
        activated = (up * below).astype(bf16)
        activated_ref[0] = activated
        own_ref[0] = own(activated)
        slope = below + up * (jnp.exp(-0.5 * up * up) * 0.3989422804014327)
        up_grad = (dot_nt(grad_ref[0], w_two_ref[...]) * slope).astype(bf16)
        up_own_ref[0] = own(up_grad)
        share_ref[0] = dot(up_grad, w_one_ref[...])

    full, low = (count, lat_count, width), (count, lat_count, rows)
    return call(
        kernel, (count,),
        [scalars(place), part(latents, first), part(out_grad, first), each(mixed), each(crossed), gain, w_one, w_two],
        [new(full), new(full, bf16), new((count, lat_count, 2 * rows), bf16), new(full), new(low, bf16), new(low, bf16)],
        [pltpu.VMEM((2, lat_count, rows), bf16)], tokens, "feed", 6, 36,
    )


def split_grad(blocks, width, rows):
    return kept((blocks // 2, width // blocks * rows // 128, 128))


def feed_weights(place, out_grad, fed, blocks, tokens=()):
    items, lat_count, width = out_grad.shape
    groups = len(fed)
    size = items // groups
    rows = fed[0][1].shape[2]

    def kernel(place_ref, grad_ref, *refs):
        item = pl.program_id(0)
        keep_one, send_one, keep_two, send_two, one_sum, two_sum = refs[3 * groups :]

        @pl.when(item == 0)
        def _():
            one_sum[...] = jnp.zeros_like(one_sum)
            two_sum[...] = jnp.zeros_like(two_sum)

        for g in range(groups):

            @pl.when(item // size == g)
            def _():
                normed_ref, activated_ref, up_grad_ref = refs[3 * g : 3 * g + 3]
                two_sum[...] += dot_tn(grad_ref[0], activated_ref[0])
                one_sum[...] += dot_tn(normed_ref[0], up_grad_ref[0])

        @pl.when(item == items - 1)
        def _():
            put_blocks(keep_two, send_two, two_sum, place_ref[1])
            put_blocks(keep_one, send_one, one_sum, place_ref[1])

    return call(
        kernel, (items,), [scalars(place), each(out_grad), *(among(a, g, size) for g in range(groups) for a in fed[g])],
        [split_grad(blocks, width, rows)] * 4, [pltpu.VMEM((width, rows), f32)] * 2, tokens, "feed_weights", 6, 26,
    )


def unmix(place, first, out_grad, hidden, share, crossed, gain, w_out, att, before, blocks, heads, tokens=()):
    count, lat_count, width = hidden.shape
    rows = w_out.shape[0]
    val = rows // heads

    def kernel(place_ref, grad_ref, hidden_ref, share_ref, crossed_ref, gain_ref, w_ref, att_ref, *refs):
        item = pl.program_id(0)
        sums_in, refs = refs[: len(before)], refs[len(before) :]
        hidden_grad_ref, att_grad_ref, att_grad_t_ref, delta_ref, gain_grad_ref, sum_ref, *split = refs

        @pl.when(item == 0)
        def _():
            for i, ref in enumerate((gain_grad_ref, sum_ref)):
                ref[...] = sums_in[i][...] if before else jnp.zeros_like(ref)

        unit, inv = row_norm(hidden_ref[0])
        norm_grad = share_ref[0] + crossed_ref[0]
        gain_grad_ref[...] += jnp.sum(norm_grad * unit, axis=0, keepdims=True)
        hidden_grad = grad_ref[0].astype(f32) + row_norm_back(norm_grad, unit, inv, gain_ref[...])
        hidden_grad_ref[0] = hidden_grad
        mixed_grad = hidden_grad.astype(bf16)
        att = att_ref[0].T
        sum_ref[...] += dot_tn(mixed_grad, att.astype(bf16))
        att_grad = dot_nt(mixed_grad, w_ref[...])
        att_grad_ref[0] = att_grad.astype(bf16)
        att_grad_t_ref[0] = att_grad.T.astype(bf16)
        product = att_grad.astype(bf16).astype(f32) * att
        lane = lax.broadcasted_iota(jnp.int32, delta_ref.shape[1:], 1)
        delta = jnp.zeros(delta_ref.shape[1:], f32)
        for h in range(heads):
            delta = jnp.where(lane == h, jnp.sum(product[:, h * val : (h + 1) * val], axis=1, keepdims=True), delta)
        delta_ref[0] = delta
        if split:

            @pl.when(item == count - 1)
            def _():
                put_blocks(*split, sum_ref, place_ref[1])

    full = (count, lat_count, width)
    return call(
        kernel, (count,),
        [
            scalars(place), part(out_grad, first), each(hidden), each(share), each(crossed), gain, w_out, each(att), *before,
        ],
        [
            new(full), new((count, lat_count, rows), bf16), new((count, rows, lat_count), bf16), new((count, lat_count, 128)),
            kept((1, width)), kept((width, rows)), *([split_grad(blocks, width, rows)] * 2 if first else []),
        ],
        [], tokens, "unmix", 6, 32,
    )


def branch(activated, w_two, tokens=()):
    count, lat_count, _ = activated[0].shape
    groups = len(activated)
    width = w_two.shape[1]

    def kernel(*refs):
        *group_refs, w_ref, out_ref = refs
        for g in range(groups):

            @pl.when(pl.program_id(0) // count == g)
            def _():
                out_ref[0] = dot(group_refs[g][0], w_ref[...])

    return call(
        kernel, (count * groups,), [*(among(a, g, count) for g, a in enumerate(activated)), w_two],
        [new((count * groups, lat_count, width))], [], tokens, "branch", 4, 20,
    )[0]


def block_output(hidden, share, crossed, tokens=()):
    count = hidden[0].shape[0]
    groups = len(hidden)

    def kernel(*refs):
        *hidden_refs, share_ref, crossed_ref, out_ref = refs
        for g in range(groups):

            @pl.when(pl.program_id(0) // count == g)
            def _():
                out_ref[0] = (hidden_refs[g][0] + (share_ref[0] + crossed_ref[0])).astype(bf16)

    return call(
        kernel, (count * groups,), [*(among(a, g, count) for g, a in enumerate(hidden)), each(share), each(crossed)],
        [new(share.shape, bf16)], [], tokens, "block_output", 4, 20,
    )[0]


def latent(place, query_grad, latents, hidden_grad, gain, w_query, blocks):
    items, lat_count, width = latents.shape
    rows = w_query[0].shape[0]
    groups = len(hidden_grad)
    size = items // groups

    def kernel(
        place_ref, own_ref, core_ref, far_ref, far_core_ref, lat_ref, gain_ref, w_own, w_core, w_far, w_far_core, *refs,
    ):
        grad_ref, gain_grad_ref, keep_ref, send_ref, w_ref, parts_ref, sum_ref, turned_ref = refs[groups:]
        item = pl.program_id(0)
        place = place_ref[0]

        def put(target, refs, value):
            for step, ref in enumerate(refs):
                target[pl.ds(pl.multiple_of((place ^ step) * rows, 16), rows)] = value(ref).astype(bf16)

        @pl.when(item == 0)
        def _():
            put(w_ref, (w_own, w_core, w_far, w_far_core), lambda ref: ref[...])
            gain_grad_ref[...] = jnp.zeros_like(gain_grad_ref)
            sum_ref[...] = jnp.zeros_like(sum_ref)

        put(parts_ref, (own_ref, core_ref, far_ref, far_core_ref), lambda ref: ref[0])
        unit, inv = row_norm(lat_ref[0].astype(f32))
        gain = gain_ref[...]
        sum_ref[...] += dot(own_ref[0].astype(bf16), (unit * gain).astype(bf16))
        norm_grad = dot_tn(parts_ref[...], w_ref[...])
        gain_grad_ref[...] += jnp.sum(norm_grad * unit, axis=0, keepdims=True)
        for g in range(groups):

            @pl.when(item // size == g)
            def _():
                grad_ref[0] = refs[g][0] + row_norm_back(norm_grad, unit, inv, gain)

        @pl.when(item == items - 1)
        def _():
            turned_ref[...] = sum_ref[...].T
            put_blocks(keep_ref, send_ref, turned_ref, place_ref[1])

    return call(
        kernel, (items,),
        [
            scalars(place), *(each(q) for q in query_grad), each(latents), gain, *w_query,
            *(among(a, g, size) for g, a in enumerate(hidden_grad)),
        ],
        [new(latents.shape), kept((1, width)), *([split_grad(blocks, width, rows)] * 2)],
        [
            pltpu.VMEM((4 * rows, width), bf16), pltpu.VMEM((4 * rows, lat_count), bf16), pltpu.VMEM((rows, width), f32),
            pltpu.VMEM((width, rows), f32),
        ], (), "latent", 16, 36,
    )


def at(array, index):
    return array, (1, *array.shape[1:]), lambda *_: (index, *(0,) * (array.ndim - 1))


def pos_blocks(columns, slots):
    return [
        (packed(columns[:, c : c + slots]), packed(columns[:, c + slots : c + 2 * slots]))
        for c in range(0, columns.shape[1], 2 * slots)
    ]


def first_sums(place, pos, near, far, slots):
    share, cols = far.shape

    def kernel(place_ref, pos_ref, near_ref, far_ref, keep_ref, send_ref):
        side = place_ref[1] % 2
        for i, (low, high) in enumerate(pos_blocks(pos_ref[0] + near_ref[0] + far_ref[...], slots)):
            keep_ref[i] = jnp.where(side == 0, low, high)
            send_ref[i] = jnp.where(side == 0, high, low)

    split = kept((cols // slots // 2, share * slots // 128, 128))
    return call(
        kernel, (1,), [scalars(place), at(pos, 0), at(near, 2), far], [split, split], [], (), "first_sums", 3, 40
    )


def second_sums(place, tiles, gain_lat, gain_mlp, slots, vocab):
    share, cols = tiles[-1][2].shape
    own = gain_lat.shape[1] // 4
    count = TILE // slots // 2 * len(tiles)
    rows = share * slots // 128
    byte_rows = share // 2 * (cols - TILE) // 128
    first = vocab + 1 + -(vocab + 1) % 8

    def kernel(place_ref, *refs):
        tile_refs = [refs[3 * t : 3 * t + 3] for t in range(len(tiles))]
        lat_ref, mlp_ref, keep_ref, send_ref, byte_ref, gains_ref = refs[3 * len(tiles) :]
        side = place_ref[1] % 2
        blocks = []
        for pos_ref, near_ref, far_ref in tile_refs:
            mine = pos_ref[0] + near_ref[0] + far_ref[...]
            blocks += pos_blocks(mine[:, :TILE], slots)
        byte_ref[...] = mine[:, TILE:]
        gains = jnp.concatenate([lat_ref[...], mlp_ref[...], jnp.zeros((6, lat_ref.shape[1]), f32)], axis=0)
        gains_ref[...] = gains.T
        gains = gains_ref[pl.ds(pl.multiple_of(place_ref[0] * own, 8), own)]
        byte_ref[:, first : first + 8] = gains[:share]
        byte_ref[: own - share, first + 8 : first + 16] = gains[share:]
        blocks.append((packed(byte_ref[: share // 2]), packed(byte_ref[share // 2 :])))
        start = 0
        for low, high in blocks:
            stretch = slice(start, start + low.shape[0])
            keep_ref[stretch] = jnp.where(side == 0, low, high)
            send_ref[stretch] = jnp.where(side == 0, high, low)
            start += low.shape[0]

    split = kept((count * rows + byte_rows, 128))
    return call(
        kernel, (1,),
        [scalars(place), *(a for pos, near, far in tiles for a in (at(pos, 0), at(near, 2), far)), gain_lat, gain_mlp],
        [split, split], [pltpu.VMEM((share, cols - TILE), f32), pltpu.VMEM((gain_lat.shape[1], 8), f32)], (), "second_sums", 3,
        40,
    )


def third_sums(place, keep_ab, cross_ab, query, keep, cross, byte_rows, half, tokens=()):
    before, rows, _ = keep_ab.shape
    last = (keep.shape[0] - byte_rows) // rows
    count = before + last
    size, part = byte_rows // count, half // count

    def kernel(
        place_ref, keep_ab_ref, cross_ab_ref, query_ref, keep_ref, cross_ref, pos_keep_ref, pos_send_ref, byte_ref, query_out_ref
    ):
        ring = place_ref[1] // 2
        query_out_ref[...] = query_ref[...]
        sums = [keep_ab_ref[i] + cross_ab_ref[i] for i in range(before)]
        total = keep_ref[...] + cross_ref[...]
        sums += [total[i * rows : (i + 1) * rows] for i in range(last)]
        for i in range(count // 2):
            pos_keep_ref[i] = jnp.where(ring % 2 == 0, sums[2 * i], sums[2 * i + 1])
            pos_send_ref[i] = jnp.where(ring % 2 == 0, sums[2 * i + 1], sums[2 * i])
        total = total[last * rows :]
        for j in range(count):
            distance = ring ^ j
            place, bits = 0, count.bit_length() - 1
            for b in range(bits):
                place += (distance >> b & 1) << (bits - 1 - b)
            byte_ref[place] = jnp.concatenate(
                [total[c + j * part : c + (j + 1) * part] for c in range(0, byte_rows, half)], axis=0
            )

    split = kept((count // 2, rows, 128))
    return call(
        kernel, (1,), [scalars(place), keep_ab, cross_ab, query, keep, cross],
        [split, split, kept((count, size, 128)), kept(query.shape)], [], tokens, "third_sums", 3, 40,
    )


def next_sums(place, keep, cross, bit, parts=(), query=(), tokens=()):
    count, rows, _ = keep.shape

    def kernel(place_ref, *refs):
        part_refs, refs = refs[: len(parts)], refs[len(parts) :]
        query_refs, refs = refs[: len(query)], refs[len(query) :]
        keep_ref, cross_ref, pos_keep_ref, pos_send_ref, *refs = refs
        mine = place_ref[1] // bit % 2
        sums = [keep_ref[i] + cross_ref[i] for i in range(count)]
        for i in range(count // 2):
            pos_keep_ref[i] = jnp.where(mine == 0, sums[2 * i], sums[2 * i + 1])
            pos_send_ref[i] = jnp.where(mine == 0, sums[2 * i + 1], sums[2 * i])
        if parts:
            refs[0][...] = sum(ref[0] if len(ref.shape) == 3 else ref[...] for ref in part_refs)
        if query:
            total = query_refs[0][...] + query_refs[1][...]
            refs[-2][...] = total[: total.shape[0] // 2]
            refs[-1][...] = total[total.shape[0] // 2 :]

    split = kept((count // 2, rows, 128))
    outputs = [split, split, *([kept(parts[1].shape)] if parts else [])]
    if query:
        outputs += [kept((query[0].shape[0] // 2, *query[0].shape[1:]))] * 2
    return call(
        kernel, (1,), [scalars(place), *parts, *query, keep, cross], outputs, [], tokens, "next_sums", 2, 40
    )


def last_sums(place, keep, cross, parts, query, share):
    count = len(parts)
    size = parts[0].shape[0]
    rows = keep.shape[1]
    half = share // 2
    part = half // count
    lanes = size // part

    def kernel(place_ref, *refs):
        part_refs, (one_ref, other_ref, keep_ref, cross_ref, pos_ref, byte_ref, query_ref, held_ref) = refs[:count], refs[count:]
        query_ref[...] = one_ref[...] + other_ref[...]
        pos_ref[...] = unpacked(keep_ref[0] + cross_ref[0], pos_ref.shape[1])
        for distance, ref in enumerate(part_refs):
            held_ref[place_ref[1] // 2 ^ distance] = ref[...]
        byte_ref[...] = jnp.concatenate(
            [held_ref[j, c * part : (c + 1) * part] for c in range(lanes) for j in range(count)], axis=0
        )

    return call(
        kernel, (1,), [scalars(place), *parts, *query, keep, cross],
        [kept((share, rows * 128 // share)), kept((count * size, 128)), kept(query[0].shape)],
        [pltpu.VMEM((count, size, 128), f32)], (), "last_sums", 2, 40,
    )


def byte_sums(place, own, other, share, vocab, gain_cols):
    cols = own.shape[0] * 128 // (share // 2)
    first = vocab + 1 + -(vocab + 1) % 8

    def kernel(place_ref, own_ref, other_ref, table_ref, gain_ref, gains_ref):
        side = place_ref[1] % 2
        low = jnp.where(side == 0, own_ref[...], other_ref[...])
        high = jnp.where(side == 0, other_ref[...], own_ref[...])
        turned = jnp.concatenate([unpacked(low, cols), unpacked(high, cols)], axis=0).T
        table_ref[...] = turned[:vocab]
        gain_ref[...] = turned[vocab : vocab + 1]
        gains_ref[...] = jnp.concatenate([turned[first : first + 2], turned[first + 8 : first + 10, : gain_cols - share]], axis=1)

    return call(
        kernel, (1,), [scalars(place), own, other], [kept((vocab, share)), kept((1, share)), kept((2, gain_cols))], [], (),
        "byte_sums", 2, 40,
    )


def finish(sums, cols, tokens=()):
    def kernel(*refs):
        for i, out_ref in enumerate(refs[2 * len(sums) :]):
            out_ref[...] = unpacked(refs[2 * i][0] + refs[2 * i + 1][0], cols)

    rows = sums[0][0].shape[1] * 128 // cols
    return call(
        kernel, (1,), [at(a, 0) for pair in sums for a in pair], [kept((rows, cols))] * len(sums), [], tokens, "finish", 3, 40
    )


def swap(tensor, axis, bit):
    return lax.ppermute(tensor, axis, [(i, i ^ bit) for i in range(lax.axis_size(axis))])


def stage(always, work):
    shapes = jax.eval_shape(work)
    return lax.cond(always, work, lambda: jax.tree.map(lambda s: jnp.zeros(s.shape, s.dtype), shapes))


def body(
    byte_ids, lengths, latents, byte_table, pos_table, gain_in, gain_lat, gain_mlp,
    w_query, w_key, w_value, w_out, w_one, w_two, out_grad,
):
    items, slots = byte_ids.shape
    vocab, width = byte_table.shape
    lat_count, lat_width = latents.shape[1:]
    mp, dp = lax.axis_size("mp"), lax.axis_size("dp")
    mp_place, dp_place = lax.axis_index("mp"), lax.axis_index("dp")
    place = jnp.stack([mp_place, dp_place]).astype(jnp.int32)
    heads = HEADS // mp
    qk_cols = w_query.shape[1]
    val_cols = w_value.shape[1]
    corner, side = dp_place % 4, dp_place % 2

    shards = [w_out, w_one.T, w_two]
    quarter = val_cols // 4
    always = lengths[0] > 0
    over_y = lambda w: swap(lax.dynamic_slice_in_dim(w, corner * quarter, quarter, 0).astype(f32), "mp", 2)
    over_x, over_z, over_both = (lambda a, bits=bits: swap(a, "dp", bits) for bits in (1, 2, 3))
    core = lambda a: swap(a, "mp", 1)
    half = items // 2

    def first_stage():
        out = over_y(shards[0])
        weights = (gain_in[None], w_key.T, w_value.T, *shards[1:])
        *tables, w_back, w_rows, one, two = tables_of(place, byte_table, pos_table, *weights)
        far = swap(one, "mp", 2), swap(two, "mp", 2)
        return front_of(0, tables), out, [over_x(out), over_z(out)], over_both(out), far, (tables, w_back, w_rows)

    def front_of(first, tables):
        return front(first, half, lengths, byte_ids, *tables, latents, gain_lat[None], w_query.T, heads)

    (*made_a, att_a), out, crossed_out, last_out, (one, two), (tables, w_back, w_rows) = stage(always, first_stage)

    def third_stage():
        return front_of(half, tables), [over_x(one), over_z(one), over_both(one)], over_both(two), swap(att_a, "mp", 2)

    (*made_b, att_b), crossed_one, last_two, far_a = stage(always, third_stage)

    def fourth_stage():
        crossed_two = [over_x(two), over_z(two), last_two]
        far_b = swap(att_b, "mp", 2)
        w_out_whole = assemble(place, shards[0], [out, *crossed_out, last_out])
        w_one_whole = assemble(place, shards[1], [one, *crossed_one], [w_out_whole])
        mixed_a = mix(place, att_a, far_a, w_out_whole, [w_one_whole])
        return w_out_whole, w_one_whole, mixed_a, crossed_two[:2], far_b

    w_out_whole, w_one_whole, mixed_a, crossed_two, far_b = stage(always, fourth_stage)
    w_two_whole = assemble(place, shards[2], [two, *crossed_two, last_two])
    mixed_b = mix(place, att_b, far_b, w_out_whole, [w_two_whole])
    gain = gain_mlp[None]
    weights = (gain, w_one_whole, w_two_whole)
    hidden_a, normed_a, activated_a, share_a, act_a, up_a = feed(
        place, 0, latents, out_grad, mixed_a, core(mixed_a), *weights, [mixed_b]
    )
    hidden_b, normed_b, activated_b, share_b, act_b, up_b = feed(
        place, half, latents, out_grad, mixed_b, core(mixed_b), *weights, [share_a]
    )
    keep_one, send_one, keep_two, send_two = feed_weights(
        place, out_grad, [(normed_a, act_a, up_a), (normed_b, act_b, up_b)], dp
    )
    w_query_own = w_query.T.astype(f32)
    crossed_a, crossed_b = core(share_a), core(share_b)

    def unmix_stage():
        grads_a = unmix(place, 0, out_grad, hidden_a, share_a, crossed_a, gain, w_out, att_a, [], dp, heads)
        grads_b = unmix(place, half, out_grad, hidden_b, share_b, crossed_b, gain, w_out, att_b, grads_a[4:], dp, heads)
        w_query_parts = core(w_query_own), swap(w_query_own, "mp", 2)
        share_out = branch((activated_a, activated_b), w_two_whole)
        return grads_a[:4], grads_b[:5], grads_b[6:], swap(send_two, "dp", 1), w_query_parts, share_out

    unmixed_a, unmixed_b, (keep_out, send_out), cross_two, w_query_parts, share_out = stage(always, unmix_stage)
    (hidden_grad_a, *grads_a), (hidden_grad_b, *grads_b, gain_mlp_grad) = unmixed_a, unmixed_b
    made = [(*made_a, *grads_a), (*made_b, *grads_b)]
    byte_cols = vocab + -vocab % 128
    bits = [1 << i for i in range(1, dp.bit_length() - 1)]

    def back_of(first, count, sums):
        return back(place, first, count, lengths, byte_ids, made, w_back, w_rows, tables[3], sums, heads, vocab)

    def halve(blocks, bits):
        for bit in bits:
            count = blocks.shape[0] // 2
            blocks = blocks[:count] + swap(blocks[count:], "dp", bit)
        return blocks

    two_blocks = keep_two + cross_two

    def back_stage_a():
        transfers = swap(send_one, "dp", 1), halve(two_blocks, bits[:1]), core(w_query_parts[1]), core(share_out)
        return back_of(0, 2, []), transfers

    (pos_a, *sums), (cross_one, two_blocks, w_query_last, crossed_out) = stage(always, back_stage_a)
    w_query_all = [w_query_own, *w_query_parts, w_query_last]

    def last_pair(blocks):
        return blocks[:1], swap(blocks[1:], "dp", bits[-1])

    def back_stage_b():
        near_a = core(pos_a)
        two, one = halve(two_blocks, bits[1:-1]), halve(keep_one + cross_one, bits[:1])
        two = last_pair(two)
        cross_out = swap(send_out, "dp", 1)
        return back_of(2, 1, sums), (near_a, two, one, cross_out), pos_a[1] + near_a[3]

    (pos_b, *sums), (near_a, two_pair, one_blocks, cross_out), send_a = stage(always, back_stage_b)

    def back_stage_c():
        near_b = core(pos_b)
        one, out = last_pair(halve(one_blocks, bits[1:-1])), halve(keep_out + cross_out, bits[:1])
        far_a = swap(send_a, "mp", 2)
        return back_of(3, 1, sums), far_a, near_b, one, out

    (pos_c, query_own, keep_kv, send_kv), far_a, near_b, one_pair, out_blocks = stage(always, back_stage_c)
    slot_share, share = slots // dp, width // mp

    def tail_stage_a():
        near_c = core(pos_c)
        out = last_pair(halve(out_blocks, bits[1:-1]))
        cross_kv, query_far = swap(send_kv, "dp", 1), swap(query_own, "mp", 2)
        far_b = swap(pos_b[1] + near_b[3], "mp", 2)
        latents_out = block_output((hidden_a, hidden_b), share_out, crossed_out)
        transfers = near_c, out, cross_kv, query_far, far_b
        return latents_out, first_sums(place, pos_a, near_a, far_a, slot_share), transfers, pos_c[1] + near_c[3]

    latents_out, (keep_a, send_x), transfers, send_c = stage(always, tail_stage_a)
    near_c, out_pair, cross_kv, query_far, far_b = transfers

    def tail_stage_b():
        query_all = [query_own, core(query_own), query_far, core(query_far)]
        kv_blocks = halve(keep_kv + cross_kv, bits[:1])
        cross_a = swap(send_x, "dp", 1)
        far_c = swap(send_c, "mp", 2)
        latent_out = latent(
            place, query_all, latents, (hidden_grad_a, hidden_grad_b), gain_lat[None], w_query_all, dp
        )
        tiles = [(pos_b, near_b, far_b), (pos_c, near_c, far_c)]
        return latent_out, cross_a, kv_blocks, second_sums(place, tiles, latent_out[1], gain_mlp_grad, slot_share, vocab)

    latent_out, cross_a, kv_blocks, (keep_c, send_c) = stage(always, tail_stage_b)
    latent_grad, gain_lat_grad, keep_query, send_query = latent_out
    byte_rows = share // 2 * byte_cols // 128
    cross_c = swap(send_c, "dp", 1)
    byte_rows = share // 2 * byte_cols // 128
    kv_sum = halve(kv_blocks, bits[1:])[0]
    pos_keep, pos_send, byte_blocks, send_query = third_sums(
        place, keep_a, cross_a, send_query, keep_c, cross_c, byte_rows, share // 2, [kv_sum]
    )
    cross = swap(pos_send, "dp", bits[0])
    two_sum, one_sum, out_sum = finish([two_pair, one_pair, out_pair], val_cols, [pos_keep])
    query = keep_query, swap(send_query, "dp", 1)
    byte_parts = [byte_blocks[:1]] + [swap(byte_blocks[j], "dp", 2 * d) for j, d in enumerate(reversed_bits(dp // 2)) if d]
    pos_keep, pos_send, byte_sum, keep_query, send_query = next_sums(
        place, pos_keep, cross, bits[1], byte_parts, query, [two_sum]
    )
    cross = swap(pos_send, "dp", bits[1])
    for bit in bits[2:]:
        pos_keep, pos_send = next_sums(place, pos_keep, cross, bit)
        cross = swap(pos_send, "dp", bit)
    byte_parts = [byte_sum] + [swap(byte_sum, "dp", 2 * d) for d in range(1, dp // 2)]
    query = keep_query, swap(send_query, "dp", bits[0])
    pos_sum, byte_half, query_blocks = last_sums(place, pos_keep, cross, byte_parts, query, share)
    query_sum = halve(query_blocks, bits[1:])[0]
    byte_grad, gain_in_grad, gains = byte_sums(place, byte_half, swap(byte_half, "dp", 1), share, vocab, val_cols)
    return (
        latents_out, latent_grad, byte_grad, pos_sum.T, gain_in_grad[0], gains[0], gains[1],
        unpacked(query_sum, qk_cols), kv_sum[:, :qk_cols], kv_sum[:, qk_cols:], out_sum.T, one_sum, two_sum.T,
    )


def solution(mesh):
    return jax.shard_map(
        body,
        mesh=mesh,
        in_specs=(
            P("dp", None),
            P("dp"),
            P("dp", None, None),
            P(),
            P(),
            P(),
            P(),
            P(),
            P(None, "mp"),
            P(None, "mp"),
            P(None, "mp"),
            P("mp", None),
            P(None, "mp"),
            P("mp", None),
            P("dp", None, None),
        ),
        out_specs=(
            P("dp", None, None),
            P("dp", None, None),
            P(None, "mp"),
            P("dp", "mp"),
            P("mp"),
            P("mp"),
            P("mp"),
            P("dp", "mp"),
            P("dp", "mp"),
            P("dp", "mp"),
            P("mp", "dp"),
            P("dp", "mp"),
            P("mp", "dp"),
        ),
        check_vma=False,
    )
```

```python
import functools

import jax
import jax.numpy as jnp
from jax import lax
from jax.experimental import pallas as pl
from jax.experimental.pallas import tpu as pltpu
from jax.sharding import PartitionSpec as P

HEADS = 8
EPSILON = 1e-05
MASKED = -1e30
LOG2E = 1.4426950408889634
TILE = 512
COST = 11500000000
f32, bf16 = jnp.float32, jnp.bfloat16
ANYWHERE = pl.BlockSpec(memory_space=pl.ANY)


def dot(left, right):
    return jnp.dot(left, right, preferred_element_type=f32)


def dot_nt(left, right):
    return lax.dot_general(left, right, (((1,), (1,)), ((), ())), preferred_element_type=f32)


def dot_tn(left, right):
    return lax.dot_general(left, right, (((0,), (0,)), ((), ())), preferred_element_type=f32)


def cost(microseconds):
    return pl.CostEstimate(flops=microseconds * COST, bytes_accessed=0, transcendentals=0)


def limits(mebibytes):
    return pltpu.CompilerParams(vmem_limit_bytes=mebibytes * 2**20)


def ignoring(kernel, start, count):
    def inner(*refs):
        return kernel(*refs[:start], *refs[start + count :])

    return inner


def row_norm(rows):
    centered = rows - jnp.mean(rows, axis=-1, keepdims=True)
    inv_std = lax.rsqrt(jnp.mean(centered * centered, axis=-1, keepdims=True) + EPSILON)
    return centered * inv_std, inv_std


def row_norm_back(upstream, unit, inv, gain):
    scaled = upstream * gain
    row_mean = jnp.mean(scaled, axis=-1, keepdims=True)
    row_cross = jnp.mean(scaled * unit, axis=-1, keepdims=True)
    return inv * (scaled - row_mean - unit * row_cross)


def front_kernel(
    lengths, ids_ref, table_ref, pos_ref, pos_mean_ref, gain_ref, w_kv_ref, lat_ref, gain_lat_ref, w_query_ref,
    unit_ref, inv_ref, kv_ref, lse_ref, query_ref, query_t_ref, att_ref,
    x_ref, normed_ref, scores_ref, total_ref, peak_ref,
    *, first, width, heads,
):
    step = pl.program_id(1)
    item = first + pl.program_id(0)
    length = lengths[item]
    lat_count = lat_ref.shape[1]
    qk_cols = w_query_ref.shape[0]
    qk = qk_cols // heads
    val = (w_kv_ref.shape[0] - qk_cols) // heads
    scale = qk**-0.5 * LOG2E
    chunk = 64

    @pl.when(step == 0)
    def _():
        unit_lat, _ = row_norm(lat_ref[0].astype(f32))
        queries = dot_nt((unit_lat * gain_lat_ref[...]).astype(bf16), w_query_ref[...])
        query_ref[0] = queries.astype(bf16)
        query_t_ref[0] = queries.T.astype(bf16)
        peak_ref[...] = jnp.full_like(peak_ref, MASKED)

    @pl.when(step * TILE < length)
    def _():
        cols = pl.ds(pl.multiple_of(step * TILE, TILE), TILE)
        hits = (lax.broadcasted_iota(jnp.int32, (table_ref.shape[1], TILE), 0) == ids_ref[pl.ds(item, 1), cols]).astype(bf16)
        x_ref[...] = dot(table_ref[...], hits)
        mean = x_ref[width : width + 1] + x_ref[width + 1 : width + 2] + x_ref[width + 2 : width + 3]
        mean = mean + pos_mean_ref[:, cols]
        square = jnp.zeros((8, TILE), f32)
        for r in range(0, width, chunk):
            rows = x_ref[r : r + chunk] + pos_ref[r : r + chunk].astype(f32) - mean
            x_ref[r : r + chunk] = rows
            rows = rows * rows
            square += sum(rows[i : i + 8] for i in range(0, chunk, 8))
        inv = lax.rsqrt(jnp.sum(square, axis=0, keepdims=True) * (1.0 / width) + EPSILON)
        inv_ref[0, :, cols] = inv
        for r in range(0, width, chunk):
            unit = x_ref[r : r + chunk] * inv
            unit_ref[0, r : r + chunk] = unit.astype(bf16)
            gain = jnp.concatenate([gain_ref[r : r + chunk]] * (TILE // 128), axis=1)
            normed_ref[r : r + chunk] = (unit * gain).astype(bf16)
        kv_ref[0, :, cols] = dot(w_kv_ref[...], normed_ref[...]).astype(bf16)
        live = step * TILE + lax.broadcasted_iota(jnp.int32, (1, TILE), 1) < length
        for h in range(heads):
            scores = dot(query_ref[0, :, h * qk : (h + 1) * qk], kv_ref[0, h * qk : (h + 1) * qk, cols])
            scores = jnp.where(live, scores, MASKED)
            scores_ref[h, :, cols] = scores
            peak = peak_ref[h]
            for c in range(0, TILE, 128):
                peak = jnp.maximum(peak, scores[:, c : c + 128])
            peak_ref[h] = peak

    @pl.when(step == pl.num_programs(1) - 1)
    def _():
        peaks = [jnp.max(peak_ref[h], axis=1, keepdims=True) for h in range(heads)]
        total_ref[...] = jnp.zeros_like(total_ref)

        def attend(t, sums):
            cols = pl.ds(pl.multiple_of(t * TILE, TILE), TILE)
            new = []
            for h in range(heads):
                raised = jnp.exp2((scores_ref[h, :, cols] - peaks[h]) * scale)
                new.append(sums[h] + sum(raised[:, c : c + 128] for c in range(0, TILE, 128)))
                start = qk_cols + h * val
                total_ref[h] += dot_nt(raised.astype(bf16), kv_ref[0, start : start + val, cols])
            return tuple(new)

        sums = lax.fori_loop(0, pl.cdiv(length, TILE), attend, (jnp.zeros((lat_count, 128), f32),) * heads)
        lane = lax.broadcasted_iota(jnp.int32, (lat_count, 128), 1)
        packed = jnp.zeros((lat_count, 128), f32)
        out = []
        for h in range(heads):
            total = jnp.sum(sums[h], axis=1, keepdims=True)
            out.append(total_ref[h] / total)
            packed = jnp.where(lane == h, peaks[h] * scale + jnp.log2(total), packed)
        att_ref[0] = jnp.concatenate(out, axis=1).T
        lse_ref[0] = packed


def front(first, count, lengths, ids, table, pos, pos_mean, gain, w_kv, latents, gain_lat, w_query, heads):
    slots = ids.shape[1]
    width = pos.shape[0]
    lat_count, lat_width = latents.shape[1:]
    qk_cols = w_query.shape[0]
    kv_cols = w_kv.shape[0]
    val_cols = kv_cols - qk_cols
    whole = lambda a: pl.BlockSpec(a.shape, lambda i, t, *_: (0,) * a.ndim)
    each = lambda *s: pl.BlockSpec((1, *s), lambda i, t, *_: (first + i, 0, 0))
    made = lambda *s: pl.BlockSpec((1, *s), lambda i, t, *_: (i, 0, 0))
    shape = lambda s, d: jax.ShapeDtypeStruct((count, *s), d)

    def live(i, t, lengths):
        return jnp.minimum(t, pl.cdiv(lengths[first + i], TILE) - 1)

    return pl.pallas_call(
        functools.partial(front_kernel, first=first, width=width, heads=heads),
        grid_spec=pltpu.PrefetchScalarGridSpec(
            num_scalar_prefetch=1,
            grid=(count, slots // TILE),
            in_specs=[
                whole(ids), whole(table), pl.BlockSpec((width, TILE), lambda i, t, l: (0, live(i, t, l))), whole(pos_mean),
                whole(gain), whole(w_kv), each(lat_count, lat_width), whole(gain_lat), whole(w_query),
            ],
            out_specs=[
                pl.BlockSpec((1, width, TILE), lambda i, t, l: (i, 0, live(i, t, l))), made(1, slots), made(kv_cols, slots),
                made(lat_count, 128), made(lat_count, qk_cols), made(qk_cols, lat_count), made(val_cols, lat_count),
            ],
            scratch_shapes=[
                pltpu.VMEM((table.shape[0], TILE), f32),
                pltpu.VMEM((width, TILE), bf16),
                pltpu.VMEM((heads, lat_count, slots), f32),
                pltpu.VMEM((heads, lat_count, val_cols // heads), f32),
                pltpu.VMEM((heads, lat_count, 128), f32),
            ],
        ),
        out_shape=[
            shape((width, slots), bf16), shape((1, slots), f32), shape((kv_cols, slots), bf16), shape((lat_count, 128), f32),
            shape((lat_count, qk_cols), bf16), shape((qk_cols, lat_count), bf16),
            shape((val_cols, lat_count), f32),
        ],
        compiler_params=limits(56),
        cost_estimate=cost(18),
        name="front",
    )(lengths, ids, table, pos, pos_mean, gain, w_kv, latents, gain_lat, w_query)


def tables_kernel(
    place_ref, byte_ref, pos_ref, gain_ref, w_key_ref, w_value_ref, w_one_ref, w_two_ref, table_ref, pos_t_ref, mean_ref, gains_ref, w_kv_ref, w_back_ref,
    w_rows_ref, one_ref, two_ref, pad_ref,
):
    vocab, width = byte_ref.shape

    @pl.when(pl.program_id(0) == 0)
    def _():
        rows = one_ref.shape[0]
        quarter = pl.ds(pl.multiple_of(place_ref[1] % 4 * rows, 16), rows)
        one_ref[...] = w_one_ref[quarter].astype(f32)
        two_ref[...] = w_two_ref[quarter].astype(f32)
        gain = gain_ref[...]
        gains_ref[...] = jnp.broadcast_to(gain, (128, width)).T
        first = w_key_ref.shape[0]
        w_kv_ref[:first] = w_key_ref[...]
        w_kv_ref[first:] = w_value_ref[...]
        w_rows_ref[...] = w_kv_ref[...].astype(f32).T.astype(bf16)
        scaled = w_kv_ref[...].astype(f32) * gain
        w_back_ref[...] = (scaled - jnp.mean(scaled, axis=1, keepdims=True)).T.astype(bf16)
        pad_ref[...] = jnp.zeros_like(pad_ref)
        pad_ref[:vocab] = byte_ref[...].astype(f32)
        table = pad_ref[...].T
        table_ref[:width] = table[:, : table_ref.shape[1]].astype(bf16)
        mean = jnp.mean(table, axis=0, keepdims=True)[:, : table_ref.shape[1]]
        high = mean.astype(bf16)
        rest = mean - high.astype(f32)
        middle = rest.astype(bf16)
        low = (rest - middle.astype(f32)).astype(bf16)
        more = table_ref.shape[0] - width
        row = lax.broadcasted_iota(jnp.int32, (more, table_ref.shape[1]), 0)
        rows = jnp.zeros(row.shape, f32)
        for place, value in enumerate((high, middle, low)):
            rows = jnp.where(row == place, value.astype(f32), rows)
        table_ref[width:] = rows.astype(bf16)

    pos = pos_ref[...].astype(f32).T
    pos_t_ref[...] = pos.astype(bf16)
    mean_ref[...] = jnp.mean(pos, axis=0, keepdims=True)


def tables_of(place, byte_table, pos_table, gain, w_key_t, w_value_t, w_one_t, w_two):
    vocab, width = byte_table.shape
    slots = pos_table.shape[0]
    kv_cols = w_key_t.shape[0] + w_value_t.shape[0]
    vocab_rows = vocab + -vocab % 16
    whole = lambda a: pl.BlockSpec(a.shape, lambda t: (0,) * a.ndim)
    shapes = [
        ((width + 16, vocab_rows), bf16), ((width, slots), bf16), ((1, slots), f32), ((width, 128), f32), ((kv_cols, width), bf16),
        ((width, kv_cols), bf16), ((width, kv_cols), bf16), *([((w_two.shape[0] // 4, w_two.shape[1]), f32)] * 2),
    ]
    shapes = [jax.ShapeDtypeStruct(*s) for s in shapes]
    specs = [whole(a) for a in shapes]
    specs[1] = pl.BlockSpec((width, TILE), lambda t: (0, t))
    specs[2] = pl.BlockSpec((1, TILE), lambda t: (0, t))
    return pl.pallas_call(
        tables_kernel,
        grid=(slots // TILE,),
        in_specs=[
            pl.BlockSpec(memory_space=pltpu.SMEM), whole(byte_table), pl.BlockSpec((TILE, width), lambda t: (t, 0)), whole(gain),
            whole(w_key_t), whole(w_value_t), whole(w_one_t), whole(w_two),
        ],
        out_specs=specs,
        out_shape=shapes,
        scratch_shapes=[pltpu.VMEM((vocab + -vocab % 128, width), f32)],
        compiler_params=limits(40),
        cost_estimate=cost(8),
        name="tables",
    )(place, byte_table, pos_table, gain, w_key_t, w_value_t, w_one_t, w_two)


def back_kernel(
    lengths, place_ref, ids_ref, w_ref, w_rows_ref, gain_ref, *refs,
    first, heads, groups, last, vocab,
):
    step, item = pl.program_id(0), pl.program_id(1)
    length = lengths[item]
    tile = step + first
    sums_in, refs = (refs[:3], refs[3:]) if first else ((), refs)
    made = [refs[9 * g : 9 * g + 9] for g in range(groups)]
    refs = refs[9 * groups :]
    pos_ref, query_out_ref, *refs = refs
    if last:
        keep_ref, send_ref, *refs, byte_ref, unit_kv_ref, turned_ref = refs
    else:
        byte_ref, unit_kv_ref, *refs = refs
    (
        unit_ref, inv_ref, kv_ref, lse_ref, query_ref, query_t_ref, att_grad_ref, att_grad_t_ref, delta_ref, kv_grad_ref, low_ref,
    ) = refs
    width, kv_cols = w_ref.shape
    qk_cols = query_ref.shape[1]
    qk, val = qk_cols // heads, (kv_cols - qk_cols) // heads
    factor = qk**-0.5
    scale = factor * LOG2E
    chunk = 64
    share = pos_ref.shape[1]

    def order(block):
        distance = place_ref[0] ^ block
        return distance % 2 * 2 + distance // 2

    @pl.when((step == 0) & (item == 0))
    def _():
        for i, ref in enumerate((query_out_ref, byte_ref, unit_kv_ref)):
            ref[...] = sums_in[i][...] if first else jnp.zeros_like(ref)

    @pl.when(item == 0)
    def _():
        pos_ref[:, :, :TILE] = jnp.zeros((4, share, TILE), f32)

    for g in range(groups):

        @pl.when((tile * TILE < length) & (item // (pl.num_programs(1) // groups) == g))
        def _():
            copies = (unit_ref, inv_ref, kv_ref, lse_ref, query_ref, query_t_ref, att_grad_ref, att_grad_t_ref, delta_ref)
            for target, ref in zip(copies, made[g]):
                target[...] = ref[0]

    @pl.when(tile * TILE < length)
    def _():
        live = tile * TILE + lax.broadcasted_iota(jnp.int32, (1, TILE), 1) < length
        cross = jnp.zeros((8, TILE), f32)
        for h in range(heads):
            keys = slice(h * qk, (h + 1) * qk)
            values = slice(qk_cols + h * val, qk_cols + (h + 1) * val)
            cols = slice(h * val, (h + 1) * val)
            scores = dot(query_ref[:, keys], kv_ref[keys])
            chances = jnp.exp2(scores * scale - lse_ref[:, h : h + 1])
            chances = jnp.where(live, chances, 0.0)
            weights_grad = dot(att_grad_ref[:, cols], kv_ref[values])
            scores_grad = (chances * (weights_grad - delta_ref[:, h : h + 1])).astype(bf16)
            query_out_ref[item, keys] += dot_nt(kv_ref[keys], scores_grad)
            kv_grad_ref[keys] = (dot(query_t_ref[keys], scores_grad) * factor).astype(bf16)
            kv_grad_ref[values] = dot(att_grad_t_ref[cols], chances.astype(bf16)).astype(bf16)
        for r in range(0, kv_cols, chunk):
            rows = kv_grad_ref[r : r + chunk].astype(f32) * kv_ref[r : r + chunk].astype(f32)
            cross += sum(rows[i : i + 8] for i in range(0, chunk, 8))
        inv = inv_ref[...]
        cross = jnp.sum(cross, axis=0, keepdims=True) * (1.0 / width) * inv
        back = dot(w_ref[...], kv_grad_ref[...])
        for r in range(0, width, chunk):
            rows = slice(r, r + chunk)
            grads = back[rows] * inv - unit_ref[rows].astype(f32) * cross
            pos_ref[order(r // share), r % share : r % share + chunk, :TILE] += grads
            low_ref[rows] = grads.astype(bf16)
        hits = (lax.broadcasted_iota(jnp.int32, (byte_ref.shape[0], TILE), 0) == ids_ref[pl.ds(item, 1)]).astype(bf16)
        byte_ref[...] += dot_nt(hits, low_ref[...])
        unit_kv_ref[...] += dot_nt(kv_grad_ref[...], unit_ref[...])

    if last:

        @pl.when((step == pl.num_programs(0) - 1) & (item == pl.num_programs(1) - 1))
        def _():
            query_out_ref[...] = (query_out_ref[...] * factor).astype(bf16).astype(f32)
            turned_ref[...] = unit_kv_ref[...].T
            gain_grad = jnp.sum(turned_ref[...] * w_rows_ref[...].astype(f32), axis=1, keepdims=True)
            spare = pos_ref.shape[2] - TILE - byte_ref.shape[0]
            byte = jnp.concatenate([byte_ref[...], jnp.zeros((spare, width), f32)], axis=0).T
            byte = jnp.where(lax.broadcasted_iota(jnp.int32, byte.shape, 1) == vocab, gain_grad, byte)
            for block in range(4):
                pos_ref[order(block), :, TILE:] = byte[block * share : (block + 1) * share]
            turned_ref[...] *= gain_ref[:, :1]
            split_blocks(keep_ref, send_ref, turned_ref, place_ref[1])


def back(place, first, count, lengths, ids, made, w_back, w_rows, gains, sums, heads, vocab):
    items, slots = ids.shape
    last = (first + count) * TILE == slots
    groups = len(made)
    size = items // groups
    width, kv_cols = w_back.shape
    lat_count, qk_cols = made[0][4].shape[1:]
    val_cols = kv_cols - qk_cols
    whole = lambda a: pl.BlockSpec(a.shape, lambda t, i, *_: (0,) * a.ndim)
    clip = lambda i, g: jnp.clip(i - g * size, 0, size - 1)
    tiles = lambda g, *s: pl.BlockSpec((1, *s, TILE), lambda t, i, *_: (clip(i, g), 0, t + first))
    each = lambda g, *s: pl.BlockSpec((1, *s), lambda t, i, *_: (clip(i, g), 0, 0))
    shape = lambda s: jax.ShapeDtypeStruct(s, f32)
    kernel = functools.partial(back_kernel, first=first, heads=heads, groups=groups, last=last, vocab=vocab)
    operands = (ids, w_back, w_rows, gains, *sums, *(a for nine in made for a in nine))
    byte_cols = vocab + -vocab % 128
    sums_of = (items, qk_cols, lat_count), (vocab + -vocab % 16, width), (kv_cols, width)
    query_sum, byte_sum, unit_kv = (shape(a) for a in sums_of)
    blocks = lax.axis_size("dp")
    if last:
        assert count == 1
        split = shape((blocks // 2, width // blocks, kv_cols))
        out_shape = [shape((4, width // 4, TILE + byte_cols)), query_sum, split, split]
        out_specs = [whole(a) for a in out_shape]
    else:
        out_shape = [shape((4, width // 4, count * TILE)), query_sum, byte_sum, unit_kv]
        out_specs = [pl.BlockSpec((4, width // 4, TILE), lambda t, i, *_: (0, 0, t)), *(whole(a) for a in out_shape[1:])]
    return pl.pallas_call(
        kernel,
        grid_spec=pltpu.PrefetchScalarGridSpec(
            num_scalar_prefetch=2,
            grid=(count, items),
            in_specs=[
                pl.BlockSpec((items, TILE), lambda t, i, *_: (0, t + first)),
                *(whole(a) for a in (w_back, w_rows, gains, *sums)),
                *(
                    spec
                    for g in range(groups)
                    for spec in (
                        tiles(g, width), tiles(g, 1), tiles(g, kv_cols), each(g, lat_count, 128), each(g, lat_count, qk_cols),
                        each(g, qk_cols, lat_count), each(g, lat_count, val_cols), each(g, val_cols, lat_count), each(g, lat_count, 128),
                    )
                ),
            ],
            out_specs=out_specs,
            scratch_shapes=[
                pltpu.VMEM((width, TILE), bf16), pltpu.VMEM((1, TILE), f32), pltpu.VMEM((kv_cols, TILE), bf16),
                pltpu.VMEM((lat_count, 128), f32), pltpu.VMEM((lat_count, qk_cols), bf16),
                pltpu.VMEM((qk_cols, lat_count), bf16), pltpu.VMEM((lat_count, val_cols), bf16),
                pltpu.VMEM((val_cols, lat_count), bf16), pltpu.VMEM((lat_count, 128), f32),
                pltpu.VMEM((kv_cols, TILE), bf16), pltpu.VMEM((width, TILE), bf16),
                *([pltpu.VMEM(s, f32) for s in (*sums_of[1:], (width, kv_cols))] if last else []),
            ],
        ),
        out_shape=out_shape,
        compiler_params=limits(58),
        cost_estimate=cost(12 * count),
        name="back",
    )(lengths, place, *operands)


def assemble_kernel(place_ref, own_ref, *refs):
    *far_refs, out_ref = refs
    side, corner = place_ref[0] // 2, place_ref[1] % 4
    rows = own_ref.shape[0]
    quarter = rows // 4

    def put(start, ref):
        out_ref[pl.ds(pl.multiple_of(start, 16), ref.shape[0])] = ref[...].astype(bf16)

    put(side * rows, own_ref)
    for step, ref in enumerate(far_refs):
        put((1 - side) * rows + (corner ^ step) * quarter, ref)


def assemble(place, own, far, tokens=()):
    rows, width = own.shape
    operands = (own, *far)
    return pl.pallas_call(
        ignoring(assemble_kernel, 1 + len(operands), len(tokens)),
        in_specs=[
            pl.BlockSpec(memory_space=pltpu.SMEM), *([pl.BlockSpec(memory_space=pltpu.VMEM)] * len(operands)),
            *([ANYWHERE] * len(tokens)),
        ],
        out_specs=pl.BlockSpec(memory_space=pltpu.VMEM),
        out_shape=jax.ShapeDtypeStruct((2 * rows, width), bf16),
        compiler_params=limits(40),
        cost_estimate=cost(2),
        name="assemble",
    )(place, *operands, *tokens)


def packed(block):
    rows, cols = block.shape
    parts = [block[:, c : c + 128] for c in range(0, cols - 127, 128)]
    if cols % 128:
        last = block[:, cols - 64 :]
        parts.append(jnp.concatenate([last[: rows // 2], last[rows // 2 :]], axis=1))
    return jnp.concatenate(parts, axis=0)


def unpacked(block, cols):
    rows = block.shape[0] * 128 // cols
    count = cols // 128
    parts = [block[c * rows : (c + 1) * rows] for c in range(count)]
    if cols % 128:
        last = block[count * rows :]
        parts.append(jnp.concatenate([last[:, :64], last[:, 64:]], axis=0))
    return jnp.concatenate(parts, axis=1)


def reversed_bits(count):
    order = [0]
    while len(order) < count:
        order = [2 * o for o in order] + [2 * o + 1 for o in order]
    return order


def split_blocks(keep_ref, send_ref, total, dp_place, shape=lambda block: block):
    count = keep_ref.shape[0]
    size = total.shape[0] // count // 2
    for ref, flip in ((keep_ref, 0), (send_ref, 1)):
        for j, distance in enumerate(reversed_bits(count)):
            target = dp_place ^ (2 * distance + flip)
            ref[j] = shape(total[pl.ds(pl.multiple_of(target * size, 8), size)])


def put_blocks(keep_ref, send_ref, total, dp_place):
    split_blocks(keep_ref, send_ref, total, dp_place, packed)


def call(kernel, grid, inputs, outputs, scratch=(), tokens=(), name=None, time=1, limit=56):
    whole = lambda a: (a, a.shape, lambda *_: (0,) * a.ndim)
    inputs = [i if isinstance(i, tuple) else whole(i) for i in inputs]
    specs = [pl.BlockSpec(block, index) if block else pl.BlockSpec(memory_space=pltpu.SMEM) for _, block, index in inputs]
    return pl.pallas_call(
        ignoring(kernel, len(inputs), len(tokens)),
        grid=grid,
        in_specs=[*specs, *([ANYWHERE] * len(tokens))],
        out_specs=[pl.BlockSpec(block, index) for _, _, block, index in outputs],
        out_shape=[jax.ShapeDtypeStruct(shape, kind) for shape, kind, _, _ in outputs],
        scratch_shapes=list(scratch),
        compiler_params=limits(limit),
        cost_estimate=cost(time),
        name=name,
    )(*(a for a, _, _ in inputs), *tokens)


def scalars(place):
    return place, None, None


def each(array):
    return array, (1, *array.shape[1:]), lambda i: (i, *(0,) * (array.ndim - 1))


def part(array, first):
    return array, (1, *array.shape[1:]), lambda i: (first + i, *(0,) * (array.ndim - 1))


def among(array, group, size):
    return array, (1, *array.shape[1:]), lambda i: (jnp.clip(i - group * size, 0, size - 1), 0, 0)


def new(shape, kind=f32):
    return shape, kind, (1, *shape[1:]), lambda i: (i, *(0,) * (len(shape) - 1))


def kept(shape, kind=f32):
    return shape, kind, shape, lambda i: (0,) * len(shape)


def mix(place, own, far, w_out, tokens=()):
    count, rows, lat_count = own.shape

    def kernel(place_ref, own_ref, far_ref, w_ref, out_ref, att_ref):
        side = place_ref[0] // 2
        for ref, at in ((own_ref, side), (far_ref, 1 - side)):
            att_ref[pl.ds(pl.multiple_of(at * rows, 16), rows)] = ref[0].astype(bf16)
        out_ref[0] = dot_tn(att_ref[...], w_ref[...])

    return call(
        kernel, (count,), [scalars(place), each(own), each(far), w_out], [new((count, lat_count, w_out.shape[1]))],
        [pltpu.VMEM((2 * rows, lat_count), bf16)], tokens, "mix", 3, 14,
    )[0]


def feed(place, first, latents, out_grad, mixed, crossed, gain, w_one, w_two, tokens=()):
    count, lat_count, width = mixed.shape
    rows = w_one.shape[0] // 2

    def kernel(
        place_ref, lat_ref, grad_ref, mixed_ref, crossed_ref, gain_ref, w_one_ref, w_two_ref,
        hidden_ref, normed_ref, activated_ref, share_ref, own_ref, up_own_ref, parts_ref,
    ):
        side = place_ref[0] // 2

        def own(tensor):
            parts_ref[0] = tensor[:, :rows]
            parts_ref[1] = tensor[:, rows:]
            return parts_ref[side]

        hidden = lat_ref[0].astype(f32) + (mixed_ref[0] + crossed_ref[0])
        hidden_ref[0] = hidden
        unit, _ = row_norm(hidden)
        normed = (unit * gain_ref[...]).astype(bf16)
        normed_ref[0] = normed
        up = dot_nt(normed, w_one_ref[...])
        below = 0.5 * (1.0 + lax.erf(up * 0.5**0.5))
        activated = (up * below).astype(bf16)
        activated_ref[0] = activated
        own_ref[0] = own(activated)
        slope = below + up * (jnp.exp(-0.5 * up * up) * 0.3989422804014327)
        up_grad = (dot_nt(grad_ref[0], w_two_ref[...]) * slope).astype(bf16)
        up_own_ref[0] = own(up_grad)
        share_ref[0] = dot(up_grad, w_one_ref[...])

    full, low = (count, lat_count, width), (count, lat_count, rows)
    return call(
        kernel, (count,),
        [scalars(place), part(latents, first), part(out_grad, first), each(mixed), each(crossed), gain, w_one, w_two],
        [new(full), new(full, bf16), new((count, lat_count, 2 * rows), bf16), new(full), new(low, bf16), new(low, bf16)],
        [pltpu.VMEM((2, lat_count, rows), bf16)], tokens, "feed", 6, 36,
    )


def split_grad(blocks, width, rows):
    return kept((blocks // 2, width // blocks * rows // 128, 128))


def feed_weights(place, out_grad, fed, blocks, tokens=()):
    items, lat_count, width = out_grad.shape
    groups = len(fed)
    size = items // groups
    rows = fed[0][1].shape[2]

    def kernel(place_ref, grad_ref, *refs):
        item = pl.program_id(0)
        keep_one, send_one, keep_two, send_two, one_sum, two_sum = refs[3 * groups :]

        @pl.when(item == 0)
        def _():
            one_sum[...] = jnp.zeros_like(one_sum)
            two_sum[...] = jnp.zeros_like(two_sum)

        for g in range(groups):

            @pl.when(item // size == g)
            def _():
                normed_ref, activated_ref, up_grad_ref = refs[3 * g : 3 * g + 3]
                two_sum[...] += dot_tn(grad_ref[0], activated_ref[0])
                one_sum[...] += dot_tn(normed_ref[0], up_grad_ref[0])

        @pl.when(item == items - 1)
        def _():
            put_blocks(keep_two, send_two, two_sum, place_ref[1])
            put_blocks(keep_one, send_one, one_sum, place_ref[1])

    return call(
        kernel, (items,), [scalars(place), each(out_grad), *(among(a, g, size) for g in range(groups) for a in fed[g])],
        [split_grad(blocks, width, rows)] * 4, [pltpu.VMEM((width, rows), f32)] * 2, tokens, "feed_weights", 6, 26,
    )


def unmix(place, first, out_grad, hidden, share, crossed, gain, w_out, att, before, blocks, heads, tokens=()):
    count, lat_count, width = hidden.shape
    rows = w_out.shape[0]
    val = rows // heads

    def kernel(place_ref, grad_ref, hidden_ref, share_ref, crossed_ref, gain_ref, w_ref, att_ref, *refs):
        item = pl.program_id(0)
        sums_in, refs = refs[: len(before)], refs[len(before) :]
        hidden_grad_ref, att_grad_ref, att_grad_t_ref, delta_ref, gain_grad_ref, sum_ref, *split = refs

        @pl.when(item == 0)
        def _():
            for i, ref in enumerate((gain_grad_ref, sum_ref)):
                ref[...] = sums_in[i][...] if before else jnp.zeros_like(ref)

        unit, inv = row_norm(hidden_ref[0])
        norm_grad = share_ref[0] + crossed_ref[0]
        gain_grad_ref[...] += jnp.sum(norm_grad * unit, axis=0, keepdims=True)
        hidden_grad = grad_ref[0].astype(f32) + row_norm_back(norm_grad, unit, inv, gain_ref[...])
        hidden_grad_ref[0] = hidden_grad
        mixed_grad = hidden_grad.astype(bf16)
        att = att_ref[0].T
        sum_ref[...] += dot_tn(mixed_grad, att.astype(bf16))
        att_grad = dot_nt(mixed_grad, w_ref[...])
        att_grad_ref[0] = att_grad.astype(bf16)
        att_grad_t_ref[0] = att_grad.T.astype(bf16)
        product = att_grad.astype(bf16).astype(f32) * att
        lane = lax.broadcasted_iota(jnp.int32, delta_ref.shape[1:], 1)
        delta = jnp.zeros(delta_ref.shape[1:], f32)
        for h in range(heads):
            delta = jnp.where(lane == h, jnp.sum(product[:, h * val : (h + 1) * val], axis=1, keepdims=True), delta)
        delta_ref[0] = delta
        if split:

            @pl.when(item == count - 1)
            def _():
                put_blocks(*split, sum_ref, place_ref[1])

    full = (count, lat_count, width)
    return call(
        kernel, (count,),
        [
            scalars(place), part(out_grad, first), each(hidden), each(share), each(crossed), gain, w_out, each(att), *before,
        ],
        [
            new(full), new((count, lat_count, rows), bf16), new((count, rows, lat_count), bf16), new((count, lat_count, 128)),
            kept((1, width)), kept((width, rows)), *([split_grad(blocks, width, rows)] * 2 if first else []),
        ],
        [], tokens, "unmix", 6, 32,
    )


def branch(activated, w_two, tokens=()):
    count, lat_count, _ = activated[0].shape
    groups = len(activated)
    width = w_two.shape[1]

    def kernel(*refs):
        *group_refs, w_ref, out_ref = refs
        for g in range(groups):

            @pl.when(pl.program_id(0) // count == g)
            def _():
                out_ref[0] = dot(group_refs[g][0], w_ref[...])

    return call(
        kernel, (count * groups,), [*(among(a, g, count) for g, a in enumerate(activated)), w_two],
        [new((count * groups, lat_count, width))], [], tokens, "branch", 4, 20,
    )[0]


def block_output(hidden, share, crossed, tokens=()):
    count = hidden[0].shape[0]
    groups = len(hidden)

    def kernel(*refs):
        *hidden_refs, share_ref, crossed_ref, out_ref = refs
        for g in range(groups):

            @pl.when(pl.program_id(0) // count == g)
            def _():
                out_ref[0] = (hidden_refs[g][0] + (share_ref[0] + crossed_ref[0])).astype(bf16)

    return call(
        kernel, (count * groups,), [*(among(a, g, count) for g, a in enumerate(hidden)), each(share), each(crossed)],
        [new(share.shape, bf16)], [], tokens, "block_output", 4, 20,
    )[0]


def latent(place, query_grad, latents, hidden_grad, gain, w_query, blocks):
    items, lat_count, width = latents.shape
    rows = w_query[0].shape[0]
    groups = len(hidden_grad)
    size = items // groups

    def kernel(
        place_ref, own_ref, core_ref, far_ref, far_core_ref, lat_ref, gain_ref, w_own, w_core, w_far, w_far_core, *refs,
    ):
        grad_ref, gain_grad_ref, keep_ref, send_ref, w_ref, parts_ref, sum_ref, turned_ref = refs[groups:]
        item = pl.program_id(0)
        place = place_ref[0]

        def put(target, refs, value):
            for step, ref in enumerate(refs):
                target[pl.ds(pl.multiple_of((place ^ step) * rows, 16), rows)] = value(ref).astype(bf16)

        @pl.when(item == 0)
        def _():
            put(w_ref, (w_own, w_core, w_far, w_far_core), lambda ref: ref[...])
            gain_grad_ref[...] = jnp.zeros_like(gain_grad_ref)
            sum_ref[...] = jnp.zeros_like(sum_ref)

        put(parts_ref, (own_ref, core_ref, far_ref, far_core_ref), lambda ref: ref[0])
        unit, inv = row_norm(lat_ref[0].astype(f32))
        gain = gain_ref[...]
        sum_ref[...] += dot(own_ref[0].astype(bf16), (unit * gain).astype(bf16))
        norm_grad = dot_tn(parts_ref[...], w_ref[...])
        gain_grad_ref[...] += jnp.sum(norm_grad * unit, axis=0, keepdims=True)
        for g in range(groups):

            @pl.when(item // size == g)
            def _():
                grad_ref[0] = refs[g][0] + row_norm_back(norm_grad, unit, inv, gain)

        @pl.when(item == items - 1)
        def _():
            turned_ref[...] = sum_ref[...].T
            put_blocks(keep_ref, send_ref, turned_ref, place_ref[1])

    return call(
        kernel, (items,),
        [
            scalars(place), *(each(q) for q in query_grad), each(latents), gain, *w_query,
            *(among(a, g, size) for g, a in enumerate(hidden_grad)),
        ],
        [new(latents.shape), kept((1, width)), *([split_grad(blocks, width, rows)] * 2)],
        [
            pltpu.VMEM((4 * rows, width), bf16), pltpu.VMEM((4 * rows, lat_count), bf16), pltpu.VMEM((rows, width), f32),
            pltpu.VMEM((width, rows), f32),
        ], (), "latent", 16, 36,
    )


def at(array, index):
    return array, (1, *array.shape[1:]), lambda *_: (index, *(0,) * (array.ndim - 1))


def pos_blocks(columns, slots):
    return [
        (packed(columns[:, c : c + slots]), packed(columns[:, c + slots : c + 2 * slots]))
        for c in range(0, columns.shape[1], 2 * slots)
    ]


def first_sums(place, pos, near, far, slots):
    share, cols = far.shape

    def kernel(place_ref, pos_ref, near_ref, far_ref, keep_ref, send_ref):
        side = place_ref[1] % 2
        for i, (low, high) in enumerate(pos_blocks(pos_ref[0] + near_ref[0] + far_ref[...], slots)):
            keep_ref[i] = jnp.where(side == 0, low, high)
            send_ref[i] = jnp.where(side == 0, high, low)

    split = kept((cols // slots // 2, share * slots // 128, 128))
    return call(
        kernel, (1,), [scalars(place), at(pos, 0), at(near, 2), far], [split, split], [], (), "first_sums", 3, 16
    )


def second_sums(place, tiles, gain_lat, gain_mlp, slots, vocab):
    share, cols = tiles[-1][2].shape
    own = gain_lat.shape[1] // 4
    count = TILE // slots // 2 * len(tiles)
    rows = share * slots // 128
    byte_rows = share // 2 * (cols - TILE) // 128
    first = vocab + 1 + -(vocab + 1) % 8

    def kernel(place_ref, *refs):
        tile_refs = [refs[3 * t : 3 * t + 3] for t in range(len(tiles))]
        lat_ref, mlp_ref, keep_ref, send_ref, byte_ref, gains_ref = refs[3 * len(tiles) :]
        side = place_ref[1] % 2
        blocks = []
        for pos_ref, near_ref, far_ref in tile_refs:
            mine = pos_ref[0] + near_ref[0] + far_ref[...]
            blocks += pos_blocks(mine[:, :TILE], slots)
        byte_ref[...] = mine[:, TILE:]
        gains = jnp.concatenate([lat_ref[...], mlp_ref[...], jnp.zeros((6, lat_ref.shape[1]), f32)], axis=0)
        gains_ref[...] = gains.T
        gains = gains_ref[pl.ds(pl.multiple_of(place_ref[0] * own, 8), own)]
        byte_ref[:, first : first + 8] = gains[:share]
        byte_ref[: own - share, first + 8 : first + 16] = gains[share:]
        blocks.append((packed(byte_ref[: share // 2]), packed(byte_ref[share // 2 :])))
        start = 0
        for low, high in blocks:
            stretch = slice(start, start + low.shape[0])
            keep_ref[stretch] = jnp.where(side == 0, low, high)
            send_ref[stretch] = jnp.where(side == 0, high, low)
            start += low.shape[0]

    split = kept((count * rows + byte_rows, 128))
    return call(
        kernel, (1,),
        [scalars(place), *(a for pos, near, far in tiles for a in (at(pos, 0), at(near, 2), far)), gain_lat, gain_mlp],
        [split, split], [pltpu.VMEM((share, cols - TILE), f32), pltpu.VMEM((gain_lat.shape[1], 8), f32)], (), "second_sums", 3,
        16,
    )


def third_sums(place, keep_ab, cross_ab, query, keep, cross, byte_rows, half, tokens=()):
    before, rows, _ = keep_ab.shape
    last = (keep.shape[0] - byte_rows) // rows
    count = before + last
    size, part = byte_rows // count, half // count

    def kernel(
        place_ref, keep_ab_ref, cross_ab_ref, query_ref, keep_ref, cross_ref, pos_keep_ref, pos_send_ref, byte_ref, query_out_ref
    ):
        ring = place_ref[1] // 2
        query_out_ref[...] = query_ref[...]
        sums = [keep_ab_ref[i] + cross_ab_ref[i] for i in range(before)]
        total = keep_ref[...] + cross_ref[...]
        sums += [total[i * rows : (i + 1) * rows] for i in range(last)]
        for i in range(count // 2):
            pos_keep_ref[i] = jnp.where(ring % 2 == 0, sums[2 * i], sums[2 * i + 1])
            pos_send_ref[i] = jnp.where(ring % 2 == 0, sums[2 * i + 1], sums[2 * i])
        total = total[last * rows :]
        for j in range(count):
            distance = ring ^ j
            place, bits = 0, count.bit_length() - 1
            for b in range(bits):
                place += (distance >> b & 1) << (bits - 1 - b)
            byte_ref[place] = jnp.concatenate(
                [total[c + j * part : c + (j + 1) * part] for c in range(0, byte_rows, half)], axis=0
            )

    split = kept((count // 2, rows, 128))
    return call(
        kernel, (1,), [scalars(place), keep_ab, cross_ab, query, keep, cross],
        [split, split, kept((count, size, 128)), kept(query.shape)], [], tokens, "third_sums", 3, 16,
    )


def next_sums(place, keep, cross, bit, parts=(), query=(), tokens=()):
    count, rows, _ = keep.shape

    def kernel(place_ref, *refs):
        part_refs, refs = refs[: len(parts)], refs[len(parts) :]
        query_refs, refs = refs[: len(query)], refs[len(query) :]
        keep_ref, cross_ref, pos_keep_ref, pos_send_ref, *refs = refs
        mine = place_ref[1] // bit % 2
        sums = [keep_ref[i] + cross_ref[i] for i in range(count)]
        for i in range(count // 2):
            pos_keep_ref[i] = jnp.where(mine == 0, sums[2 * i], sums[2 * i + 1])
            pos_send_ref[i] = jnp.where(mine == 0, sums[2 * i + 1], sums[2 * i])
        if parts:
            refs[0][...] = sum(ref[0] if len(ref.shape) == 3 else ref[...] for ref in part_refs)
        if query:
            total = query_refs[0][...] + query_refs[1][...]
            refs[-2][...] = total[: total.shape[0] // 2]
            refs[-1][...] = total[total.shape[0] // 2 :]

    split = kept((count // 2, rows, 128))
    outputs = [split, split, *([kept(parts[1].shape)] if parts else [])]
    if query:
        outputs += [kept((query[0].shape[0] // 2, *query[0].shape[1:]))] * 2
    return call(
        kernel, (1,), [scalars(place), *parts, *query, keep, cross], outputs, [], tokens, "next_sums", 2, 16
    )


def last_sums(place, keep, cross, parts, query, share):
    count = len(parts)
    size = parts[0].shape[0]
    rows = keep.shape[1]
    half = share // 2
    part = half // count
    lanes = size // part

    def kernel(place_ref, *refs):
        part_refs, (one_ref, other_ref, keep_ref, cross_ref, pos_ref, byte_ref, query_ref, held_ref) = refs[:count], refs[count:]
        query_ref[...] = one_ref[...] + other_ref[...]
        pos_ref[...] = unpacked(keep_ref[0] + cross_ref[0], pos_ref.shape[1])
        for distance, ref in enumerate(part_refs):
            held_ref[place_ref[1] // 2 ^ distance] = ref[...]
        byte_ref[...] = jnp.concatenate(
            [held_ref[j, c * part : (c + 1) * part] for c in range(lanes) for j in range(count)], axis=0
        )

    return call(
        kernel, (1,), [scalars(place), *parts, *query, keep, cross],
        [kept((share, rows * 128 // share)), kept((count * size, 128)), kept(query[0].shape)],
        [pltpu.VMEM((count, size, 128), f32)], (), "last_sums", 2, 16,
    )


def byte_sums(place, own, other, share, vocab, gain_cols):
    cols = own.shape[0] * 128 // (share // 2)
    first = vocab + 1 + -(vocab + 1) % 8

    def kernel(place_ref, own_ref, other_ref, table_ref, gain_ref, gains_ref):
        side = place_ref[1] % 2
        low = jnp.where(side == 0, own_ref[...], other_ref[...])
        high = jnp.where(side == 0, other_ref[...], own_ref[...])
        turned = jnp.concatenate([unpacked(low, cols), unpacked(high, cols)], axis=0).T
        table_ref[...] = turned[:vocab]
        gain_ref[...] = turned[vocab : vocab + 1]
        gains_ref[...] = jnp.concatenate([turned[first : first + 2], turned[first + 8 : first + 10, : gain_cols - share]], axis=1)

    return call(
        kernel, (1,), [scalars(place), own, other], [kept((vocab, share)), kept((1, share)), kept((2, gain_cols))], [], (),
        "byte_sums", 2, 16,
    )


def finish(sums, cols, tokens=()):
    def kernel(*refs):
        for i, out_ref in enumerate(refs[2 * len(sums) :]):
            out_ref[...] = unpacked(refs[2 * i][0] + refs[2 * i + 1][0], cols)

    rows = sums[0][0].shape[1] * 128 // cols
    return call(
        kernel, (1,), [at(a, 0) for pair in sums for a in pair], [kept((rows, cols))] * len(sums), [], tokens, "finish", 3, 16
    )


def swap(tensor, axis, bit):
    return lax.ppermute(tensor, axis, [(i, i ^ bit) for i in range(lax.axis_size(axis))])


def stage(always, work):
    shapes = jax.eval_shape(work)
    return lax.cond(always, work, lambda: jax.tree.map(lambda s: jnp.zeros(s.shape, s.dtype), shapes))


def body(
    byte_ids, lengths, latents, byte_table, pos_table, gain_in, gain_lat, gain_mlp,
    w_query, w_key, w_value, w_out, w_one, w_two, out_grad,
):
    items, slots = byte_ids.shape
    vocab, width = byte_table.shape
    lat_count, lat_width = latents.shape[1:]
    mp, dp = lax.axis_size("mp"), lax.axis_size("dp")
    mp_place, dp_place = lax.axis_index("mp"), lax.axis_index("dp")
    place = jnp.stack([mp_place, dp_place]).astype(jnp.int32)
    heads = HEADS // mp
    qk_cols = w_query.shape[1]
    val_cols = w_value.shape[1]
    corner, side = dp_place % 4, dp_place % 2

    shards = [w_out, w_one.T, w_two]
    quarter = val_cols // 4
    always = lengths[0] > 0
    over_y = lambda w: swap(lax.dynamic_slice_in_dim(w, corner * quarter, quarter, 0).astype(f32), "mp", 2)
    over_x, over_z, over_both = (lambda a, bits=bits: swap(a, "dp", bits) for bits in (1, 2, 3))
    core = lambda a: swap(a, "mp", 1)
    half = items // 2

    def first_stage():
        out = over_y(shards[0])
        weights = (gain_in[None], w_key.T, w_value.T, *shards[1:])
        *tables, w_back, w_rows, one, two = tables_of(place, byte_table, pos_table, *weights)
        far = swap(one, "mp", 2), swap(two, "mp", 2)
        return front_of(0, tables), out, [over_x(out), over_z(out)], over_both(out), far, (tables, w_back, w_rows)

    def front_of(first, tables):
        return front(first, half, lengths, byte_ids, *tables, latents, gain_lat[None], w_query.T, heads)

    (*made_a, att_a), out, crossed_out, last_out, (one, two), (tables, w_back, w_rows) = stage(always, first_stage)

    def third_stage():
        return front_of(half, tables), [over_x(one), over_z(one), over_both(one)], over_both(two), swap(att_a, "mp", 2)

    (*made_b, att_b), crossed_one, last_two, far_a = stage(always, third_stage)

    def fourth_stage():
        crossed_two = [over_x(two), over_z(two), last_two]
        far_b = swap(att_b, "mp", 2)
        w_out_whole = assemble(place, shards[0], [out, *crossed_out, last_out])
        w_one_whole = assemble(place, shards[1], [one, *crossed_one], [w_out_whole])
        mixed_a = mix(place, att_a, far_a, w_out_whole, [w_one_whole])
        return w_out_whole, w_one_whole, mixed_a, crossed_two[:2], far_b

    w_out_whole, w_one_whole, mixed_a, crossed_two, far_b = stage(always, fourth_stage)
    w_two_whole = assemble(place, shards[2], [two, *crossed_two, last_two])
    mixed_b = mix(place, att_b, far_b, w_out_whole, [w_two_whole])
    gain = gain_mlp[None]
    weights = (gain, w_one_whole, w_two_whole)
    hidden_a, normed_a, activated_a, share_a, act_a, up_a = feed(
        place, 0, latents, out_grad, mixed_a, core(mixed_a), *weights, [mixed_b]
    )
    hidden_b, normed_b, activated_b, share_b, act_b, up_b = feed(
        place, half, latents, out_grad, mixed_b, core(mixed_b), *weights, [share_a]
    )
    keep_one, send_one, keep_two, send_two = feed_weights(
        place, out_grad, [(normed_a, act_a, up_a), (normed_b, act_b, up_b)], dp
    )
    w_query_own = w_query.T.astype(f32)
    crossed_a, crossed_b = core(share_a), core(share_b)

    def unmix_stage():
        grads_a = unmix(place, 0, out_grad, hidden_a, share_a, crossed_a, gain, w_out, att_a, [], dp, heads)
        grads_b = unmix(place, half, out_grad, hidden_b, share_b, crossed_b, gain, w_out, att_b, grads_a[4:], dp, heads)
        w_query_parts = core(w_query_own), swap(w_query_own, "mp", 2)
        share_out = branch((activated_a, activated_b), w_two_whole)
        return grads_a[:4], grads_b[:5], grads_b[6:], swap(send_two, "dp", 1), w_query_parts, share_out

    unmixed_a, unmixed_b, (keep_out, send_out), cross_two, w_query_parts, share_out = stage(always, unmix_stage)
    (hidden_grad_a, *grads_a), (hidden_grad_b, *grads_b, gain_mlp_grad) = unmixed_a, unmixed_b
    made = [(*made_a, *grads_a), (*made_b, *grads_b)]
    byte_cols = vocab + -vocab % 128
    bits = [1 << i for i in range(1, dp.bit_length() - 1)]

    def back_of(first, count, sums):
        return back(place, first, count, lengths, byte_ids, made, w_back, w_rows, tables[3], sums, heads, vocab)

    def halve(blocks, bits):
        for bit in bits:
            count = blocks.shape[0] // 2
            blocks = blocks[:count] + swap(blocks[count:], "dp", bit)
        return blocks

    two_blocks = keep_two + cross_two

    def back_stage_a():
        transfers = swap(send_one, "dp", 1), halve(two_blocks, bits[:1]), core(w_query_parts[1]), core(share_out)
        return back_of(0, 2, []), transfers

    (pos_a, *sums), (cross_one, two_blocks, w_query_last, crossed_out) = stage(always, back_stage_a)
    w_query_all = [w_query_own, *w_query_parts, w_query_last]

    def last_pair(blocks):
        return blocks[:1], swap(blocks[1:], "dp", bits[-1])

    def back_stage_b():
        near_a = core(pos_a)
        two, one = halve(two_blocks, bits[1:-1]), halve(keep_one + cross_one, bits[:1])
        two = last_pair(two)
        cross_out = swap(send_out, "dp", 1)
        return back_of(2, 1, sums), (near_a, two, one, cross_out), pos_a[1] + near_a[3]

    (pos_b, *sums), (near_a, two_pair, one_blocks, cross_out), send_a = stage(always, back_stage_b)

    def back_stage_c():
        near_b = core(pos_b)
        one, out = last_pair(halve(one_blocks, bits[1:-1])), halve(keep_out + cross_out, bits[:1])
        far_a = swap(send_a, "mp", 2)
        return back_of(3, 1, sums), far_a, near_b, one, out

    (pos_c, query_own, keep_kv, send_kv), far_a, near_b, one_pair, out_blocks = stage(always, back_stage_c)
    slot_share, share = slots // dp, width // mp

    def tail_stage_a():
        near_c = core(pos_c)
        out = last_pair(halve(out_blocks, bits[1:-1]))
        cross_kv, query_far = swap(send_kv, "dp", 1), swap(query_own, "mp", 2)
        far_b = swap(pos_b[1] + near_b[3], "mp", 2)
        latents_out = block_output((hidden_a, hidden_b), share_out, crossed_out)
        transfers = near_c, out, cross_kv, query_far, far_b
        return latents_out, first_sums(place, pos_a, near_a, far_a, slot_share), transfers, pos_c[1] + near_c[3]

    latents_out, (keep_a, send_x), transfers, send_c = stage(always, tail_stage_a)
    near_c, out_pair, cross_kv, query_far, far_b = transfers

    def tail_stage_b():
        query_all = [query_own, core(query_own), query_far, core(query_far)]
        kv_blocks = halve(keep_kv + cross_kv, bits[:1])
        cross_a = swap(send_x, "dp", 1)
        far_c = swap(send_c, "mp", 2)
        latent_out = latent(
            place, query_all, latents, (hidden_grad_a, hidden_grad_b), gain_lat[None], w_query_all, dp
        )
        tiles = [(pos_b, near_b, far_b), (pos_c, near_c, far_c)]
        return latent_out, cross_a, kv_blocks, second_sums(place, tiles, latent_out[1], gain_mlp_grad, slot_share, vocab)

    latent_out, cross_a, kv_blocks, (keep_c, send_c) = stage(always, tail_stage_b)
    latent_grad, gain_lat_grad, keep_query, send_query = latent_out
    byte_rows = share // 2 * byte_cols // 128
    cross_c = swap(send_c, "dp", 1)
    byte_rows = share // 2 * byte_cols // 128
    kv_sum = halve(kv_blocks, bits[1:])[0]
    pos_keep, pos_send, byte_blocks, send_query = third_sums(
        place, keep_a, cross_a, send_query, keep_c, cross_c, byte_rows, share // 2, [kv_sum]
    )
    cross = swap(pos_send, "dp", bits[0])
    two_sum, one_sum, out_sum = finish([two_pair, one_pair, out_pair], val_cols, [pos_keep])
    query = keep_query, swap(send_query, "dp", 1)
    byte_parts = [byte_blocks[:1]] + [swap(byte_blocks[j], "dp", 2 * d) for j, d in enumerate(reversed_bits(dp // 2)) if d]
    pos_keep, pos_send, byte_sum, keep_query, send_query = next_sums(
        place, pos_keep, cross, bits[1], byte_parts, query, [two_sum]
    )
    cross = swap(pos_send, "dp", bits[1])
    for bit in bits[2:]:
        pos_keep, pos_send = next_sums(place, pos_keep, cross, bit)
        cross = swap(pos_send, "dp", bit)
    byte_parts = [byte_sum] + [swap(byte_sum, "dp", 2 * d) for d in range(1, dp // 2)]
    query = keep_query, swap(send_query, "dp", bits[0])
    pos_sum, byte_half, query_blocks = last_sums(place, pos_keep, cross, byte_parts, query, share)
    query_sum = halve(query_blocks, bits[1:])[0]
    byte_grad, gain_in_grad, gains = byte_sums(place, byte_half, swap(byte_half, "dp", 1), share, vocab, val_cols)
    return (
        latents_out, latent_grad, byte_grad, pos_sum.T, gain_in_grad[0], gains[0], gains[1],
        unpacked(query_sum, qk_cols), kv_sum[:, :qk_cols], kv_sum[:, qk_cols:], out_sum.T, one_sum, two_sum.T,
    )


def solution(mesh):
    return jax.shard_map(
        body,
        mesh=mesh,
        in_specs=(
            P("dp", None),
            P("dp"),
            P("dp", None, None),
            P(),
            P(),
            P(),
            P(),
            P(),
            P(None, "mp"),
            P(None, "mp"),
            P(None, "mp"),
            P("mp", None),
            P(None, "mp"),
            P("mp", None),
            P("dp", None, None),
        ),
        out_specs=(
            P("dp", None, None),
            P("dp", None, None),
            P(None, "mp"),
            P("dp", "mp"),
            P("mp"),
            P("mp"),
            P("mp"),
            P("dp", "mp"),
            P("dp", "mp"),
            P("dp", "mp"),
            P("mp", "dp"),
            P("dp", "mp"),
            P("mp", "dp"),
        ),
        check_vma=False,
    )
```
